32 devices in a mesh: comp: 8 (over z, y), band: 4 (over x, core).
Axes of the slice: x: 2, y: 2, z: 4, core: 2. Of those that a mesh axis runs over, the one named last changes fastest.
Arguments:
- spectra: bfloat16 [32, 36, 16, 1440], P('comp', None, 'band'), may hold values from 0 to 6, as said below
- depth_class: int32 [16, 1440], P('band'), may hold values from 0 to 63
- group_speed: float32 [64, 32], replicated, may hold values from 0.15 to 0.5
- current: float32 [2, 16, 1440], P(None, 'band'), may hold values from -0.3 to 0.3
- depth_slope: float32 [2, 16, 1440], P(None, 'band'), may hold values from -4 to 4
- wind: float32 [2, 16, 1440], P(None, 'band'), may hold values from -32 to 32
- land_mask: int32 [16, 1440], P('band'), may hold values from 0 to 1, as said below
- block_counts: int32 [4, 8], P('band'), may hold values from 210 to 630, as said below
Outputs:
- spectra_out: bfloat16 [1152, 20160], P(None, ('comp', 'band'))
The draws below stay inside these ranges and needn't reach their ends.
Inputs may be any that keep to these rules, and one draw needn't show every extreme that they name: `spectra`: nonnegative densities. `land_mask`: band b's rows hold exactly as many sea cells as row b of block_counts sums to. `block_counts`: in every band one block has exactly 630 sea points.
All inputs are finite; a program needn't handle non-finite values.
Results may differ from the reference program's by a relative error of at most 0.0004.
Values may be sent and summed in bfloat16 or wider, within the bound.
No kernel may reach another device: no remote copies, remote signals or barrier semaphores. Data moves between devices by JAX's collectives and lax.ppermute only.
A program may use at most 64 MiB of HBM per device.

```python
import math
import jax
import jax.numpy as jnp
from jax import lax

NF = 32
ND = 36
NLON = 1440
ROWS = 4
DEPTHS = 64
NLAT = 16
SLOTS = 630
N_COMP = 8
N_BAND = 4


def sea_plan(key):
    cell_count = ROWS * NLON
    first, second, third = jax.random.split(key, 3)
    block_sizes = jax.random.randint(first, (N_BAND, N_COMP), SLOTS // 3, SLOTS + 1)
    fullest = jax.random.randint(second, (N_BAND,), 0, N_COMP)
    block_sizes = jnp.where(jnp.arange(N_COMP)[None, :] == fullest[:, None], SLOTS, block_sizes).astype(jnp.int32)
    totals = jnp.sum(block_sizes, axis=1)

    def shuffled(band_key):
        return jax.random.permutation(band_key, cell_count)
    orders = jax.vmap(shuffled)(jax.random.split(third, N_BAND))
    chosen = (jnp.arange(cell_count)[None, :] < totals[:, None]).astype(jnp.int32)

    def placed(order_row, chosen_row):
        return jnp.zeros((cell_count,), jnp.int32).at[order_row].set(chosen_row)
    flags = jax.vmap(placed)(orders, chosen)
    return (flags, block_sizes)


def draw_land_mask(key, part):
    flags, unused = sea_plan(key)
    return (1 - flags).reshape(NLAT, NLON).astype(jnp.int32)


def draw_block_counts(key, part):
    unused, block_sizes = sea_plan(key)
    return block_sizes


def draw_spectra(key, part):
    key = jax.random.fold_in(key, 7)
    first = jax.random.fold_in(key, 0)
    ramp = (0.6 + 1.2 * jnp.arange(NF, dtype=jnp.float32) / max(NF - 1, 1))[:, None, None, None]
    values = jnp.exp(jax.random.uniform(first, (NF, ND, NLAT, NLON), jnp.float32, math.log(0.05), 0.0)) * ramp
    return values.astype(jnp.bfloat16)


def touch_ends(entries, key, low, high):
    longest = entries.shape.index(max(entries.shape))
    spots = []
    for shift in (0, 1):
        where = [jax.random.randint(jax.random.fold_in(key, axis), (), 0, length) for axis, length in enumerate(entries.shape)]
        where[longest] = (where[longest] + shift) % entries.shape[longest]
        spots.append(tuple(where))
    return entries.at[spots[0]].set(low).at[spots[1]].set(high)


def steps_of(key, shape, shards, smallest, top_value):
    level, own = 1.0, jax.random.fold_in(key, 6)
    for axis_at, shards_of in shards:
        steps = jnp.exp(jax.random.uniform(jax.random.fold_in(own, axis_at), (shards_of,), jnp.float32, smallest / len(shards), top_value / len(shards)))
        level = level * jnp.repeat(steps, shape[axis_at] // shards_of).reshape([-1 if axis == axis_at else 1 for axis in range(len(shape))])
    return level


def bell_draw(own_key, extent, deviation, bound, shards=(), kind=jnp.bfloat16):
    drawn = jax.random.normal(own_key, extent, jnp.float32) * deviation
    if len(shards) > 0:
        drawn = steps_of(own_key, extent, shards, -0.22, 0.18) * drawn
    return jnp.clip(drawn, min=-bound, max=bound).astype(kind)


def setup_inputs(seed: int = 0) -> dict:
    key_list = jax.random.split(jax.random.key(seed), 9)
    return {
        "spectra": draw_spectra(jax.random.fold_in(key_list[8], 71), 0),
        "depth_class": touch_ends(jax.random.randint(key_list[1], (NLAT, NLON), 0, DEPTHS), jax.random.fold_in(key_list[1], 1), 0, DEPTHS - 1).astype(jnp.int32),
        "group_speed": jnp.clip(jnp.exp(jax.random.uniform(key_list[2], (DEPTHS, NF), jnp.float32, math.log(0.15), math.log(0.5))), 0.15, 0.5),
        "current": bell_draw(key_list[3], (2, NLAT, NLON), 0.1, 0.3, ((1, 4),), jnp.float32),
        "depth_slope": bell_draw(key_list[4], (2, NLAT, NLON), 1.0, 4.0, ((1, 4),), jnp.float32),
        "wind": bell_draw(key_list[5], (2, NLAT, NLON), 8.0, 32.0, ((1, 4),), jnp.float32),
        "land_mask": draw_land_mask(jax.random.fold_in(key_list[8], 71), 0),
        "block_counts": draw_block_counts(jax.random.fold_in(key_list[8], 71), 0),
    }


GROWTH_RATE = 0.05
DAMPING = 1.5
TURNING_SCALE = 0.5

def upwind(far_behind, behind, centre, ahead, far_ahead, celerity):
    forward = (2.0 * ahead + 3.0 * centre - 6.0 * behind + far_behind) / 6.0
    backward = (-far_ahead + 6.0 * ahead - 3.0 * centre - 2.0 * behind) / 6.0
    return celerity * jnp.where(celerity > 0, forward, backward)

def wrapped(values, celerity, axis):
    return upwind(jnp.roll(values, 2, axis), jnp.roll(values, 1, axis), values, jnp.roll(values, -1, axis), jnp.roll(values, -2, axis), celerity)

def frequencies(count):
    angular = 2.0 * math.pi * 0.0418 * jnp.power(1.1, jnp.arange(count, dtype=jnp.float32))
    return (angular / angular[-1], 9.81 / angular)

def angles(count):
    heading = jnp.arange(count, dtype=jnp.float32) * (2.0 * math.pi / count)
    return (jnp.cos(heading), jnp.sin(heading))

def block_lists(band_mask, block_sizes, slot_count):
    sea_flag = (band_mask.reshape(-1) == 0).astype(jnp.int32)
    cell_count = sea_flag.shape[0]
    capacity = block_sizes.shape[0] * slot_count
    ranking = jnp.cumsum(sea_flag) - 1
    target = jnp.where(sea_flag == 1, ranking, capacity).astype(jnp.int32)
    ordered = jnp.zeros((capacity,), jnp.int32).at[target].set(jnp.arange(cell_count, dtype=jnp.int32), mode='drop')
    starts = jnp.cumsum(block_sizes) - block_sizes
    slot_ids = jnp.arange(slot_count, dtype=jnp.int32)
    position = jnp.minimum(starts[:, None] + slot_ids[None, :], capacity - 1).astype(jnp.int32)
    return jnp.where(slot_ids[None, :] < block_sizes[:, None], ordered[position], -1).astype(jnp.int32)

def sources(values, mean_sq, wind_u, wind_v, ratio, phase, cos_t, sin_t):
    strength = jnp.sqrt(mean_sq + 1e-06)
    wind_along = wind_u[None, None, :] * cos_t[None, :, None] + wind_v[None, None, :] * sin_t[None, :, None]
    growth = GROWTH_RATE * ratio[:, None, None] * jnp.maximum(wind_along / phase[:, None, None] - 1.0, 0.0)
    decay = DAMPING * ratio[:, None, None] * strength[None, None, :]
    return values * jnp.exp(growth - decay)

def reference(spectra, depth_class, group_speed, current, depth_slope, wind, land_mask, block_counts):
    sea_flag = (land_mask == 0).astype(jnp.float32)
    cos_t, sin_t = angles(ND)
    ratio, phase = frequencies(NF)
    latitude = (-60.0 + 120.0 * (jnp.arange(NLAT, dtype=jnp.float32) + 0.5) / NLAT) * (math.pi / 180.0)
    stretch = 1.0 / jnp.cos(latitude)
    speeds = jnp.moveaxis(group_speed[depth_class], -1, 0)

    def one_frequency(inputs):
        spectrum, celerity = inputs
        density = spectrum.astype(jnp.float32) * sea_flag
        speed_x = celerity[None] * cos_t[:, None, None] * stretch[None, :, None] + current[0][None]
        speed_y = celerity[None] * sin_t[:, None, None] + current[1][None]
        padded = jnp.pad(density, ((0, 0), (2, 2), (0, 0)))
        across = upwind(padded[:, :-4], padded[:, 1:-3], density, padded[:, 3:-1], padded[:, 4:], speed_y)
        advected = (density - wrapped(density, speed_x, 2) - across) * sea_flag
        turning = TURNING_SCALE * celerity[None] * (sin_t[:, None, None] * depth_slope[0][None] - cos_t[:, None, None] * depth_slope[1][None])
        return (advected - wrapped(advected, turning, 0)) * sea_flag
    refracted = lax.map(one_frequency, (spectra, speeds))
    flattened = refracted.reshape(NF * ND, NLAT * NLON)
    wind_east = wind[0].reshape(-1)
    wind_north = wind[1].reshape(-1)
    blocks_out = []
    for band_index in range(N_BAND):
        slot_cells = block_lists(land_mask[band_index * ROWS:(band_index + 1) * ROWS], block_counts[band_index], SLOTS)
        all_cells = (jnp.maximum(slot_cells, 0) + band_index * ROWS * NLON).reshape(-1).astype(jnp.int32)
        picked = jnp.take(flattened, all_cells, axis=1).reshape(NF, ND, -1)
        mean_sq = lax.optimization_barrier(jnp.mean(picked * picked, axis=(0, 1)))
        result = sources(picked, mean_sq, jnp.take(wind_east, all_cells), jnp.take(wind_north, all_cells), ratio, phase, cos_t, sin_t)
        occupied = (slot_cells.reshape(-1) >= 0).astype(jnp.float32)
        blocks_out.append((result * occupied[None, None, :]).astype(jnp.bfloat16).reshape(NF * ND, N_COMP, SLOTS))
    stacked = jnp.stack(blocks_out, axis=2)
    return stacked.reshape(NF * ND, N_COMP * N_BAND * SLOTS)
```

```python
import functools
import math

import jax
import jax.numpy as jnp
import numpy as np
from jax import lax
from jax.experimental import pallas as pl
from jax.experimental.pallas import tpu as pltpu
from jax.sharding import PartitionSpec as P

GROWTH_RATE = 0.05
DAMPING = 1.5
TURNING_SCALE = 0.5

LANES = 128
SUBLANES = 8
UNIT = 9
WORDS = 5
STEP_COUNT = 65500.0
EXPONENT_ZERO = 99
WINDOW = 4
VMEM_BYTES = 32 * 1024 * 1024

F32 = jnp.float32
I32 = jnp.int32


def call(kernel, out_shape, cost, **options):
    flops, moved = cost
    return pl.pallas_call(
        kernel,
        out_shape=out_shape,
        cost_estimate=pl.CostEstimate(flops=flops, bytes_accessed=moved, transcendentals=0),
        compiler_params=pltpu.CompilerParams(vmem_limit_bytes=VMEM_BYTES),
        **options,
    )


def iota(shape, axis):
    return lax.broadcasted_iota(I32, shape, axis)


def upwind(speed, far_behind, behind, centre, ahead, far_ahead):
    positive = speed > 0
    near = jnp.where(positive, behind, ahead)
    after = jnp.where(positive, ahead, behind)
    far = jnp.where(positive, far_behind, far_ahead)
    return jnp.abs(speed) * (2.0 * after + far + 3.0 * (centre - 2.0 * near))


def arrange_kernel(x_ref, sea_ref, top_ref, bottom_ref, scratch):
    freqs, parts, step, rows, lon = x_ref.shape
    chunks = scratch.shape[1]
    tail = lon - (chunks - 1) * LANES
    filler = jnp.zeros((rows, LANES - tail), F32)
    lane = iota((SUBLANES * rows, LANES), 1)
    for j in range(step):
        for f in range(freqs):
            for h in range(parts):
                place = pl.ds(f * parts + h, rows, stride=SUBLANES)
                for k in range(chunks):
                    if k < chunks - 1:
                        piece = x_ref[f, h, j, :, k * LANES : (k + 1) * LANES].astype(F32)
                    else:
                        piece = x_ref[f, h, j, :, k * LANES : lon].astype(F32)
                        piece = jnp.concatenate([piece, filler], axis=1)
                    scratch[j, k, place, :] = piece
        initial = None
        for k in range(chunks):
            span = slice(k * LANES, (k + 1) * LANES)
            piece = scratch[j, k] * sea_ref[:, span]
            if k == 0:
                initial = piece
            if k == chunks - 1:
                wrapped = jnp.where(
                    lane < tail + 2,
                    pltpu.roll(initial, tail, axis=1),
                    pltpu.roll(piece, LANES - tail, axis=1),
                )
                piece = jnp.where(lane < tail, piece, wrapped)
            piece = piece.astype(jnp.bfloat16)
            top_ref[j, :, span] = piece[: 2 * SUBLANES]
            bottom_ref[j, :, span] = piece[2 * SUBLANES :]


def index_kernel(land_ref, counts_ref, cells_ref, ranges_ref):
    chunks = land_ref.shape[0]
    groups, _, slots = cells_ref.shape
    spans = slots // LANES
    sea = (land_ref[...] == 0).astype(jnp.bfloat16)
    square = (LANES, LANES)
    ones_before = (iota(square, 1) <= iota(square, 0)).astype(jnp.bfloat16)
    ranks = lax.dot_general(ones_before, sea, (((1,), (1,)), ((), ())), preferred_element_type=F32)
    totals = jnp.dot(sea, jnp.ones(square, jnp.bfloat16), preferred_element_type=F32)
    chunk_square = (chunks, chunks)
    chunks_before = (iota(chunk_square, 1) <= iota(chunk_square, 0)).astype(jnp.bfloat16)
    through = jnp.dot(chunks_before, totals.astype(jnp.bfloat16), preferred_element_type=F32)
    through_column = through[:, :1]
    total_column = totals[:, :1]
    ranks = ranks.astype(jnp.bfloat16)
    chunk_ids = iota((chunks, slots), 0)
    slot_ids = iota((1, slots), 1)
    span_lane = iota((1, LANES), 1)
    start = jnp.int32(0)
    for c in range(groups):
        count = counts_ref[0, c]
        number = (slot_ids + start).astype(F32)
        passed = (through_column <= number).astype(F32)
        chunk_of = jnp.sum(passed, axis=0, keepdims=True)
        before = jnp.sum(passed * total_column, axis=0, keepdims=True)
        chunk_of = chunk_of.astype(I32)
        chosen = (chunk_ids == chunk_of).astype(jnp.bfloat16)
        inside = jnp.dot(ranks, chosen, preferred_element_type=F32)
        lane = jnp.sum((inside <= number - before).astype(F32), axis=0, keepdims=True)
        valid = slot_ids < count
        found = jnp.where(valid, chunk_of * LANES + lane.astype(I32), -1)
        cells_ref[c] = jnp.broadcast_to(found, (SUBLANES, slots))
        bounds = jnp.zeros((1, LANES), I32)
        for m in range(spans):
            span = slice(m * LANES, (m + 1) * LANES)
            own = chunk_of[:, span].astype(F32)
            low = jnp.min(jnp.where(valid[:, span], own, float(chunks)), axis=1, keepdims=True)
            high = jnp.max(jnp.where(valid[:, span], own, -1.0), axis=1, keepdims=True)
            bounds = jnp.where(span_lane == m, low.astype(I32), bounds)
            bounds = jnp.where(span_lane == m + spans, high.astype(I32), bounds)
        ranges_ref[c : c + 1, :] = bounds
        start = start + count


def advect_kernel(
    top_ref, bottom_ref, table_ref, depth_ref, fields_ref, stretch_ref, trig_ref, out_ref, coef_ref, scratch
):
    turns, _, padded = top_ref.shape
    rows = depth_ref.shape[0]
    chunks = padded // LANES
    table = table_ref[...]
    for r in range(rows):
        place = slice(r * SUBLANES, (r + 1) * SUBLANES)
        for k in range(chunks):
            span = slice(k * LANES, (k + 1) * LANES)

            def field(n):
                return jnp.broadcast_to(fields_ref[n, r : r + 1, span], (SUBLANES, LANES))

            classes = jnp.broadcast_to(depth_ref[r : r + 1, span], (SUBLANES, LANES))
            sixth = jnp.take_along_axis(table, classes, axis=1, mode="promise_in_bounds") * (1.0 / 6.0)
            coef_ref[0, place, span] = sixth
            coef_ref[1, place, span] = field(1) * (1.0 / 6.0)
            coef_ref[2, place, span] = sixth * TURNING_SCALE * field(2)
            coef_ref[3, place, span] = sixth * TURNING_SCALE * field(3)
            scratch[0, place, span] = sixth * stretch_ref[r]
            scratch[1, place, span] = field(0) * (1.0 / 6.0)

    width = LANES * (4 if chunks % 4 == 0 else 1)

    def window(ref, j, low, high):
        parts = []
        if low < LANES:
            parts.append(ref[j, :, padded - LANES :])
            parts.append(ref[j, :, : min(high + LANES, padded)])
        else:
            parts.append(ref[j, :, low - LANES : min(high + LANES, padded)])
        if high + LANES > padded:
            parts.append(ref[j, :, :LANES])
        return jnp.concatenate([part.astype(F32) for part in parts], axis=1)

    def one_turn(j, carry):
        sin = trig_ref[0, j][:, :1]
        cos = trig_ref[1, j][:, :1]
        for low in range(0, padded, width):
            high = low + width
            centres, shifted = [], []
            for ref in (top_ref, bottom_ref):
                wide = window(ref, j, low, high)
                moved = [
                    pltpu.roll(wide, shift % wide.shape[1], axis=1)[:, LANES : LANES + width] for shift in (2, 1, -1, -2)
                ]
                for half in (slice(0, SUBLANES), slice(SUBLANES, 2 * SUBLANES)):
                    centres.append(wide[half, LANES : LANES + width])
                    shifted.append([one[half] for one in moved])
            for r in range(rows):
                place = slice(r * SUBLANES, (r + 1) * SUBLANES)
                span = slice(low, high)
                speed_x = scratch[0, place, span] * cos + scratch[1, place, span]
                speed_y = coef_ref[0, place, span] * sin + coef_ref[1, place, span]
                near = [centres[n] if 0 <= n < rows else 0.0 for n in range(r - 2, r + 3)]
                far_behind, behind, ahead, far_ahead = shifted[r]
                along = upwind(speed_x, far_behind, behind, centres[r], ahead, far_ahead)
                across = upwind(speed_y, *near)
                out_ref[j, place, span] = centres[r] - along - across
        return carry

    lax.fori_loop(0, turns, one_turn, 0)


def pack_kernel(
    group,
    freqs,
    adv_ref,
    above_ref,
    below_ref,
    coef_ref,
    trig_ref,
    scale_ref,
    cells_ref,
    ranges_ref,
    out_ref,
    packed,
):
    turns, height, padded = adv_ref.shape
    rows = height // SUBLANES
    chunks = padded // LANES
    parts = SUBLANES // freqs
    shape = (SUBLANES, LANES)
    part = iota(shape, 0) % parts
    scale = scale_ref[0]
    first = group * UNIT

    def turned(value, by):
        if by == 0:
            return value
        if by > 0:
            return jnp.where(
                part == parts - 1, pltpu.roll(value, parts - 1, axis=0), pltpu.roll(value, SUBLANES - 1, axis=0)
            )
        return jnp.where(part == 0, pltpu.roll(value, SUBLANES - parts + 1, axis=0), pltpu.roll(value, 1, axis=0))

    for r in range(rows):
        place = slice(r * SUBLANES, (r + 1) * SUBLANES)

        def one_chunk(k, carry):
            span = pl.ds(pl.multiple_of(k * LANES, LANES), LANES)
            sixth, current_y, turn_x, turn_y = [coef_ref[n, place, span] for n in range(4)]
            known = {}

            def advected(j):
                j = j % turns
                if j not in known:
                    speed = sixth * trig_ref[0, j] + current_y
                    positive = speed > 0
                    ref = above_ref if r < 2 else below_ref
                    outer = ref[j, :, span].astype(F32)
                    low, high = outer[:SUBLANES], outer[SUBLANES:]
                    if r == 0:
                        share = jnp.where(positive, low - 6.0 * high, 2.0 * high)
                    elif r == 1:
                        share = jnp.where(positive, high, 0.0)
                    elif r == rows - 2:
                        share = jnp.where(positive, 0.0, low)
                    else:
                        share = jnp.where(positive, 2.0 * low, high - 6.0 * low)
                    known[j] = adv_ref[j, place, span] - jnp.abs(speed) * share
                return known[j]

            around = {j: turned(advected(j), j // turns) for j in range(first - 2, first + UNIT + 2)}
            values = []
            for j in range(first, first + UNIT):
                speed = trig_ref[0, j] * turn_x - trig_ref[1, j] * turn_y
                values.append(around[j] - upwind(speed, *[around[n] for n in range(j - 2, j + 3)]))
            largest = functools.reduce(jnp.maximum, [jnp.abs(value) for value in values])
            level = jnp.ceil(jnp.log2(jnp.maximum(largest, 2.0**-98)))
            level = jnp.minimum(level, 28.0).astype(I32) + EXPONENT_ZERO
            level = jnp.maximum(level, 1)
            inverse = jnp.take_along_axis(scale, level, axis=1, mode="promise_in_bounds")
            codes = [(value * inverse + 65536.5).astype(I32) for value in values]
            chunk = r * chunks + k
            rest = codes[8] | (level << 17)
            for n in range(4):
                even, odd = codes[2 * n], codes[2 * n + 1]
                packed[chunk, n * SUBLANES : (n + 1) * SUBLANES, :] = even | (odd << 17)
                rest = rest | ((odd >> 15) << (24 + 2 * n))
            packed[chunk, 4 * SUBLANES :, :] = rest
            return carry

        lax.fori_loop(0, chunks, one_chunk, 0)

    groups, _, slots = out_ref.shape
    spans = slots // LANES
    last = rows * chunks - 1

    def one_block(c, carry):
        for m in range(spans):
            span = slice(m * LANES, (m + 1) * LANES)
            cells = cells_ref[c, :, span]
            low, high = ranges_ref[c, m], ranges_ref[c, m + spans]

            def merged(chunk, sums):
                lane = cells - chunk * LANES
                here = (lane >= 0) & (lane < LANES)
                lane = lane & (LANES - 1)
                return tuple(
                    jnp.where(
                        here,
                        jnp.take_along_axis(
                            packed[chunk, n * SUBLANES : (n + 1) * SUBLANES, :],
                            lane,
                            axis=1,
                            mode="promise_in_bounds",
                        ),
                        sums[n],
                    )
                    for n in range(WORDS)
                )

            sums = tuple(jnp.zeros(shape, I32) for _ in range(WORDS))
            for t in range(WINDOW):
                sums = merged(jnp.minimum(low + t, last), sums)
            for n in range(WORDS):
                out_ref[c, n * SUBLANES : (n + 1) * SUBLANES, span] = sums[n]

            @pl.when(high >= low + WINDOW)
            def _():
                again = tuple(out_ref[c, n * SUBLANES : (n + 1) * SUBLANES, span] for n in range(WORDS))
                again = lax.fori_loop(low + WINDOW, high + 1, merged, again)
                for n in range(WORDS):
                    out_ref[c, n * SUBLANES : (n + 1) * SUBLANES, span] = again[n]

        return carry

    lax.fori_loop(0, groups, one_block, 0)


def finish_kernel(units, *refs):
    arrived = refs[:units]
    wind_ref, count_ref, trig_ref, scale_ref, rate_ref, out_ref, values, ordered = refs[units:]
    groups = arrived[0].shape[0]
    turns = values.shape[1]
    shape = (SUBLANES, LANES)
    scale = scale_ref[1]

    def decode(source, sums):
        for unit in range(units):
            words = [arrived[unit][source, n * SUBLANES : (n + 1) * SUBLANES, :] for n in range(WORDS)]
            rest = words[4]
            level = lax.shift_right_logical(rest, 17) & 127
            size = jnp.take_along_axis(scale, level, axis=1, mode="promise_in_bounds")
            offset = size * 65536.0
            for n in range(UNIT):
                if n == 8:
                    code = rest & 0x1FFFF
                elif n % 2 == 0:
                    code = words[n // 2] & 0x1FFFF
                else:
                    code = lax.shift_right_logical(words[n // 2], 17) | (
                        lax.shift_right_logical(rest, 9 + n - 1) & 0x18000
                    )
                value = code.astype(F32) * size - offset
                values[source, unit * UNIT + n] = value
                sums = sums + value * value
        return sums

    sums = lax.fori_loop(0, groups, decode, jnp.zeros(shape, F32))
    mean_sq = jnp.sum(sums, axis=0, keepdims=True) / float(groups * turns * SUBLANES)
    strength = jnp.broadcast_to(jnp.sqrt(mean_sq + 1e-06), shape)
    east = jnp.broadcast_to(wind_ref[0:1, :], shape)
    north = jnp.broadcast_to(wind_ref[1:2, :], shape)
    occupied = (pl.program_id(0) * LANES + iota(shape, 1)) < count_ref[0]

    def weigh(source, carry):
        decay = rate_ref[0, source] * strength
        slope, threshold = rate_ref[1, source], rate_ref[2, source]
        for j in range(turns):
            along = east * trig_ref[1, j] + north * trig_ref[0, j]
            growth = jnp.maximum(along * slope - threshold, 0.0)
            value = values[source, j] * jnp.exp(growth - decay)
            ordered[pl.ds(source * (turns * SUBLANES) + j, SUBLANES, stride=turns), :] = jnp.where(occupied, value, 0.0)
        return carry

    lax.fori_loop(0, groups, weigh, 0)
    square = (LANES, LANES)
    unit_matrix = (iota(square, 0) == iota(square, 1)).astype(jnp.bfloat16)
    turned = lax.dot_general(
        unit_matrix,
        ordered[...].astype(jnp.bfloat16),
        (((1,), (1,)), ((), ())),
        preferred_element_type=F32,
    )
    out_ref[...] = turned.astype(jnp.bfloat16)


def body(spectra, depth_class, group_speed, current, depth_slope, wind, land_mask, block_counts):
    freqs, directions, rows, lon = spectra.shape
    depths, total_freqs = group_speed.shape
    groups = lax.axis_size("comp")
    bands = lax.axis_size("band")
    comp = lax.axis_index("comp")
    band = lax.axis_index("band")
    slot_count = rows * lon * 7 // (8 * groups)
    slots = -(-slot_count // LANES) * LANES
    parts = SUBLANES // freqs
    turns = directions // parts
    units = turns // UNIT
    chunks = -(-lon // LANES)
    padded = chunks * LANES
    height = rows * SUBLANES
    spare = ((0, 0), (0, padded - lon))
    hbm = 2 * turns * height * padded

    heading = 2.0 * math.pi / directions * (
        np.arange(parts)[None, None, :] * turns + np.arange(turns)[:, None, None]
    )
    heading = np.broadcast_to(heading, (turns, freqs, parts)).reshape(turns, SUBLANES, 1)
    trig = np.stack([np.sin(heading), np.cos(heading)])
    trig = jnp.asarray(np.broadcast_to(trig, (2, turns, SUBLANES, LANES)).astype(np.float32))
    angular = 2.0 * math.pi * 0.0418 * 1.1 ** np.arange(total_freqs)
    ratio = angular / angular[-1]
    phase = 9.81 / angular
    rates = np.stack([DAMPING * ratio, GROWTH_RATE * ratio / phase, GROWTH_RATE * ratio])
    rates = np.repeat(rates.reshape(3, groups, freqs), parts, axis=2)[..., None]
    rates = jnp.asarray(np.broadcast_to(rates, (3, groups, SUBLANES, LANES)).astype(np.float32))
    powers = 2.0 ** (np.arange(LANES) - EXPONENT_ZERO)
    scale = np.stack([STEP_COUNT / powers, powers / STEP_COUNT])[:, None, :]
    scale = jnp.asarray(np.broadcast_to(scale, (2, SUBLANES, LANES)).astype(np.float32))
    latitude = (-60.0 + 120.0 * (np.arange(rows * bands) + 0.5) / (rows * bands)) * (math.pi / 180.0)
    stretch = jnp.asarray((1.0 / np.cos(latitude)).astype(np.float32))
    stretch = lax.dynamic_slice_in_dim(stretch, band * rows, rows, 0)

    land = jnp.pad(land_mask, spare, constant_values=1)
    sea = jnp.repeat((land == 0).astype(F32), SUBLANES, axis=0)
    smem = pl.BlockSpec(memory_space=pltpu.SMEM)
    vmem = pl.BlockSpec(memory_space=pltpu.VMEM)

    step = 3
    half = jax.ShapeDtypeStruct((turns, height // 2, padded), jnp.bfloat16)
    half_spec = pl.BlockSpec((step, height // 2, padded), lambda i: (i, 0, 0))
    top, bottom = call(
        arrange_kernel,
        [half, half],
        (4 * hbm, 2 * hbm),
        grid=(turns // step,),
        in_specs=[
            pl.BlockSpec((freqs, parts, step, rows, lon), lambda i: (0, 0, i, 0, 0)),
            pl.BlockSpec((height, padded), lambda i: (0, 0)),
        ],
        out_specs=[half_spec, half_spec],
        scratch_shapes=[pltpu.VMEM((step, chunks, height, LANES), F32)],
    )(spectra.reshape(freqs, parts, turns, rows, lon), sea)
    down = [(i, i + 1) for i in range(bands - 1)]
    above = lax.ppermute(bottom, "band", down)
    below = lax.ppermute(top, "band", [(j, i) for i, j in down])

    cells, ranges = call(
        index_kernel,
        [jax.ShapeDtypeStruct((groups, SUBLANES, slots), I32), jax.ShapeDtypeStruct((groups, LANES), I32)],
        (100 * groups * slots, 8 * groups * slots),
        in_specs=[vmem, smem],
        out_specs=[vmem, vmem],
    )(land.reshape(rows * chunks, LANES), block_counts)

    table = lax.dynamic_slice_in_dim(group_speed.T, comp * freqs, freqs, 0)
    table = jnp.pad(jnp.repeat(table, parts, axis=0), ((0, 0), (0, LANES - depths)))
    fields = jnp.pad(jnp.concatenate([current, depth_slope]), ((0, 0),) + spare)
    depth = jnp.pad(depth_class, spare)
    advected, coefs = call(
        advect_kernel,
        [
            jax.ShapeDtypeStruct((turns, height, padded), F32),
            jax.ShapeDtypeStruct((4, height, padded), F32),
        ],
        (50 * hbm, 4 * hbm),
        in_specs=[vmem, vmem, vmem, vmem, vmem, smem, vmem],
        out_specs=[vmem, vmem],
        scratch_shapes=[pltpu.VMEM((2, height, padded), F32)],
    )(top, bottom, table, depth, fields, stretch, trig)

    arrived = []
    for unit in range(units):
        sent = call(
            functools.partial(pack_kernel, unit, freqs),
            jax.ShapeDtypeStruct((groups, WORDS * SUBLANES, slots), I32),
            (30 * hbm, 4 * hbm),
            in_specs=[vmem] * 7 + [smem],
            out_specs=vmem,
            scratch_shapes=[pltpu.VMEM((rows * chunks, WORDS * SUBLANES, LANES), I32)],
        )(advected, above, below, coefs, trig, scale, cells, ranges)
        arrived.append(lax.all_to_all(sent, "comp", split_axis=0, concat_axis=0, tiled=True))

    own = jnp.maximum(lax.dynamic_index_in_dim(cells, comp, 0, keepdims=False)[0], 0)
    winds = jnp.pad(wind, ((0, 0),) + spare).reshape(2, rows * padded)
    winds = jnp.stack([jnp.take(winds[0], own), jnp.take(winds[1], own)])
    own_count = lax.dynamic_slice_in_dim(block_counts[0], comp, 1, 0)

    total = total_freqs * directions
    result = call(
        functools.partial(finish_kernel, units),
        jax.ShapeDtypeStruct((slot_count, total), jnp.bfloat16),
        (50 * total * slots, 6 * total * slots),
        grid=(slots // LANES,),
        in_specs=[pl.BlockSpec((groups, WORDS * SUBLANES, LANES), lambda i: (0, 0, i))] * units
        + [
            pl.BlockSpec((2, LANES), lambda i: (0, i)),
            smem,
            pl.BlockSpec((2, turns, SUBLANES, LANES), lambda i: (0, 0, 0, 0)),
            pl.BlockSpec((2, SUBLANES, LANES), lambda i: (0, 0, 0)),
            pl.BlockSpec((3, groups, SUBLANES, LANES), lambda i: (0, 0, 0, 0)),
        ],
        out_specs=pl.BlockSpec((LANES, total), lambda i: (i, 0)),
        scratch_shapes=[
            pltpu.VMEM((groups, turns, SUBLANES, LANES), F32),
            pltpu.VMEM((total, LANES), F32),
        ],
    )(*arrived, winds, own_count, trig, scale, rates)
    return result.T


def solution(mesh):
    return jax.shard_map(
        body,
        mesh=mesh,
        in_specs=(
            P("comp", None, "band", None),
            P("band", None),
            P(),
            P(None, "band", None),
            P(None, "band", None),
            P(None, "band", None),
            P("band", None),
            P("band", None),
        ),
        out_specs=P(None, ("comp", "band")),
        check_vma=False,
    )
```

```python
import functools
import math

import jax
import jax.numpy as jnp
import numpy as np
from jax import lax
from jax.experimental import pallas as pl
from jax.experimental.pallas import tpu as pltpu
from jax.sharding import PartitionSpec as P

GROWTH_RATE = 0.05
DAMPING = 1.5
TURNING_SCALE = 0.5

LANES = 128
SUBLANES = 8
UNIT = 9
WORDS = 5
STEP_COUNT = 65500.0
EXPONENT_ZERO = 99
WINDOW = 4
VMEM_BYTES = 16 * 1024 * 1024

F32 = jnp.float32
I32 = jnp.int32


def call(kernel, out_shape, cost, **options):
    flops, moved = cost
    return pl.pallas_call(
        kernel,
        out_shape=out_shape,
        cost_estimate=pl.CostEstimate(flops=flops, bytes_accessed=moved, transcendentals=0),
        compiler_params=pltpu.CompilerParams(vmem_limit_bytes=VMEM_BYTES),
        **options,
    )


def iota(shape, axis):
    return lax.broadcasted_iota(I32, shape, axis)


def upwind(speed, far_behind, behind, centre, ahead, far_ahead):
    positive = speed > 0
    near = jnp.where(positive, behind, ahead)
    after = jnp.where(positive, ahead, behind)
    far = jnp.where(positive, far_behind, far_ahead)
    return jnp.abs(speed) * (2.0 * after + far + 3.0 * (centre - 2.0 * near))


def signs(part, parts, turns, directions, j):
    sin, cos = None, None
    for h in range(parts):
        angle = 2.0 * math.pi * (h * turns + j) / directions
        if h == 0:
            sin = jnp.full(part.shape, math.sin(angle), F32)
            cos = jnp.full(part.shape, math.cos(angle), F32)
        else:
            sin = jnp.where(part == h, math.sin(angle), sin)
            cos = jnp.where(part == h, math.cos(angle), cos)
    return sin, cos


def power_table(start, sign):
    lane = iota((SUBLANES, LANES), 1)
    table = jnp.full((SUBLANES, LANES), start, F32)
    for bit in range(7):
        factor = 2.0 ** (sign * 2**bit)
        table = jnp.where((lane & (1 << bit)) != 0, table * factor, table)
    return table


def arrange_kernel(x_ref, land_ref, top_ref, bottom_ref, scratch):
    freqs, parts, step, rows, lon = x_ref.shape
    chunks = scratch.shape[1]
    tail = lon - (chunks - 1) * LANES
    filler = jnp.zeros((rows, LANES - tail), F32)
    lane = iota((SUBLANES * rows, LANES), 1)
    for j in range(step):
        for f in range(freqs):
            for h in range(parts):
                place = pl.ds(f * parts + h, rows, stride=SUBLANES)
                for k in range(chunks):
                    if k < chunks - 1:
                        piece = x_ref[f, h, j, :, k * LANES : (k + 1) * LANES].astype(F32)
                    else:
                        piece = x_ref[f, h, j, :, k * LANES : lon].astype(F32)
                        piece = jnp.concatenate([piece, filler], axis=1)
                    scratch[j, k, place, :] = piece
    initial = [None] * step
    for k in range(chunks):
        span = slice(k * LANES, (k + 1) * LANES)
        land = land_ref[:, k * LANES : min((k + 1) * LANES, lon)]
        if k == chunks - 1:
            land = jnp.concatenate([land, jnp.ones((rows, LANES - tail), I32)], axis=1)
        sea = (land == 0).astype(F32)
        sea = jnp.concatenate([jnp.broadcast_to(sea[r : r + 1], (SUBLANES, LANES)) for r in range(rows)], axis=0)
        for j in range(step):
            piece = scratch[j, k] * sea
            if k == 0:
                initial[j] = piece
            if k == chunks - 1:
                wrapped = jnp.where(
                    lane < tail + 2,
                    pltpu.roll(initial[j], tail, axis=1),
                    pltpu.roll(piece, LANES - tail, axis=1),
                )
                piece = jnp.where(lane < tail, piece, wrapped)
            piece = piece.astype(jnp.bfloat16)
            top_ref[j, :, span] = piece[: 2 * SUBLANES]
            bottom_ref[j, :, span] = piece[2 * SUBLANES :]


def index_kernel(land_ref, counts_ref, cells_ref, ranges_ref, flat):
    chunks = flat.shape[0]
    rows, lon = land_ref.shape
    per_row = chunks // rows
    tail = lon - (per_row - 1) * LANES
    flat[...] = jnp.ones(flat.shape, I32)
    for r in range(rows):
        for k in range(per_row):
            size = LANES if k < per_row - 1 else tail
            piece = land_ref[r : r + 1, k * LANES : k * LANES + size]
            flat[r * per_row + k : r * per_row + k + 1, :size] = piece
    groups, _, slots = cells_ref.shape
    spans = slots // LANES
    sea = (flat[...] == 0).astype(jnp.bfloat16)
    square = (LANES, LANES)
    ones_before = (iota(square, 1) <= iota(square, 0)).astype(jnp.bfloat16)
    ranks = lax.dot_general(ones_before, sea, (((1,), (1,)), ((), ())), preferred_element_type=F32)
    totals = jnp.dot(sea, jnp.ones(square, jnp.bfloat16), preferred_element_type=F32)
    chunk_square = (chunks, chunks)
    chunks_before = (iota(chunk_square, 1) <= iota(chunk_square, 0)).astype(jnp.bfloat16)
    through = jnp.dot(chunks_before, totals.astype(jnp.bfloat16), preferred_element_type=F32)
    through_column = through[:, :1]
    total_column = totals[:, :1]
    ranks = ranks.astype(jnp.bfloat16)
    chunk_ids = iota((chunks, slots), 0)
    slot_ids = iota((1, slots), 1)
    span_lane = iota((1, LANES), 1)
    start = jnp.int32(0)
    longest = jnp.zeros((1, 1), F32)
    for c in range(groups):
        count = counts_ref[0, c]
        number = (slot_ids + start).astype(F32)
        passed = (through_column <= number).astype(F32)
        chunk_of = jnp.sum(passed, axis=0, keepdims=True)
        before = jnp.sum(passed * total_column, axis=0, keepdims=True)
        chunk_of = chunk_of.astype(I32)
        chosen = (chunk_ids == chunk_of).astype(jnp.bfloat16)
        inside = jnp.dot(ranks, chosen, preferred_element_type=F32)
        lane = jnp.sum((inside <= number - before).astype(F32), axis=0, keepdims=True)
        valid = slot_ids < count
        found = jnp.where(valid, chunk_of * LANES + lane.astype(I32), -1)
        cells_ref[c] = jnp.broadcast_to(found, (SUBLANES, slots))
        bounds = jnp.zeros((1, LANES), I32)
        for m in range(spans):
            span = slice(m * LANES, (m + 1) * LANES)
            own = chunk_of[:, span].astype(F32)
            low = jnp.min(jnp.where(valid[:, span], own, float(chunks)), axis=1, keepdims=True)
            high = jnp.max(jnp.where(valid[:, span], own, -1.0), axis=1, keepdims=True)
            longest = jnp.maximum(longest, high - low + 1.0)
            bounds = jnp.where(span_lane == m, low.astype(I32), bounds)
            bounds = jnp.where(span_lane == m + spans, high.astype(I32), bounds)
        ranges_ref[c : c + 1, :] = bounds
        start = start + count
    ranges_ref[groups : groups + 1, :] = jnp.broadcast_to(longest.astype(I32), (1, LANES))


def advect_kernel(
    directions, stretch, top_ref, bottom_ref, speed_ref, depth_ref, current_ref, slope_ref, out_ref, coef_ref, scratch
):
    turns, _, padded = top_ref.shape
    rows, lon = depth_ref.shape
    chunks = padded // LANES
    tail = lon - (chunks - 1) * LANES
    total_freqs, depths = speed_ref.shape
    parts = directions // turns
    freqs = SUBLANES // parts
    comp, band = lax.axis_index("comp"), lax.axis_index("band")
    speeds = speed_ref[...]
    freq_ids = iota(speeds.shape, 0)
    table = []
    for f in range(freqs):
        row = jnp.sum(jnp.where(freq_ids == comp * freqs + f, speeds, 0.0), axis=0, keepdims=True)
        table.append(jnp.broadcast_to(row, (parts, depths)))
    table = jnp.concatenate(table, axis=0)
    table = jnp.concatenate([table, jnp.zeros((SUBLANES, LANES - depths), F32)], axis=1) * (1.0 / 6.0)
    shape = (SUBLANES, LANES)
    for r in range(rows):
        place = slice(r * SUBLANES, (r + 1) * SUBLANES)
        widening = jnp.float32(0.0)
        for b in range(len(stretch) // rows):
            widening = jnp.where(band == b, jnp.float32(stretch[b * rows + r]), widening)
        for k in range(chunks):
            span = slice(k * LANES, (k + 1) * LANES)

            def field(row):
                if k == chunks - 1:
                    row = jnp.concatenate([row[:, :tail], jnp.zeros((1, LANES - tail), row.dtype)], axis=1)
                return jnp.broadcast_to(row, shape)

            own = slice(k * LANES, min((k + 1) * LANES, lon))
            classes = field(depth_ref[r : r + 1, own])
            sixth = jnp.take_along_axis(table, classes, axis=1, mode="promise_in_bounds")
            coef_ref[0, place, span] = sixth
            coef_ref[1, place, span] = field(current_ref[1, r : r + 1, own]) * (1.0 / 6.0)
            coef_ref[2, place, span] = sixth * TURNING_SCALE * field(slope_ref[0, r : r + 1, own])
            coef_ref[3, place, span] = sixth * TURNING_SCALE * field(slope_ref[1, r : r + 1, own])
            scratch[0, place, span] = sixth * widening
            scratch[1, place, span] = field(current_ref[0, r : r + 1, own]) * (1.0 / 6.0)

    width = LANES * (4 if chunks % 4 == 0 else 1)

    def window(ref, j, low, high):
        parts = []
        if low < LANES:
            parts.append(ref[j, :, padded - LANES :])
            parts.append(ref[j, :, : min(high + LANES, padded)])
        else:
            parts.append(ref[j, :, low - LANES : min(high + LANES, padded)])
        if high + LANES > padded:
            parts.append(ref[j, :, :LANES])
        return jnp.concatenate([part.astype(F32) for part in parts], axis=1)

    turn_sin, turn_cos = math.sin(2.0 * math.pi / directions), math.cos(2.0 * math.pi / directions)

    def one_turn(j, carry):
        sin, cos = carry
        for low in range(0, padded, width):
            high = low + width
            centres, shifted = [], []
            for ref in (top_ref, bottom_ref):
                wide = window(ref, j, low, high)
                moved = [
                    pltpu.roll(wide, shift % wide.shape[1], axis=1)[:, LANES : LANES + width] for shift in (2, 1, -1, -2)
                ]
                for half in (slice(0, SUBLANES), slice(SUBLANES, 2 * SUBLANES)):
                    centres.append(wide[half, LANES : LANES + width])
                    shifted.append([one[half] for one in moved])
            for r in range(rows):
                place = slice(r * SUBLANES, (r + 1) * SUBLANES)
                span = slice(low, high)
                speed_x = scratch[0, place, span] * cos + scratch[1, place, span]
                speed_y = coef_ref[0, place, span] * sin + coef_ref[1, place, span]
                near = [centres[n] if 0 <= n < rows else 0.0 for n in range(r - 2, r + 3)]
                far_behind, behind, ahead, far_ahead = shifted[r]
                along = upwind(speed_x, far_behind, behind, centres[r], ahead, far_ahead)
                across = upwind(speed_y, *near)
                out_ref[j, place, span] = centres[r] - along - across
        return sin * turn_cos + cos * turn_sin, cos * turn_cos - sin * turn_sin

    part = iota((SUBLANES, 1), 0) % parts
    lax.fori_loop(0, turns, one_turn, signs(part, parts, turns, directions, 0))


def pack_kernel(
    directions, adv_ref, above_ref, below_ref, coef_ref, cells_ref, ranges_ref, out_ref, packed, turned_values
):
    turns, height, padded = adv_ref.shape
    rows = height // SUBLANES
    chunks = padded // LANES
    parts = directions // turns
    units = turns // UNIT
    shape = (SUBLANES, LANES)
    part = iota(shape, 0) % parts
    scale = power_table(STEP_COUNT * 2.0**EXPONENT_ZERO, -1)
    together = turned_values.shape[0]

    def turned(value, by):
        if by == 0:
            return value
        if by > 0:
            return jnp.where(
                part == parts - 1, pltpu.roll(value, parts - 1, axis=0), pltpu.roll(value, SUBLANES - 1, axis=0)
            )
        return jnp.where(part == 0, pltpu.roll(value, SUBLANES - parts + 1, axis=0), pltpu.roll(value, 1, axis=0))

    def refract(r, k, into):
        place = slice(r * SUBLANES, (r + 1) * SUBLANES)
        span = pl.ds(pl.multiple_of(k * LANES, LANES), LANES)
        sixth, current_y, turn_x, turn_y = [coef_ref[n, place, span] for n in range(4)]
        advected = []
        for j in range(turns):
            sin, _ = signs(part, parts, turns, directions, j)
            speed = sixth * sin + current_y
            positive = speed > 0
            ref = above_ref if r < 2 else below_ref
            outer = ref[j, :, span].astype(F32)
            low, high = outer[:SUBLANES], outer[SUBLANES:]
            if r == 0:
                share = jnp.where(positive, low - 6.0 * high, 2.0 * high)
            elif r == 1:
                share = jnp.where(positive, high, 0.0)
            elif r == rows - 2:
                share = jnp.where(positive, 0.0, low)
            else:
                share = jnp.where(positive, 2.0 * low, high - 6.0 * low)
            advected.append(adv_ref[j, place, span] - jnp.abs(speed) * share)
        around = {j: turned(advected[j % turns], j // turns) for j in range(-2, turns + 2)}
        largest = [None] * units
        for j in range(turns):
            sin, cos = signs(part, parts, turns, directions, j)
            speed = sin * turn_x - cos * turn_y
            value = around[j] - upwind(speed, *[around[n] for n in range(j - 2, j + 3)])
            turned_values[into, j] = value
            size = jnp.abs(value)
            unit = j // UNIT
            largest[unit] = size if largest[unit] is None else jnp.maximum(largest[unit], size)
        return largest

    def code(chunk, come_from, unit, largest):
        level = jnp.ceil(jnp.log2(jnp.maximum(largest, 2.0**-98)))
        level = jnp.minimum(level, 28.0).astype(I32) + EXPONENT_ZERO
        level = jnp.maximum(level, 1)
        inverse = jnp.take_along_axis(scale, level, axis=1, mode="promise_in_bounds")
        codes = [
            (turned_values[come_from, unit * UNIT + n] * inverse + 65536.5).astype(I32) for n in range(UNIT)
        ]
        first = unit * WORDS
        rest = codes[8] | (level << 17)
        for n in range(4):
            even, odd = codes[2 * n], codes[2 * n + 1]
            packed[chunk, first + n] = even | (odd << 17)
            rest = rest | ((odd >> 15) << (24 + 2 * n))
        packed[chunk, first + 4] = rest

    for r in range(rows):

        def some_chunks(i, carry):
            found = [refract(r, i * together + n, n) for n in range(together)]
            for n in range(together):
                for unit in range(units):
                    code(r * chunks + i * together + n, n, unit, found[n][unit])
            return carry

        lax.fori_loop(0, chunks // together, some_chunks, 0)

    groups, words, slots = out_ref.shape
    words = words // SUBLANES
    spans = slots // LANES
    last = rows * chunks - 1

    def merged(cells, chunk, sums):
        lane = cells - chunk * LANES
        here = (lane >= 0) & (lane < LANES)
        lane = lane & (LANES - 1)
        return tuple(
            jnp.where(
                here, jnp.take_along_axis(packed[chunk, n], lane, axis=1, mode="promise_in_bounds"), sums[n]
            )
            for n in range(words)
        )

    def one_block(c, carry):
        for m in range(spans):
            span = slice(m * LANES, (m + 1) * LANES)
            cells = cells_ref[c, :, span]
            low = ranges_ref[c, m]
            sums = tuple(jnp.zeros(shape, I32) for _ in range(words))
            for t in range(WINDOW):
                sums = merged(cells, jnp.minimum(low + t, last), sums)
            for n in range(words):
                out_ref[c, n * SUBLANES : (n + 1) * SUBLANES, span] = sums[n]
        return carry

    lax.fori_loop(0, groups, one_block, 0)

    @pl.when(ranges_ref[groups, 0] > WINDOW)
    def _():
        def longer_block(c, carry):
            for m in range(spans):
                span = slice(m * LANES, (m + 1) * LANES)
                cells = cells_ref[c, :, span]
                low, high = ranges_ref[c, m], ranges_ref[c, m + spans]
                sums = tuple(out_ref[c, n * SUBLANES : (n + 1) * SUBLANES, span] for n in range(words))
                sums = lax.fori_loop(
                    low + WINDOW, high + 1, lambda chunk, sums: merged(cells, chunk, sums), sums
                )
                for n in range(words):
                    out_ref[c, n * SUBLANES : (n + 1) * SUBLANES, span] = sums[n]
            return carry

        lax.fori_loop(0, groups, longer_block, 0)


def grow_kernel(directions, wind_ref, cells_ref, ranges_ref, out_ref, flat, slot_wind):
    groups, turns, _, slots = out_ref.shape
    rows, lon = wind_ref.shape[1:]
    chunks = flat.shape[0] // rows
    tail = lon - (chunks - 1) * LANES
    spans = slots // LANES
    parts = directions // turns
    freqs = SUBLANES // parts
    shape = (SUBLANES, LANES)
    part = iota(shape, 0) % parts
    freq = iota(shape, 0) // parts
    comp = lax.axis_index("comp")
    for r in range(rows):
        for k in range(chunks):
            size = LANES if k < chunks - 1 else tail
            for n in range(2):
                flat[r * chunks + k, n : n + 1, :size] = wind_ref[n, r : r + 1, k * LANES : k * LANES + size]
    for m in range(spans):
        span = slice(m * LANES, (m + 1) * LANES)
        cells = cells_ref[comp, :, span]

        def merged(chunk, sums):
            lane = cells - chunk * LANES
            here = (lane >= 0) & (lane < LANES)
            lane = lane & (LANES - 1)
            return jnp.where(
                here, jnp.take_along_axis(flat[chunk], lane, axis=1, mode="promise_in_bounds"), sums
            )

        found = lax.fori_loop(
            ranges_ref[comp, m], ranges_ref[comp, m + spans] + 1, merged, jnp.zeros(shape, F32)
        )
        slot_wind[0, :, span] = jnp.broadcast_to(found[0:1], shape)
        slot_wind[1, :, span] = jnp.broadcast_to(found[1:2], shape)

    rates = []
    for source in range(groups):
        slope, threshold = jnp.zeros(shape, F32), jnp.zeros(shape, F32)
        for f in range(freqs):
            angular, ratio = frequency(source * freqs + f, groups * freqs)
            slope = jnp.where(freq == f, GROWTH_RATE * ratio * angular / 9.81, slope)
            threshold = jnp.where(freq == f, GROWTH_RATE * ratio, threshold)
        rates.append((slope, threshold))

    def one_span(m, carry):
        span = pl.ds(pl.multiple_of(m * LANES, LANES), LANES)
        east, north = slot_wind[0, :, span], slot_wind[1, :, span]
        for j in range(turns):
            sin, cos = signs(part, parts, turns, directions, j)
            along = east * cos + north * sin
            for source in range(groups):
                slope, threshold = rates[source]
                out_ref[source, j, :, span] = jnp.exp(jnp.maximum(along * slope - threshold, 0.0))
        return carry

    lax.fori_loop(0, spans, one_span, 0)


def finish_kernel(freqs, arrived, counts_ref, grown_ref, out_ref, values, ordered):
    groups = arrived.shape[0]
    turns = values.shape[1]
    units = turns // UNIT
    directions_per = turns * SUBLANES
    shape = (SUBLANES, LANES)
    scale = power_table(2.0**-EXPONENT_ZERO / STEP_COUNT, 1)
    comp = lax.axis_index("comp")
    sums = [jnp.zeros(shape, F32) for _ in range(2)]
    for source in range(groups):
        for unit in range(units):
            words = [
                arrived[source, n * SUBLANES : (n + 1) * SUBLANES, :]
                for n in range(unit * WORDS, (unit + 1) * WORDS)
            ]
            rest = words[4]
            level = lax.shift_right_logical(rest, 17) & 127
            size = jnp.take_along_axis(scale, level, axis=1, mode="promise_in_bounds")
            offset = size * 65536.0
            for n in range(UNIT):
                if n == 8:
                    coded = rest & 0x1FFFF
                elif n % 2 == 0:
                    coded = words[n // 2] & 0x1FFFF
                else:
                    coded = lax.shift_right_logical(words[n // 2], 17) | (
                        lax.shift_right_logical(rest, 9 + n - 1) & 0x18000
                    )
                value = coded.astype(F32) * size - offset
                j = unit * UNIT + n
                sums[n % 2] = sums[n % 2] + value * value
                values[source, j] = value * grown_ref[source, j]
    mean_sq = jnp.sum(sums[0] + sums[1], axis=0, keepdims=True) / float(groups * directions_per)
    strength = jnp.sqrt(mean_sq + 1e-06)
    strength = jnp.broadcast_to(strength, shape)
    occupied = (pl.program_id(0) * LANES + iota(shape, 1)) < counts_ref[0, comp]
    freq = iota(shape, 0) // (SUBLANES // freqs)
    for source in range(groups):
        rate = jnp.zeros(shape, F32)
        for f in range(freqs):
            rate = jnp.where(freq == f, DAMPING * frequency(source * freqs + f, groups * freqs)[1], rate)
        factor = jnp.exp(-(rate * strength))
        for j in range(turns):
            value = jnp.where(occupied, values[source, j] * factor, 0.0)
            ordered[pl.ds(source * directions_per + j, SUBLANES, stride=turns), :] = value
    square = (LANES, LANES)
    unit_matrix = (iota(square, 0) == iota(square, 1)).astype(jnp.bfloat16)
    turned = lax.dot_general(
        unit_matrix,
        ordered[...].astype(jnp.bfloat16),
        (((1,), (1,)), ((), ())),
        preferred_element_type=F32,
    )
    out_ref[...] = turned.astype(jnp.bfloat16)


def frequency(index, count):
    angular = 2.0 * math.pi * 0.0418 * 1.1**index
    return angular, 1.1 ** (index - (count - 1))


def body(spectra, depth_class, group_speed, current, depth_slope, wind, land_mask, block_counts):
    freqs, directions, rows, lon = spectra.shape
    total_freqs = group_speed.shape[1]
    groups = lax.axis_size("comp")
    bands = lax.axis_size("band")
    slot_count = rows * lon * 7 // (8 * groups)
    slots = -(-slot_count // LANES) * LANES
    parts = SUBLANES // freqs
    turns = directions // parts
    units = turns // UNIT
    chunks = -(-lon // LANES)
    padded = chunks * LANES
    height = rows * SUBLANES
    words = units * WORDS
    hbm = 2 * turns * height * padded
    latitude = (-60.0 + 120.0 * (np.arange(rows * bands) + 0.5) / (rows * bands)) * (math.pi / 180.0)
    stretch = [float(value) for value in 1.0 / np.cos(latitude)]
    smem = pl.BlockSpec(memory_space=pltpu.SMEM)
    vmem = pl.BlockSpec(memory_space=pltpu.VMEM)

    step = 3
    half = jax.ShapeDtypeStruct((turns, height // 2, padded), jnp.bfloat16)
    half_spec = pl.BlockSpec((step, height // 2, padded), lambda i: (i, 0, 0))
    top, bottom = call(
        arrange_kernel,
        [half, half],
        (4 * hbm, 2 * hbm),
        grid=(turns // step,),
        in_specs=[
            pl.BlockSpec((freqs, parts, step, rows, lon), lambda i: (0, 0, i, 0, 0)),
            pl.BlockSpec((rows, lon), lambda i: (0, 0)),
        ],
        out_specs=[half_spec, half_spec],
        scratch_shapes=[pltpu.VMEM((step, chunks, height, LANES), F32)],
    )(spectra.reshape(freqs, parts, turns, rows, lon), land_mask)
    down = [(i, i + 1) for i in range(bands - 1)]
    above = lax.ppermute(bottom, "band", down)
    below = lax.ppermute(top, "band", [(j, i) for i, j in down])

    range_rows = 2 * SUBLANES if groups < 2 * SUBLANES else 3 * SUBLANES
    cells, ranges = call(
        index_kernel,
        [
            jax.ShapeDtypeStruct((groups, SUBLANES, slots), I32),
            jax.ShapeDtypeStruct((range_rows, LANES), I32),
        ],
        (100 * groups * slots, 8 * groups * slots),
        in_specs=[vmem, smem],
        out_specs=[vmem, vmem],
        scratch_shapes=[pltpu.VMEM((rows * chunks, LANES), I32)],
    )(land_mask, block_counts)

    advected, coefs = call(
        functools.partial(advect_kernel, directions, stretch),
        [
            jax.ShapeDtypeStruct((turns, height, padded), F32),
            jax.ShapeDtypeStruct((4, height, padded), F32),
        ],
        (50 * hbm, 4 * hbm),
        in_specs=[vmem] * 6,
        out_specs=[vmem, vmem],
        scratch_shapes=[pltpu.VMEM((2, height, padded), F32)],
    )(top, bottom, group_speed.T, depth_class, current, depth_slope)

    sent = call(
        functools.partial(pack_kernel, directions),
        jax.ShapeDtypeStruct((groups, words * SUBLANES, slots), I32),
        (50 * hbm, 4 * hbm),
        in_specs=[vmem] * 5 + [smem],
        out_specs=vmem,
        scratch_shapes=[
            pltpu.VMEM((rows * chunks, words, SUBLANES, LANES), I32),
            pltpu.VMEM((4 if chunks % 4 == 0 else 1, turns, SUBLANES, LANES), F32),
        ],
    )(advected, above, below, coefs, cells, ranges)
    arrived = lax.all_to_all(sent, "comp", split_axis=0, concat_axis=0, tiled=True)

    total = total_freqs * directions
    grown = call(
        functools.partial(grow_kernel, directions),
        jax.ShapeDtypeStruct((groups, turns, SUBLANES, slots), F32),
        (20 * total * slots, 4 * total * slots),
        in_specs=[vmem, vmem, smem],
        out_specs=vmem,
        scratch_shapes=[
            pltpu.VMEM((rows * chunks, SUBLANES, LANES), F32),
            pltpu.VMEM((2, SUBLANES, slots), F32),
        ],
    )(wind, cells, ranges)

    result = call(
        functools.partial(finish_kernel, freqs),
        jax.ShapeDtypeStruct((slot_count, total), jnp.bfloat16),
        (50 * total * slots, 6 * total * slots),
        grid=(slots // LANES,),
        in_specs=[
            pl.BlockSpec((groups, words * SUBLANES, LANES), lambda i: (0, 0, i)),
            smem,
            pl.BlockSpec((groups, turns, SUBLANES, LANES), lambda i: (0, 0, 0, i)),
        ],
        out_specs=pl.BlockSpec((LANES, total), lambda i: (i, 0)),
        scratch_shapes=[
            pltpu.VMEM((groups, turns, SUBLANES, LANES), F32),
            pltpu.VMEM((total, LANES), F32),
        ],
    )(arrived, block_counts, grown)
    return result.T


def solution(mesh):
    return jax.shard_map(
        body,
        mesh=mesh,
        in_specs=(
            P("comp", None, "band", None),
            P("band", None),
            P(),
            P(None, "band", None),
            P(None, "band", None),
            P(None, "band", None),
            P("band", None),
            P("band", None),
        ),
        out_specs=P(None, ("comp", "band")),
        check_vma=False,
    )
```

```python
import functools
import math

import jax
import jax.numpy as jnp
import numpy as np
from jax import lax
from jax.experimental import pallas as pl
from jax.experimental.pallas import tpu as pltpu
from jax.sharding import PartitionSpec as P

GROWTH_RATE = 0.05
DAMPING = 1.5
TURNING_SCALE = 0.5

LANES = 128
SUBLANES = 8
UNIT = 9
WORDS = 5
STEP_COUNT = 65500.0
EXPONENT_ZERO = 99
WINDOW = 4
VMEM_BYTES = 16 * 1024 * 1024
WHOLE_VMEM = 62_000_000

F32 = jnp.float32
I32 = jnp.int32


def call(kernel, out_shape, cost, vmem=VMEM_BYTES, **options):
    flops, moved = cost
    return pl.pallas_call(
        kernel,
        out_shape=out_shape,
        cost_estimate=pl.CostEstimate(flops=flops, bytes_accessed=moved, transcendentals=0),
        compiler_params=pltpu.CompilerParams(vmem_limit_bytes=vmem),
        **options,
    )


def iota(shape, axis):
    return lax.broadcasted_iota(I32, shape, axis)


def upwind(speed, far_behind, behind, centre, ahead, far_ahead):
    positive = speed > 0
    near = jnp.where(positive, behind, ahead)
    after = jnp.where(positive, ahead, behind)
    far = jnp.where(positive, far_behind, far_ahead)
    return jnp.abs(speed) * (2.0 * after + far + 3.0 * (centre - 2.0 * near))


def signs(part, parts, turns, directions, j):
    sin, cos = None, None
    for h in range(parts):
        angle = 2.0 * math.pi * (h * turns + j) / directions
        if h == 0:
            sin = jnp.full(part.shape, math.sin(angle), F32)
            cos = jnp.full(part.shape, math.cos(angle), F32)
        else:
            sin = jnp.where(part == h, math.sin(angle), sin)
            cos = jnp.where(part == h, math.cos(angle), cos)
    return sin, cos


def power_table(start, sign):
    lane = iota((SUBLANES, LANES), 1)
    table = jnp.full((SUBLANES, LANES), start, F32)
    for bit in range(7):
        factor = 2.0 ** (sign * 2**bit)
        table = jnp.where((lane & (1 << bit)) != 0, table * factor, table)
    return table


def arrange_kernel(x_ref, land_ref, top_ref, bottom_ref, scratch):
    freqs, parts, step, rows, lon = x_ref.shape
    chunks = scratch.shape[1]
    tail = lon - (chunks - 1) * LANES
    filler = jnp.zeros((rows, LANES - tail), F32)
    lane = iota((SUBLANES * rows, LANES), 1)
    for j in range(step):
        for f in range(freqs):
            for h in range(parts):
                place = pl.ds(f * parts + h, rows, stride=SUBLANES)
                for k in range(chunks):
                    if k < chunks - 1:
                        piece = x_ref[f, h, j, :, k * LANES : (k + 1) * LANES].astype(F32)
                    else:
                        piece = x_ref[f, h, j, :, k * LANES : lon].astype(F32)
                        piece = jnp.concatenate([piece, filler], axis=1)
                    scratch[j, k, place, :] = piece
    initial = [None] * step
    for k in range(chunks):
        span = slice(k * LANES, (k + 1) * LANES)
        land = land_ref[:, k * LANES : min((k + 1) * LANES, lon)]
        if k == chunks - 1:
            land = jnp.concatenate([land, jnp.ones((rows, LANES - tail), I32)], axis=1)
        sea = (land == 0).astype(F32)
        sea = jnp.concatenate([jnp.broadcast_to(sea[r : r + 1], (SUBLANES, LANES)) for r in range(rows)], axis=0)
        for j in range(step):
            piece = scratch[j, k] * sea
            if k == 0:
                initial[j] = piece
            if k == chunks - 1:
                wrapped = jnp.where(
                    lane < tail + 2,
                    pltpu.roll(initial[j], tail, axis=1),
                    pltpu.roll(piece, LANES - tail, axis=1),
                )
                piece = jnp.where(lane < tail, piece, wrapped)
            piece = piece.astype(jnp.bfloat16)
            top_ref[j, :, span] = piece[: 2 * SUBLANES]
            bottom_ref[j, :, span] = piece[2 * SUBLANES :]


def index_kernel(land_ref, counts_ref, cells_ref, ranges_ref, flat):
    chunks = flat.shape[0]
    rows, lon = land_ref.shape
    per_row = chunks // rows
    tail = lon - (per_row - 1) * LANES
    flat[...] = jnp.ones(flat.shape, I32)
    for r in range(rows):
        for k in range(per_row):
            size = LANES if k < per_row - 1 else tail
            piece = land_ref[r : r + 1, k * LANES : k * LANES + size]
            flat[r * per_row + k : r * per_row + k + 1, :size] = piece
    groups, _, slots = cells_ref.shape
    spans = slots // LANES
    sea = (flat[...] == 0).astype(jnp.bfloat16)
    square = (LANES, LANES)
    ones_before = (iota(square, 1) <= iota(square, 0)).astype(jnp.bfloat16)
    ranks = lax.dot_general(ones_before, sea, (((1,), (1,)), ((), ())), preferred_element_type=F32)
    totals = jnp.dot(sea, jnp.ones(square, jnp.bfloat16), preferred_element_type=F32)
    chunk_square = (chunks, chunks)
    chunks_before = (iota(chunk_square, 1) <= iota(chunk_square, 0)).astype(jnp.bfloat16)
    through = jnp.dot(chunks_before, totals.astype(jnp.bfloat16), preferred_element_type=F32)
    through_column = through[:, :1]
    total_column = totals[:, :1]
    ranks = ranks.astype(jnp.bfloat16)
    chunk_ids = iota((chunks, slots), 0)
    slot_ids = iota((1, slots), 1)
    span_lane = iota((1, LANES), 1)
    start = jnp.int32(0)
    longest = jnp.zeros((1, 1), F32)
    for c in range(groups):
        count = counts_ref[0, c]
        number = (slot_ids + start).astype(F32)
        passed = (through_column <= number).astype(F32)
        chunk_of = jnp.sum(passed, axis=0, keepdims=True)
        before = jnp.sum(passed * total_column, axis=0, keepdims=True)
        chunk_of = chunk_of.astype(I32)
        chosen = (chunk_ids == chunk_of).astype(jnp.bfloat16)
        inside = jnp.dot(ranks, chosen, preferred_element_type=F32)
        lane = jnp.sum((inside <= number - before).astype(F32), axis=0, keepdims=True)
        valid = slot_ids < count
        found = jnp.where(valid, chunk_of * LANES + lane.astype(I32), -1)
        cells_ref[c] = jnp.broadcast_to(found, (SUBLANES, slots))
        bounds = jnp.zeros((1, LANES), I32)
        final = jnp.zeros((1, 1), F32)
        for m in range(spans):
            span = slice(m * LANES, (m + 1) * LANES)
            own = chunk_of[:, span].astype(F32)
            low = jnp.min(jnp.where(valid[:, span], own, float(chunks)), axis=1, keepdims=True)
            high = jnp.max(jnp.where(valid[:, span], own, -1.0), axis=1, keepdims=True)
            longest = jnp.maximum(longest, high - low + 1.0)
            final = jnp.maximum(final, high)
            bounds = jnp.where(span_lane == m, low.astype(I32), bounds)
            bounds = jnp.where(span_lane == m + spans, high.astype(I32), bounds)
        bounds = jnp.where(span_lane == 2 * spans, final.astype(I32), bounds)
        ranges_ref[c : c + 1, :] = bounds
        start = start + count
    ranges_ref[groups : groups + 1, :] = jnp.broadcast_to(longest.astype(I32), (1, LANES))


def advect_kernel(
    directions, stretch, top_ref, bottom_ref, speed_ref, depth_ref, current_ref, slope_ref, out_ref, coef_ref, scratch
):
    turns, _, padded = top_ref.shape
    rows, lon = depth_ref.shape
    chunks = padded // LANES
    tail = lon - (chunks - 1) * LANES
    total_freqs, depths = speed_ref.shape
    parts = directions // turns
    freqs = SUBLANES // parts
    comp, band = lax.axis_index("comp"), lax.axis_index("band")
    speeds = speed_ref[...]
    freq_ids = iota(speeds.shape, 0)
    table = []
    for f in range(freqs):
        row = jnp.sum(jnp.where(freq_ids == comp * freqs + f, speeds, 0.0), axis=0, keepdims=True)
        table.append(jnp.broadcast_to(row, (parts, depths)))
    table = jnp.concatenate(table, axis=0)
    table = jnp.concatenate([table, jnp.zeros((SUBLANES, LANES - depths), F32)], axis=1) * (1.0 / 6.0)
    shape = (SUBLANES, LANES)
    for r in range(rows):
        place = slice(r * SUBLANES, (r + 1) * SUBLANES)
        widening = jnp.float32(0.0)
        for b in range(len(stretch) // rows):
            widening = jnp.where(band == b, jnp.float32(stretch[b * rows + r]), widening)
        for k in range(chunks):
            span = slice(k * LANES, (k + 1) * LANES)

            def field(row):
                if k == chunks - 1:
                    row = jnp.concatenate([row[:, :tail], jnp.zeros((1, LANES - tail), row.dtype)], axis=1)
                return jnp.broadcast_to(row, shape)

            own = slice(k * LANES, min((k + 1) * LANES, lon))
            classes = field(depth_ref[r : r + 1, own])
            sixth = jnp.take_along_axis(table, classes, axis=1, mode="promise_in_bounds")
            coef_ref[0, place, span] = sixth
            coef_ref[1, place, span] = field(current_ref[1, r : r + 1, own]) * (1.0 / 6.0)
            coef_ref[2, place, span] = sixth * TURNING_SCALE * field(slope_ref[0, r : r + 1, own])
            coef_ref[3, place, span] = sixth * TURNING_SCALE * field(slope_ref[1, r : r + 1, own])
            scratch[0, place, span] = sixth * widening
            scratch[1, place, span] = field(current_ref[0, r : r + 1, own]) * (1.0 / 6.0)

    width = LANES * (4 if chunks % 4 == 0 else 1)

    def window(ref, j, low, high):
        parts = []
        if low < LANES:
            parts.append(ref[j, :, padded - LANES :])
            parts.append(ref[j, :, : min(high + LANES, padded)])
        else:
            parts.append(ref[j, :, low - LANES : min(high + LANES, padded)])
        if high + LANES > padded:
            parts.append(ref[j, :, :LANES])
        return jnp.concatenate([part.astype(F32) for part in parts], axis=1)

    turn_sin, turn_cos = math.sin(2.0 * math.pi / directions), math.cos(2.0 * math.pi / directions)

    def one_turn(j, carry):
        sin, cos = carry
        for low in range(0, padded, width):
            high = low + width
            centres, shifted = [], []
            for ref in (top_ref, bottom_ref):
                wide = window(ref, j, low, high)
                moved = [
                    pltpu.roll(wide, shift % wide.shape[1], axis=1)[:, LANES : LANES + width] for shift in (2, 1, -1, -2)
                ]
                for half in (slice(0, SUBLANES), slice(SUBLANES, 2 * SUBLANES)):
                    centres.append(wide[half, LANES : LANES + width])
                    shifted.append([one[half] for one in moved])
            for r in range(rows):
                place = slice(r * SUBLANES, (r + 1) * SUBLANES)
                span = slice(low, high)
                speed_x = scratch[0, place, span] * cos + scratch[1, place, span]
                speed_y = coef_ref[0, place, span] * sin + coef_ref[1, place, span]
                near = [centres[n] if 0 <= n < rows else 0.0 for n in range(r - 2, r + 3)]
                far_behind, behind, ahead, far_ahead = shifted[r]
                along = upwind(speed_x, far_behind, behind, centres[r], ahead, far_ahead)
                across = upwind(speed_y, *near)
                out_ref[j, place, span] = centres[r] - along - across
        return sin * turn_cos + cos * turn_sin, cos * turn_cos - sin * turn_sin

    part = iota((SUBLANES, 1), 0) % parts
    lax.fori_loop(0, turns, one_turn, signs(part, parts, turns, directions, 0))


def pack_kernel(directions, offsets, adv_ref, above_ref, below_ref, coef_ref, cells_ref, ranges_ref, after_ref, *refs):
    out_refs, (packed, turned_values, trig) = refs[:-3], refs[-3:]
    turns, height, padded = adv_ref.shape
    rows = height // SUBLANES
    chunks = padded // LANES
    parts = directions // turns
    units = turns // UNIT
    shape = (SUBLANES, LANES)
    part = iota(shape, 0) % parts
    scale = power_table(STEP_COUNT * 2.0**EXPONENT_ZERO, -1)
    together = turned_values.shape[0]
    for j in range(turns):
        trig[0, j], trig[1, j] = signs(part, parts, turns, directions, j)

    def turned(value, by):
        if by == 0:
            return value
        if by > 0:
            return jnp.where(
                part == parts - 1, pltpu.roll(value, parts - 1, axis=0), pltpu.roll(value, SUBLANES - 1, axis=0)
            )
        return jnp.where(part == 0, pltpu.roll(value, SUBLANES - parts + 1, axis=0), pltpu.roll(value, 1, axis=0))

    def refract(r, k, into):
        place = slice(r * SUBLANES, (r + 1) * SUBLANES)
        span = pl.ds(pl.multiple_of(k * LANES, LANES), LANES)
        sixth, current_y, turn_x, turn_y = [coef_ref[n, place, span] for n in range(4)]
        advected = []
        for j in range(turns):
            speed = sixth * trig[0, j] + current_y
            positive = speed > 0
            ref = above_ref if r < 2 else below_ref
            outer = ref[j, :, span].astype(F32)
            low, high = outer[:SUBLANES], outer[SUBLANES:]
            if r == 0:
                share = jnp.where(positive, low - 6.0 * high, 2.0 * high)
            elif r == 1:
                share = jnp.where(positive, high, 0.0)
            elif r == rows - 2:
                share = jnp.where(positive, 0.0, low)
            else:
                share = jnp.where(positive, 2.0 * low, high - 6.0 * low)
            advected.append(adv_ref[j, place, span] - jnp.abs(speed) * share)
        around = {j: turned(advected[j % turns], j // turns) for j in range(-2, turns + 2)}
        largest = [None] * units
        for j in range(turns):
            speed = trig[0, j] * turn_x - trig[1, j] * turn_y
            value = around[j] - upwind(speed, *[around[n] for n in range(j - 2, j + 3)])
            turned_values[into, j] = value
            size = jnp.abs(value)
            unit = j // UNIT
            largest[unit] = size if largest[unit] is None else jnp.maximum(largest[unit], size)
        return largest

    def code(chunk, come_from, unit, largest):
        level = jnp.ceil(jnp.log2(jnp.maximum(largest, 2.0**-98)))
        level = jnp.minimum(level, 28.0).astype(I32) + EXPONENT_ZERO
        level = jnp.maximum(level, 1)
        inverse = jnp.take_along_axis(scale, level, axis=1, mode="promise_in_bounds")
        codes = [
            (turned_values[come_from, unit * UNIT + n] * inverse + 65536.5).astype(I32) for n in range(UNIT)
        ]
        first = unit * WORDS
        rest = codes[8] | (level << 17)
        for n in range(4):
            even, odd = codes[2 * n], codes[2 * n + 1]
            packed[chunk, first + n] = even | (odd << 17)
            rest = rest | ((odd >> 15) << (24 + 2 * n))
        packed[chunk, first + 4] = rest

    half = len(offsets)
    _, words, slots = out_refs[0].shape
    words = words // SUBLANES
    spans = slots // LANES
    comp = lax.axis_index("comp")
    base = ((comp ^ offsets[0]) // half) * half
    first_set = ranges_ref[base, 0] // together
    last_set = ranges_ref[base + half - 1, 2 * spans] // together
    sets = chunks // together
    for r in range(rows):

        def some_chunks(i, carry):
            found = [refract(r, i * together + n, n) for n in range(together)]
            for n in range(together):
                for unit in range(units):
                    code(r * chunks + i * together + n, n, unit, found[n][unit])
            return carry

        low = jnp.clip(first_set - r * sets, 0, sets)
        high = jnp.clip(last_set + 1 - r * sets, 0, sets)
        lax.fori_loop(low, high, some_chunks, 0)

    last = rows * chunks - 1

    def merged(cells, chunk, sums):
        lane = cells - chunk * LANES
        here = (lane >= 0) & (lane < LANES)
        lane = lane & (LANES - 1)
        return tuple(
            jnp.where(
                here, jnp.take_along_axis(packed[chunk, n], lane, axis=1, mode="promise_in_bounds"), sums[n]
            )
            for n in range(words)
        )

    if len(out_refs) == half:
        places = [(comp ^ offset, out_ref, 0) for offset, out_ref in zip(offsets, out_refs)]
    else:
        places = [(base + n, out_refs[0], n) for n in range(half)]
    for block, out_ref, at in places:
        for m in range(spans):
            span = slice(m * LANES, (m + 1) * LANES)
            cells = cells_ref[block, :, span]
            low = ranges_ref[block, m]
            sums = tuple(jnp.zeros(shape, I32) for _ in range(words))
            for t in range(WINDOW):
                sums = merged(cells, jnp.minimum(low + t, last), sums)
            for n in range(words):
                out_ref[at, n * SUBLANES : (n + 1) * SUBLANES, span] = sums[n]

    @pl.when(ranges_ref[cells_ref.shape[0], 0] > WINDOW)
    def _():
        for block, out_ref, at in places:
            for m in range(spans):
                span = slice(m * LANES, (m + 1) * LANES)
                cells = cells_ref[block, :, span]
                low, high = ranges_ref[block, m], ranges_ref[block, m + spans]
                sums = tuple(out_ref[at, n * SUBLANES : (n + 1) * SUBLANES, span] for n in range(words))
                sums = lax.fori_loop(
                    low + WINDOW, high + 1, lambda chunk, sums: merged(cells, chunk, sums), sums
                )
                for n in range(words):
                    out_ref[at, n * SUBLANES : (n + 1) * SUBLANES, span] = sums[n]


def grow_kernel(directions, wind_ref, cells_ref, ranges_ref, out_ref, flat, slot_wind):
    groups, turns, _, slots = out_ref.shape
    rows, lon = wind_ref.shape[1:]
    chunks = flat.shape[0] // rows
    tail = lon - (chunks - 1) * LANES
    spans = slots // LANES
    parts = directions // turns
    freqs = SUBLANES // parts
    shape = (SUBLANES, LANES)
    part = iota(shape, 0) % parts
    freq = iota(shape, 0) // parts
    comp = lax.axis_index("comp")
    for r in range(rows):
        for k in range(chunks):
            size = LANES if k < chunks - 1 else tail
            for n in range(2):
                flat[r * chunks + k, n : n + 1, :size] = wind_ref[n, r : r + 1, k * LANES : k * LANES + size]
    for m in range(spans):
        span = slice(m * LANES, (m + 1) * LANES)
        cells = cells_ref[comp, :, span]

        def merged(chunk, sums):
            lane = cells - chunk * LANES
            here = (lane >= 0) & (lane < LANES)
            lane = lane & (LANES - 1)
            return jnp.where(
                here, jnp.take_along_axis(flat[chunk], lane, axis=1, mode="promise_in_bounds"), sums
            )

        found = lax.fori_loop(
            ranges_ref[comp, m], ranges_ref[comp, m + spans] + 1, merged, jnp.zeros(shape, F32)
        )
        slot_wind[0, :, span] = jnp.broadcast_to(found[0:1], shape)
        slot_wind[1, :, span] = jnp.broadcast_to(found[1:2], shape)

    rates, places = [], []
    half = groups // 2
    for source in range(groups):
        index = source % half
        places.append(jnp.where(comp // half == source // half, index, half + ((comp % half) ^ index)))
        slope, threshold = jnp.zeros(shape, F32), jnp.zeros(shape, F32)
        for f in range(freqs):
            angular, ratio = frequency(source * freqs + f, groups * freqs)
            slope = jnp.where(freq == f, GROWTH_RATE * ratio * angular / 9.81, slope)
            threshold = jnp.where(freq == f, GROWTH_RATE * ratio, threshold)
        rates.append((slope, threshold))

    def one_span(m, carry):
        span = pl.ds(pl.multiple_of(m * LANES, LANES), LANES)
        east, north = slot_wind[0, :, span], slot_wind[1, :, span]
        for j in range(turns):
            sin, cos = signs(part, parts, turns, directions, j)
            along = east * cos + north * sin
            for source in range(groups):
                slope, threshold = rates[source]
                out_ref[places[source], j, :, span] = jnp.exp(jnp.maximum(along * slope - threshold, 0.0))
        return carry

    lax.fori_loop(0, spans, one_span, 0)


def decode(arrived_refs, grown_ref, scale, store):
    sums = [jnp.zeros((SUBLANES, LANES), F32) for _ in range(2)]
    turns = grown_ref.shape[1]
    for source, (arrived, at) in enumerate(arrived_refs):
        for unit in range(turns // UNIT):
            words = [
                arrived[at, n * SUBLANES : (n + 1) * SUBLANES, :]
                for n in range(unit * WORDS, (unit + 1) * WORDS)
            ]
            rest = words[4]
            level = lax.shift_right_logical(rest, 17) & 127
            size = jnp.take_along_axis(scale, level, axis=1, mode="promise_in_bounds")
            offset = size * 65536.0
            for n in range(UNIT):
                if n == 8:
                    coded = rest & 0x1FFFF
                elif n % 2 == 0:
                    coded = words[n // 2] & 0x1FFFF
                else:
                    coded = lax.shift_right_logical(words[n // 2], 17) | (
                        lax.shift_right_logical(rest, 9 + n - 1) & 0x18000
                    )
                value = coded.astype(F32) * size - offset
                sums[n % 2] = sums[n % 2] + value * value
                j = unit * UNIT + n
                store(source, j, value * grown_ref[source, j])
    return sums[0] + sums[1]


def early_kernel(half, *refs):
    arrived_refs, (grown_ref, out_ref, sums_ref) = [(ref, 0) for ref in refs[:half]], refs[half:]
    own = lax.axis_index("comp") % half

    def store(source, j, value):
        out_ref[own ^ source, j] = value

    sums_ref[...] = decode(arrived_refs, grown_ref, power_table(2.0**-EXPONENT_ZERO / STEP_COUNT, 1), store)


def finish_kernel(freqs, half, *refs):
    arrived_ref, grown_ref, early_ref, sums_ref, counts_ref, out_ref, values, ordered = refs
    arrived_refs = [(arrived_ref, n) for n in range(half)]
    groups = 2 * half
    turns = values.shape[1]
    each = turns * SUBLANES
    shape = (SUBLANES, LANES)
    comp = lax.axis_index("comp")
    side = comp // half

    def store(source, j, value):
        values[source, j] = value

    sums = decode(arrived_refs, grown_ref, power_table(2.0**-EXPONENT_ZERO / STEP_COUNT, 1), store)
    mean_sq = jnp.sum(sums + sums_ref[...], axis=0, keepdims=True) / float(groups * each)
    strength = jnp.broadcast_to(jnp.sqrt(mean_sq + 1e-06), shape)
    occupied = (pl.program_id(0) * LANES + iota(shape, 1)) < counts_ref[0, comp]
    freq = iota(shape, 0) // (SUBLANES // freqs)
    for far in range(2):
        place = side ^ far
        step = jnp.where(place == 0, jnp.float32(1.0), jnp.float32(1.1 ** (half * freqs)))
        for source in range(half):
            rate = jnp.zeros(shape, F32)
            for f in range(freqs):
                rate = jnp.where(freq == f, DAMPING * frequency(source * freqs + f, groups * freqs)[1], rate)
            factor = jnp.exp(-(rate * step * strength))
            for j in range(turns):
                value = early_ref[source, j] if far else values[source, j]
                value = jnp.where(occupied, value * factor, 0.0)
                ordered[place, pl.ds(source * each + j, SUBLANES, stride=turns), :] = value
    square = (LANES, LANES)
    unit_matrix = (iota(square, 0) == iota(square, 1)).astype(jnp.bfloat16)
    for place in range(2):
        turned = lax.dot_general(
            unit_matrix,
            ordered[place].astype(jnp.bfloat16),
            (((1,), (1,)), ((), ())),
            preferred_element_type=F32,
        )
        out_ref[:, place * half * each : (place + 1) * half * each] = turned.astype(jnp.bfloat16)


def frequency(index, count):
    angular = 2.0 * math.pi * 0.0418 * 1.1**index
    return angular, 1.1 ** (index - (count - 1))


def body(spectra, depth_class, group_speed, current, depth_slope, wind, land_mask, block_counts):
    freqs, directions, rows, lon = spectra.shape
    total_freqs = group_speed.shape[1]
    groups = lax.axis_size("comp")
    bands = lax.axis_size("band")
    slot_count = rows * lon * 7 // (8 * groups)
    slots = -(-slot_count // LANES) * LANES
    parts = SUBLANES // freqs
    turns = directions // parts
    units = turns // UNIT
    chunks = -(-lon // LANES)
    padded = chunks * LANES
    height = rows * SUBLANES
    words = units * WORDS
    hbm = 2 * turns * height * padded
    latitude = (-60.0 + 120.0 * (np.arange(rows * bands) + 0.5) / (rows * bands)) * (math.pi / 180.0)
    stretch = [float(value) for value in 1.0 / np.cos(latitude)]
    smem = pl.BlockSpec(memory_space=pltpu.SMEM)
    vmem = pl.BlockSpec(memory_space=pltpu.VMEM)

    step = 3
    half = jax.ShapeDtypeStruct((turns, height // 2, padded), jnp.bfloat16)
    half_spec = pl.BlockSpec((step, height // 2, padded), lambda i: (i, 0, 0))
    top, bottom = call(
        arrange_kernel,
        [half, half],
        (4 * hbm, 2 * hbm),
        vmem=WHOLE_VMEM,
        grid=(turns // step,),
        in_specs=[
            pl.BlockSpec((freqs, parts, step, rows, lon), lambda i: (0, 0, i, 0, 0)),
            pl.BlockSpec((rows, lon), lambda i: (0, 0)),
        ],
        out_specs=[half_spec, half_spec],
        scratch_shapes=[pltpu.VMEM((step, chunks, height, LANES), F32)],
    )(spectra.reshape(freqs, parts, turns, rows, lon), land_mask)
    down = [(i, i + 1) for i in range(bands - 1)]
    above = lax.ppermute(bottom, "band", down)
    below = lax.ppermute(top, "band", [(j, i) for i, j in down])

    range_rows = 2 * SUBLANES if groups < 2 * SUBLANES else 3 * SUBLANES
    cells, ranges = call(
        index_kernel,
        [
            jax.ShapeDtypeStruct((groups, SUBLANES, slots), I32),
            jax.ShapeDtypeStruct((range_rows, LANES), I32),
        ],
        (100 * groups * slots, 8 * groups * slots),
        in_specs=[vmem, smem],
        out_specs=[vmem, vmem],
        scratch_shapes=[pltpu.VMEM((rows * chunks, LANES), I32)],
    )(land_mask, block_counts)

    advected, coefs = call(
        functools.partial(advect_kernel, directions, stretch),
        [
            jax.ShapeDtypeStruct((turns, height, padded), F32),
            jax.ShapeDtypeStruct((4, height, padded), F32),
        ],
        (50 * hbm, 4 * hbm),
        in_specs=[vmem] * 6,
        out_specs=[vmem, vmem],
        scratch_shapes=[pltpu.VMEM((2, height, padded), F32)],
    )(top, bottom, group_speed.T, depth_class, current, depth_slope)

    half = groups // 2
    block = (words * SUBLANES, slots)
    after, shipped = ranges, []
    for offsets, outputs in ((range(half, groups), [(1,) + block] * half), (range(half), [(half,) + block])):
        shipped.append(
            call(
                functools.partial(pack_kernel, directions, tuple(offsets)),
                [jax.ShapeDtypeStruct(shape, I32) for shape in outputs],
                (25 * hbm, 3 * hbm),
                in_specs=[vmem] * 5 + [smem, pl.BlockSpec(memory_space=pl.ANY)],
                out_specs=[vmem] * len(outputs),
                scratch_shapes=[
                    pltpu.VMEM((rows * chunks, words, SUBLANES, LANES), I32),
                    pltpu.VMEM((4 if chunks % 4 == 0 else 1, turns, SUBLANES, LANES), F32),
                    pltpu.VMEM((2, turns, SUBLANES, LANES), F32),
                ],
            )(advected, above, below, coefs, cells, ranges, after)
        )
        after = shipped[0][0]
    far = [
        lax.ppermute(part, "comp", [(i, i ^ (half + n)) for i in range(groups)]) for n, part in enumerate(shipped[0])
    ]
    halves = [list(range(half)), list(range(half, groups))]
    near = lax.all_to_all(shipped[1][0], "comp", split_axis=0, concat_axis=0, axis_index_groups=halves, tiled=True)

    total = total_freqs * directions
    grown = call(
        functools.partial(grow_kernel, directions),
        jax.ShapeDtypeStruct((groups, turns, SUBLANES, slots), F32),
        (20 * total * slots, 4 * total * slots),
        in_specs=[vmem, vmem, smem],
        out_specs=vmem,
        scratch_shapes=[
            pltpu.VMEM((rows * chunks, SUBLANES, LANES), F32),
            pltpu.VMEM((2, SUBLANES, slots), F32),
        ],
    )(wind, cells, ranges)

    arrived_spec = pl.BlockSpec((1, words * SUBLANES, LANES), lambda i: (0, 0, i))
    half_block = (half, turns, SUBLANES, LANES)
    sums_spec = pl.BlockSpec((SUBLANES, LANES), lambda i: (0, i))
    early, sums = call(
        functools.partial(early_kernel, half),
        [
            jax.ShapeDtypeStruct((half, turns, SUBLANES, slots), F32),
            jax.ShapeDtypeStruct((SUBLANES, slots), F32),
        ],
        (10 * total * slots, 4 * total * slots),
        grid=(slots // LANES,),
        in_specs=[arrived_spec] * half + [pl.BlockSpec(half_block, lambda i: (1, 0, 0, i))],
        out_specs=[pl.BlockSpec(half_block, lambda i: (0, 0, 0, i)), sums_spec],
    )(*far, grown)

    result = call(
        functools.partial(finish_kernel, freqs, half),
        jax.ShapeDtypeStruct((slot_count, total), jnp.bfloat16),
        (50 * total * slots, 6 * total * slots),
        grid=(slots // LANES,),
        in_specs=[
            pl.BlockSpec((half, words * SUBLANES, LANES), lambda i: (0, 0, i)),
            pl.BlockSpec(half_block, lambda i: (0, 0, 0, i)),
            pl.BlockSpec(half_block, lambda i: (0, 0, 0, i)),
            sums_spec,
            smem,
        ],
        out_specs=pl.BlockSpec((LANES, total), lambda i: (i, 0)),
        scratch_shapes=[
            pltpu.VMEM(half_block, F32),
            pltpu.VMEM((2, total // 2, LANES), F32),
        ],
    )(near, grown, early, sums, block_counts)
    return result.T


def solution(mesh):
    return jax.shard_map(
        body,
        mesh=mesh,
        in_specs=(
            P("comp", None, "band", None),
            P("band", None),
            P(),
            P(None, "band", None),
            P(None, "band", None),
            P(None, "band", None),
            P("band", None),
            P("band", None),
        ),
        out_specs=P(None, ("comp", "band")),
        check_vma=False,
    )
```

```python
import functools
import math

import jax
import jax.numpy as jnp
import numpy as np
from jax import lax
from jax.experimental import pallas as pl
from jax.experimental.pallas import tpu as pltpu
from jax.sharding import PartitionSpec as P

GROWTH_RATE = 0.05
DAMPING = 1.5
TURNING_SCALE = 0.5

LANES = 128
SUBLANES = 8
UNIT = 9
WORDS = 5
STEP_COUNT = 65500.0
EXPONENT_ZERO = 99
WINDOW = 4
VMEM_BYTES = 16 * 1024 * 1024
LITTLE = (1_000, 1_000)
MUCH = (200_000_000_000, 1_000_000)
FINISH_VMEM = 28 * 1024 * 1024

F32 = jnp.float32
I32 = jnp.int32


def call(kernel, out_shape, cost, vmem=VMEM_BYTES, **options):
    flops, moved = cost
    return pl.pallas_call(
        kernel,
        out_shape=out_shape,
        cost_estimate=pl.CostEstimate(flops=flops, bytes_accessed=moved, transcendentals=0),
        compiler_params=pltpu.CompilerParams(vmem_limit_bytes=vmem),
        **options,
    )


def iota(shape, axis):
    return lax.broadcasted_iota(I32, shape, axis)


def upwind(speed, far_behind, behind, centre, ahead, far_ahead):
    positive = speed > 0
    near = jnp.where(positive, behind, ahead)
    after = jnp.where(positive, ahead, behind)
    far = jnp.where(positive, far_behind, far_ahead)
    return jnp.abs(speed) * (2.0 * after + far + 3.0 * (centre - 2.0 * near))


def signs(part, parts, turns, directions, j):
    sin, cos = None, None
    for h in range(parts):
        angle = 2.0 * math.pi * (h * turns + j) / directions
        if h == 0:
            sin = jnp.full(part.shape, math.sin(angle), F32)
            cos = jnp.full(part.shape, math.cos(angle), F32)
        else:
            sin = jnp.where(part == h, math.sin(angle), sin)
            cos = jnp.where(part == h, math.cos(angle), cos)
    return sin, cos


def power_table(start, sign):
    lane = iota((SUBLANES, LANES), 1)
    table = jnp.full((SUBLANES, LANES), start, F32)
    for bit in range(7):
        factor = 2.0 ** (sign * 2**bit)
        table = jnp.where((lane & (1 << bit)) != 0, table * factor, table)
    return table


def arrange_kernel(x_ref, land_ref, top_ref, bottom_ref, scratch):
    freqs, parts, step, rows, lon = x_ref.shape
    chunks = scratch.shape[1]
    tail = lon - (chunks - 1) * LANES
    filler = jnp.zeros((rows, LANES - tail), F32)
    lane = iota((SUBLANES * rows, LANES), 1)
    for j in range(step):
        for f in range(freqs):
            for h in range(parts):
                place = pl.ds(f * parts + h, rows, stride=SUBLANES)
                for k in range(chunks):
                    if k < chunks - 1:
                        piece = x_ref[f, h, j, :, k * LANES : (k + 1) * LANES].astype(F32)
                    else:
                        piece = x_ref[f, h, j, :, k * LANES : lon].astype(F32)
                        piece = jnp.concatenate([piece, filler], axis=1)
                    scratch[j, k, place, :] = piece
    initial = [None] * step
    for k in range(chunks):
        span = slice(k * LANES, (k + 1) * LANES)
        land = land_ref[:, k * LANES : min((k + 1) * LANES, lon)]
        if k == chunks - 1:
            land = jnp.concatenate([land, jnp.ones((rows, LANES - tail), I32)], axis=1)
        sea = (land == 0).astype(F32)
        sea = jnp.concatenate([jnp.broadcast_to(sea[r : r + 1], (SUBLANES, LANES)) for r in range(rows)], axis=0)
        for j in range(step):
            piece = scratch[j, k] * sea
            if k == 0:
                initial[j] = piece
            if k == chunks - 1:
                wrapped = jnp.where(
                    lane < tail + 2,
                    pltpu.roll(initial[j], tail, axis=1),
                    pltpu.roll(piece, LANES - tail, axis=1),
                )
                piece = jnp.where(lane < tail, piece, wrapped)
            piece = piece.astype(jnp.bfloat16)
            top_ref[j, :, span] = piece[: 2 * SUBLANES]
            bottom_ref[j, :, span] = piece[2 * SUBLANES :]


def index_kernel(land_ref, counts_ref, cells_ref, ranges_ref, flat):
    chunks = flat.shape[0]
    rows, lon = land_ref.shape
    per_row = chunks // rows
    tail = lon - (per_row - 1) * LANES
    flat[...] = jnp.ones(flat.shape, I32)
    for r in range(rows):
        for k in range(per_row):
            size = LANES if k < per_row - 1 else tail
            piece = land_ref[r : r + 1, k * LANES : k * LANES + size]
            flat[r * per_row + k : r * per_row + k + 1, :size] = piece
    groups, _, slots = cells_ref.shape
    spans = slots // LANES
    sea = (flat[...] == 0).astype(jnp.bfloat16)
    square = (LANES, LANES)
    ones_before = (iota(square, 1) <= iota(square, 0)).astype(jnp.bfloat16)
    ranks = lax.dot_general(ones_before, sea, (((1,), (1,)), ((), ())), preferred_element_type=F32)
    totals = jnp.dot(sea, jnp.ones(square, jnp.bfloat16), preferred_element_type=F32)
    chunk_square = (chunks, chunks)
    chunks_before = (iota(chunk_square, 1) <= iota(chunk_square, 0)).astype(jnp.bfloat16)
    through = jnp.dot(chunks_before, totals.astype(jnp.bfloat16), preferred_element_type=F32)
    through_column = through[:, :1]
    total_column = totals[:, :1]
    ranks = ranks.astype(jnp.bfloat16)
    chunk_ids = iota((chunks, slots), 0)
    slot_ids = iota((1, slots), 1)
    span_lane = iota((1, LANES), 1)
    start = jnp.int32(0)
    longest = jnp.zeros((1, 1), F32)
    for c in range(groups):
        count = counts_ref[0, c]
        number = (slot_ids + start).astype(F32)
        passed = (through_column <= number).astype(F32)
        chunk_of = jnp.sum(passed, axis=0, keepdims=True)
        before = jnp.sum(passed * total_column, axis=0, keepdims=True)
        chunk_of = chunk_of.astype(I32)
        chosen = (chunk_ids == chunk_of).astype(jnp.bfloat16)
        inside = jnp.dot(ranks, chosen, preferred_element_type=F32)
        lane = jnp.sum((inside <= number - before).astype(F32), axis=0, keepdims=True)
        valid = slot_ids < count
        found = jnp.where(valid, chunk_of * LANES + lane.astype(I32), -1)
        cells_ref[c] = jnp.broadcast_to(found, (SUBLANES, slots))
        bounds = jnp.zeros((1, LANES), I32)
        final = jnp.zeros((1, 1), F32)
        for m in range(spans):
            span = slice(m * LANES, (m + 1) * LANES)
            own = chunk_of[:, span].astype(F32)
            low = jnp.min(jnp.where(valid[:, span], own, float(chunks)), axis=1, keepdims=True)
            high = jnp.max(jnp.where(valid[:, span], own, -1.0), axis=1, keepdims=True)
            longest = jnp.maximum(longest, high - low + 1.0)
            final = jnp.maximum(final, high)
            bounds = jnp.where(span_lane == m, low.astype(I32), bounds)
            bounds = jnp.where(span_lane == m + spans, high.astype(I32), bounds)
        bounds = jnp.where(span_lane == 2 * spans, final.astype(I32), bounds)
        ranges_ref[c : c + 1, :] = bounds
        start = start + count
    ranges_ref[groups : groups + 1, :] = jnp.broadcast_to(longest.astype(I32), (1, LANES))


def advect_kernel(
    directions, stretch, top_ref, bottom_ref, speed_ref, depth_ref, current_ref, slope_ref, out_ref, coef_ref, scratch
):
    turns, _, padded = top_ref.shape
    rows, lon = depth_ref.shape
    chunks = padded // LANES
    tail = lon - (chunks - 1) * LANES
    total_freqs, depths = speed_ref.shape
    parts = directions // turns
    freqs = SUBLANES // parts
    comp, band = lax.axis_index("comp"), lax.axis_index("band")
    speeds = speed_ref[...]
    freq_ids = iota(speeds.shape, 0)
    table = []
    for f in range(freqs):
        row = jnp.sum(jnp.where(freq_ids == comp * freqs + f, speeds, 0.0), axis=0, keepdims=True)
        table.append(jnp.broadcast_to(row, (parts, depths)))
    table = jnp.concatenate(table, axis=0)
    table = jnp.concatenate([table, jnp.zeros((SUBLANES, LANES - depths), F32)], axis=1) * (1.0 / 6.0)
    shape = (SUBLANES, LANES)
    for r in range(rows):
        place = slice(r * SUBLANES, (r + 1) * SUBLANES)
        widening = jnp.float32(0.0)
        for b in range(len(stretch) // rows):
            widening = jnp.where(band == b, jnp.float32(stretch[b * rows + r]), widening)
        for k in range(chunks):
            span = slice(k * LANES, (k + 1) * LANES)

            def field(row):
                if k == chunks - 1:
                    row = jnp.concatenate([row[:, :tail], jnp.zeros((1, LANES - tail), row.dtype)], axis=1)
                return jnp.broadcast_to(row, shape)

            own = slice(k * LANES, min((k + 1) * LANES, lon))
            classes = field(depth_ref[r : r + 1, own])
            sixth = jnp.take_along_axis(table, classes, axis=1, mode="promise_in_bounds")
            coef_ref[0, place, span] = sixth
            coef_ref[1, place, span] = field(current_ref[1, r : r + 1, own]) * (1.0 / 6.0)
            coef_ref[2, place, span] = sixth * TURNING_SCALE * field(slope_ref[0, r : r + 1, own])
            coef_ref[3, place, span] = sixth * TURNING_SCALE * field(slope_ref[1, r : r + 1, own])
            scratch[0, place, span] = sixth * widening
            scratch[1, place, span] = field(current_ref[0, r : r + 1, own]) * (1.0 / 6.0)

    width = LANES * (4 if chunks % 4 == 0 else 1)

    def window(ref, j, low, high):
        parts = []
        if low < LANES:
            parts.append(ref[j, :, padded - LANES :])
            parts.append(ref[j, :, : min(high + LANES, padded)])
        else:
            parts.append(ref[j, :, low - LANES : min(high + LANES, padded)])
        if high + LANES > padded:
            parts.append(ref[j, :, :LANES])
        return jnp.concatenate([part.astype(F32) for part in parts], axis=1)

    turn_sin, turn_cos = math.sin(2.0 * math.pi / directions), math.cos(2.0 * math.pi / directions)

    def one_turn(j, carry):
        sin, cos = carry
        for low in range(0, padded, width):
            high = low + width
            centres, shifted = [], []
            for ref in (top_ref, bottom_ref):
                wide = window(ref, j, low, high)
                moved = [
                    pltpu.roll(wide, shift % wide.shape[1], axis=1)[:, LANES : LANES + width] for shift in (2, 1, -1, -2)
                ]
                for half in (slice(0, SUBLANES), slice(SUBLANES, 2 * SUBLANES)):
                    centres.append(wide[half, LANES : LANES + width])
                    shifted.append([one[half] for one in moved])
            for r in range(rows):
                place = slice(r * SUBLANES, (r + 1) * SUBLANES)
                span = slice(low, high)
                speed_x = scratch[0, place, span] * cos + scratch[1, place, span]
                speed_y = coef_ref[0, place, span] * sin + coef_ref[1, place, span]
                near = [centres[n] if 0 <= n < rows else 0.0 for n in range(r - 2, r + 3)]
                far_behind, behind, ahead, far_ahead = shifted[r]
                along = upwind(speed_x, far_behind, behind, centres[r], ahead, far_ahead)
                across = upwind(speed_y, *near)
                out_ref[j, place, span] = centres[r] - along - across
        return sin * turn_cos + cos * turn_sin, cos * turn_cos - sin * turn_sin

    part = iota((SUBLANES, 1), 0) % parts
    lax.fori_loop(0, turns, one_turn, signs(part, parts, turns, directions, 0))


def pack_kernel(directions, offsets, adv_ref, above_ref, below_ref, coef_ref, cells_ref, ranges_ref, after_ref, *refs):
    out_refs, (packed, turned_values, trig) = refs[:-3], refs[-3:]
    turns, height, padded = adv_ref.shape
    rows = height // SUBLANES
    chunks = padded // LANES
    parts = directions // turns
    units = turns // UNIT
    shape = (SUBLANES, LANES)
    part = iota(shape, 0) % parts
    scale = power_table(STEP_COUNT * 2.0**EXPONENT_ZERO, -1)
    together = turned_values.shape[0]
    for j in range(turns):
        trig[0, j], trig[1, j] = signs(part, parts, turns, directions, j)

    def turned(value, by):
        if by == 0:
            return value
        if by > 0:
            return jnp.where(
                part == parts - 1, pltpu.roll(value, parts - 1, axis=0), pltpu.roll(value, SUBLANES - 1, axis=0)
            )
        return jnp.where(part == 0, pltpu.roll(value, SUBLANES - parts + 1, axis=0), pltpu.roll(value, 1, axis=0))

    def refract(r, k, into):
        place = slice(r * SUBLANES, (r + 1) * SUBLANES)
        span = pl.ds(pl.multiple_of(k * LANES, LANES), LANES)
        sixth, current_y, turn_x, turn_y = [coef_ref[n, place, span] for n in range(4)]
        advected = []
        for j in range(turns):
            speed = sixth * trig[0, j] + current_y
            positive = speed > 0
            ref = above_ref if r < 2 else below_ref
            outer = ref[j, :, span].astype(F32)
            low, high = outer[:SUBLANES], outer[SUBLANES:]
            if r == 0:
                share = jnp.where(positive, low - 6.0 * high, 2.0 * high)
            elif r == 1:
                share = jnp.where(positive, high, 0.0)
            elif r == rows - 2:
                share = jnp.where(positive, 0.0, low)
            else:
                share = jnp.where(positive, 2.0 * low, high - 6.0 * low)
            advected.append(adv_ref[j, place, span] - jnp.abs(speed) * share)
        around = {j: turned(advected[j % turns], j // turns) for j in range(-2, turns + 2)}
        largest = [None] * units
        for j in range(turns):
            speed = trig[0, j] * turn_x - trig[1, j] * turn_y
            value = around[j] - upwind(speed, *[around[n] for n in range(j - 2, j + 3)])
            turned_values[into, j] = value
            size = jnp.abs(value)
            unit = j // UNIT
            largest[unit] = size if largest[unit] is None else jnp.maximum(largest[unit], size)
        return largest

    def code(chunk, come_from, unit, largest):
        level = jnp.ceil(jnp.log2(jnp.maximum(largest, 2.0**-98)))
        level = jnp.minimum(level, 28.0).astype(I32) + EXPONENT_ZERO
        level = jnp.maximum(level, 1)
        inverse = jnp.take_along_axis(scale, level, axis=1, mode="promise_in_bounds")
        codes = [
            (turned_values[come_from, unit * UNIT + n] * inverse + 65536.5).astype(I32) for n in range(UNIT)
        ]
        first = unit * WORDS
        rest = codes[8] | (level << 17)
        for n in range(4):
            even, odd = codes[2 * n], codes[2 * n + 1]
            packed[chunk, first + n] = even | (odd << 17)
            rest = rest | ((odd >> 15) << (24 + 2 * n))
        packed[chunk, first + 4] = rest

    half = len(offsets)
    _, words, slots = out_refs[0].shape
    words = words // SUBLANES
    spans = slots // LANES
    comp = lax.axis_index("comp")
    base = ((comp ^ offsets[0]) // half) * half
    first_set = ranges_ref[base, 0] // together
    last_set = ranges_ref[base + half - 1, 2 * spans] // together
    sets = chunks // together
    for r in range(rows):

        def some_chunks(i, carry):
            found = [refract(r, i * together + n, n) for n in range(together)]
            for n in range(together):
                for unit in range(units):
                    code(r * chunks + i * together + n, n, unit, found[n][unit])
            return carry

        low = jnp.clip(first_set - r * sets, 0, sets)
        high = jnp.clip(last_set + 1 - r * sets, 0, sets)
        lax.fori_loop(low, high, some_chunks, 0)

    last = rows * chunks - 1

    def merged(cells, chunk, sums):
        lane = cells - chunk * LANES
        here = (lane >= 0) & (lane < LANES)
        lane = lane & (LANES - 1)
        return tuple(
            jnp.where(
                here, jnp.take_along_axis(packed[chunk, n], lane, axis=1, mode="promise_in_bounds"), sums[n]
            )
            for n in range(words)
        )

    if len(out_refs) == half:
        places = [(comp ^ offset, out_ref, 0) for offset, out_ref in zip(offsets, out_refs)]
    else:
        places = [(base + n, out_refs[0], n) for n in range(half)]
    for block, out_ref, at in places:
        for m in range(spans):
            span = slice(m * LANES, (m + 1) * LANES)
            cells = cells_ref[block, :, span]
            low = ranges_ref[block, m]
            sums = tuple(jnp.zeros(shape, I32) for _ in range(words))
            for t in range(WINDOW):
                sums = merged(cells, jnp.minimum(low + t, last), sums)
            for n in range(words):
                out_ref[at, n * SUBLANES : (n + 1) * SUBLANES, span] = sums[n]

    @pl.when(ranges_ref[cells_ref.shape[0], 0] > WINDOW)
    def _():
        for block, out_ref, at in places:
            for m in range(spans):
                span = slice(m * LANES, (m + 1) * LANES)
                cells = cells_ref[block, :, span]
                low, high = ranges_ref[block, m], ranges_ref[block, m + spans]
                sums = tuple(out_ref[at, n * SUBLANES : (n + 1) * SUBLANES, span] for n in range(words))
                sums = lax.fori_loop(
                    low + WINDOW, high + 1, lambda chunk, sums: merged(cells, chunk, sums), sums
                )
                for n in range(words):
                    out_ref[at, n * SUBLANES : (n + 1) * SUBLANES, span] = sums[n]


def grow_kernel(directions, wind_ref, cells_ref, ranges_ref, near_ref, far_ref, flat, slot_wind):
    half, turns, _, slots = near_ref.shape
    groups = 2 * half
    rows, lon = wind_ref.shape[1:]
    chunks = flat.shape[0] // rows
    tail = lon - (chunks - 1) * LANES
    spans = slots // LANES
    parts = directions // turns
    freqs = SUBLANES // parts
    shape = (SUBLANES, LANES)
    part = iota(shape, 0) % parts
    freq = iota(shape, 0) // parts
    comp = lax.axis_index("comp")
    for r in range(rows):
        for k in range(chunks):
            size = LANES if k < chunks - 1 else tail
            for n in range(2):
                flat[r * chunks + k, n : n + 1, :size] = wind_ref[n, r : r + 1, k * LANES : k * LANES + size]
    for m in range(spans):
        span = slice(m * LANES, (m + 1) * LANES)
        cells = cells_ref[comp, :, span]

        def merged(chunk, sums):
            lane = cells - chunk * LANES
            here = (lane >= 0) & (lane < LANES)
            lane = lane & (LANES - 1)
            return jnp.where(
                here, jnp.take_along_axis(flat[chunk], lane, axis=1, mode="promise_in_bounds"), sums
            )

        found = lax.fori_loop(
            ranges_ref[comp, m], ranges_ref[comp, m + spans] + 1, merged, jnp.zeros(shape, F32)
        )
        slot_wind[0, :, span] = jnp.broadcast_to(found[0:1], shape)
        slot_wind[1, :, span] = jnp.broadcast_to(found[1:2], shape)

    rates = []
    for far in range(2):
        step = jnp.where((comp // half) ^ far == 0, jnp.float32(1.0), jnp.float32(1.1 ** (half * freqs)))
        for source in range(half):
            slope, threshold = jnp.zeros(shape, F32), jnp.zeros(shape, F32)
            for f in range(freqs):
                angular, ratio = frequency(source * freqs + f, groups * freqs)
                slope = jnp.where(freq == f, GROWTH_RATE * ratio * angular / 9.81, slope)
                threshold = jnp.where(freq == f, GROWTH_RATE * ratio, threshold)
            rates.append((slope * (step * step), threshold * step))

    def one_span(m, carry):
        span = pl.ds(pl.multiple_of(m * LANES, LANES), LANES)
        east, north = slot_wind[0, :, span], slot_wind[1, :, span]
        for j in range(turns):
            sin, cos = signs(part, parts, turns, directions, j)
            along = east * cos + north * sin
            for source in range(half):
                slope, threshold = rates[source]
                near_ref[source, j, :, span] = jnp.exp(jnp.maximum(along * slope - threshold, 0.0))
                slope, threshold = rates[half + source]
                far_ref[(comp % half) ^ source, j, :, span] = jnp.exp(jnp.maximum(along * slope - threshold, 0.0))
        return carry

    lax.fori_loop(0, spans, one_span, 0)


def decode(arrived_refs, grown_ref, scale, span, store):
    sums = [jnp.zeros((SUBLANES, LANES), F32) for _ in range(2)]
    turns = grown_ref.shape[1]
    for source, (arrived, at) in enumerate(arrived_refs):
        for unit in range(turns // UNIT):
            words = [
                arrived[at, n * SUBLANES : (n + 1) * SUBLANES, span]
                for n in range(unit * WORDS, (unit + 1) * WORDS)
            ]
            rest = words[4]
            level = lax.shift_right_logical(rest, 17) & 127
            size = jnp.take_along_axis(scale, level, axis=1, mode="promise_in_bounds")
            offset = size * 65536.0
            for n in range(UNIT):
                if n == 8:
                    coded = rest & 0x1FFFF
                elif n % 2 == 0:
                    coded = words[n // 2] & 0x1FFFF
                else:
                    coded = lax.shift_right_logical(words[n // 2], 17) | (
                        lax.shift_right_logical(rest, 9 + n - 1) & 0x18000
                    )
                value = coded.astype(F32) * size - offset
                sums[n % 2] = sums[n % 2] + value * value
                j = unit * UNIT + n
                store(source, j, value * grown_ref[source, j, :, span])
    return sums[0] + sums[1]


def early_kernel(half, *refs):
    arrived_refs, (grown_ref, out_ref, sums_ref) = [(ref, 0) for ref in refs[:half]], refs[half:]
    own = lax.axis_index("comp") % half
    scale = power_table(2.0**-EXPONENT_ZERO / STEP_COUNT, 1)
    for low in range(0, out_ref.shape[-1], LANES):
        span = slice(low, low + LANES)

        def store(source, j, value):
            out_ref[own ^ source, j, :, span] = value

        sums_ref[:, span] = decode(arrived_refs, grown_ref, scale, span, store)


def finish_kernel(freqs, half, arrived_ref, grown_ref, early_ref, sums_ref, counts_ref, out_ref, values, ordered):
    arrived_refs = [(arrived_ref, n) for n in range(half)]
    groups = 2 * half
    turns = values.shape[2]
    each = turns * SUBLANES
    shape = (SUBLANES, LANES)
    comp = lax.axis_index("comp")
    side = comp // half
    count = counts_ref[0, comp]
    scale = power_table(2.0**-EXPONENT_ZERO / STEP_COUNT, 1)
    freq = iota(shape, 0) // (SUBLANES // freqs)
    square = (LANES, LANES)
    unit_matrix = (iota(square, 0) == iota(square, 1)).astype(jnp.bfloat16)
    steps = [jnp.where(side ^ far == 0, jnp.float32(1.0), jnp.float32(1.1 ** (half * freqs))) for far in range(2)]
    for m in range(values.shape[0]):
        span = slice(m * LANES, (m + 1) * LANES)

        def store(source, j, value):
            values[m, source, j] = value

        sums = decode(arrived_refs, grown_ref, scale, span, store)
        mean_sq = jnp.sum(sums + sums_ref[:, span], axis=0, keepdims=True) / float(groups * each)
        strength = jnp.broadcast_to(jnp.sqrt(mean_sq + 1e-06), shape)
        occupied = (m * LANES + iota(shape, 1)) < count
        for far in range(2):
            for source in range(half):
                rate = jnp.zeros(shape, F32)
                for f in range(freqs):
                    rate = jnp.where(freq == f, DAMPING * frequency(source * freqs + f, groups * freqs)[1], rate)
                factor = jnp.exp(-(rate * steps[far] * strength))
                for j in range(turns):
                    value = early_ref[source, j, :, span] if far else values[m, source, j]
                    value = jnp.where(occupied, value * factor, 0.0)
                    ordered[m, side ^ far, pl.ds(source * each + j, SUBLANES, stride=turns), :] = value
        slots = slice(m * LANES, min((m + 1) * LANES, out_ref.shape[0]))
        for place in range(2):
            turned = lax.dot_general(
                unit_matrix,
                ordered[m, place].astype(jnp.bfloat16),
                (((1,), (1,)), ((), ())),
                preferred_element_type=F32,
            )
            out_ref[slots, place * half * each : (place + 1) * half * each] = turned[
                : slots.stop - slots.start
            ].astype(jnp.bfloat16)


def frequency(index, count):
    angular = 2.0 * math.pi * 0.0418 * 1.1**index
    return angular, 1.1 ** (index - (count - 1))


def body(spectra, depth_class, group_speed, current, depth_slope, wind, land_mask, block_counts):
    freqs, directions, rows, lon = spectra.shape
    total_freqs = group_speed.shape[1]
    groups = lax.axis_size("comp")
    bands = lax.axis_size("band")
    slot_count = rows * lon * 7 // (8 * groups)
    slots = -(-slot_count // LANES) * LANES
    parts = SUBLANES // freqs
    turns = directions // parts
    units = turns // UNIT
    chunks = -(-lon // LANES)
    padded = chunks * LANES
    height = rows * SUBLANES
    words = units * WORDS
    hbm = 2 * turns * height * padded
    latitude = (-60.0 + 120.0 * (np.arange(rows * bands) + 0.5) / (rows * bands)) * (math.pi / 180.0)
    stretch = [float(value) for value in 1.0 / np.cos(latitude)]
    smem = pl.BlockSpec(memory_space=pltpu.SMEM)
    vmem = pl.BlockSpec(memory_space=pltpu.VMEM)

    step = 3
    half = jax.ShapeDtypeStruct((turns, height // 2, padded), jnp.bfloat16)
    half_spec = pl.BlockSpec((step, height // 2, padded), lambda i: (i, 0, 0))
    top, bottom = call(
        arrange_kernel,
        [half, half],
        (4 * hbm, 2 * hbm),
        grid=(turns // step,),
        in_specs=[
            pl.BlockSpec((freqs, parts, step, rows, lon), lambda i: (0, 0, i, 0, 0)),
            pl.BlockSpec((rows, lon), lambda i: (0, 0)),
        ],
        out_specs=[half_spec, half_spec],
        scratch_shapes=[pltpu.VMEM((step, chunks, height, LANES), F32)],
    )(spectra.reshape(freqs, parts, turns, rows, lon), land_mask)
    down = [(i, i + 1) for i in range(bands - 1)]
    above = lax.ppermute(bottom, "band", down)
    below = lax.ppermute(top, "band", [(j, i) for i, j in down])

    range_rows = 2 * SUBLANES if groups < 2 * SUBLANES else 3 * SUBLANES
    cells, ranges = call(
        index_kernel,
        [
            jax.ShapeDtypeStruct((groups, SUBLANES, slots), I32),
            jax.ShapeDtypeStruct((range_rows, LANES), I32),
        ],
        (100 * groups * slots, 8 * groups * slots),
        in_specs=[vmem, smem],
        out_specs=[vmem, vmem],
        scratch_shapes=[pltpu.VMEM((rows * chunks, LANES), I32)],
    )(land_mask, block_counts)

    advected, coefs = call(
        functools.partial(advect_kernel, directions, stretch),
        [
            jax.ShapeDtypeStruct((turns, height, padded), F32),
            jax.ShapeDtypeStruct((4, height, padded), F32),
        ],
        (50 * hbm, 4 * hbm),
        in_specs=[vmem] * 6,
        out_specs=[vmem, vmem],
        scratch_shapes=[pltpu.VMEM((2, height, padded), F32)],
    )(top, bottom, group_speed.T, depth_class, current, depth_slope)

    half = groups // 2
    block = (words * SUBLANES, slots)
    after, shipped = ranges, []
    for offsets, outputs in ((range(half, groups), [(1,) + block] * half), (range(half), [(half,) + block])):
        shipped.append(
            call(
                functools.partial(pack_kernel, directions, tuple(offsets)),
                [jax.ShapeDtypeStruct(shape, I32) for shape in outputs],
                (25 * hbm, 3 * hbm) if len(outputs) > 1 else LITTLE,
                in_specs=[vmem] * 5 + [smem, pl.BlockSpec(memory_space=pl.ANY)],
                out_specs=[vmem] * len(outputs),
                scratch_shapes=[
                    pltpu.VMEM((rows * chunks, words, SUBLANES, LANES), I32),
                    pltpu.VMEM((6 if chunks % 6 == 0 else 1, turns, SUBLANES, LANES), F32),
                    pltpu.VMEM((2, turns, SUBLANES, LANES), F32),
                ],
            )(advected, above, below, coefs, cells, ranges, after)
        )
        after = shipped[0][0]
    far = [
        lax.ppermute(part, "comp", [(i, i ^ (half + n)) for i in range(groups)]) for n, part in enumerate(shipped[0])
    ]
    halves = [list(range(half)), list(range(half, groups))]
    near = lax.all_to_all(shipped[1][0], "comp", split_axis=0, concat_axis=0, axis_index_groups=halves, tiled=True)

    total = total_freqs * directions
    values = jax.ShapeDtypeStruct((half, turns, SUBLANES, slots), F32)
    grown_near, grown_far = call(
        functools.partial(grow_kernel, directions),
        [values, values],
        LITTLE,
        in_specs=[vmem, vmem, smem],
        out_specs=[vmem, vmem],
        scratch_shapes=[
            pltpu.VMEM((rows * chunks, SUBLANES, LANES), F32),
            pltpu.VMEM((2, SUBLANES, slots), F32),
        ],
    )(wind, cells, ranges)

    early, sums = call(
        functools.partial(early_kernel, half),
        [values, jax.ShapeDtypeStruct((SUBLANES, slots), F32)],
        MUCH,
        in_specs=[vmem] * (half + 1),
        out_specs=[vmem, vmem],
    )(*far, grown_far)

    result = call(
        functools.partial(finish_kernel, freqs, half),
        jax.ShapeDtypeStruct((slot_count, total), jnp.bfloat16),
        (50 * total * slots, 6 * total * slots),
        vmem=FINISH_VMEM,
        in_specs=[vmem] * 4 + [smem],
        out_specs=vmem,
        scratch_shapes=[
            pltpu.VMEM((slots // LANES, half, turns, SUBLANES, LANES), F32),
            pltpu.VMEM((slots // LANES, 2, total // 2, LANES), F32),
        ],
    )(near, grown_near, early, sums, block_counts)
    return result.T


def solution(mesh):
    return jax.shard_map(
        body,
        mesh=mesh,
        in_specs=(
            P("comp", None, "band", None),
            P("band", None),
            P(),
            P(None, "band", None),
            P(None, "band", None),
            P(None, "band", None),
            P("band", None),
            P("band", None),
        ),
        out_specs=P(None, ("comp", "band")),
        check_vma=False,
    )
```

```python
import functools
import math

import jax
import jax.numpy as jnp
import numpy as np
from jax import lax
from jax.experimental import pallas as pl
from jax.experimental.pallas import tpu as pltpu
from jax.sharding import PartitionSpec as P

GROWTH_RATE = 0.05
DAMPING = 1.5
TURNING_SCALE = 0.5

LANES = 128
SUBLANES = 8
UNIT = 9
WORDS = 5
STEP_COUNT = 65500.0
EXPONENT_ZERO = 99
WINDOW = 4
VMEM_BYTES = 16 * 1024 * 1024
LITTLE = (1_000, 1_000)
MUCH = (200_000_000_000, 1_000_000)
FINISH_VMEM = 28 * 1024 * 1024

F32 = jnp.float32
I32 = jnp.int32


def call(kernel, out_shape, cost, vmem=VMEM_BYTES, **options):
    flops, moved = cost
    return pl.pallas_call(
        kernel,
        out_shape=out_shape,
        cost_estimate=pl.CostEstimate(flops=flops, bytes_accessed=moved, transcendentals=0),
        compiler_params=pltpu.CompilerParams(vmem_limit_bytes=vmem),
        **options,
    )


def iota(shape, axis):
    return lax.broadcasted_iota(I32, shape, axis)


def upwind(speed, far_behind, behind, centre, ahead, far_ahead):
    positive = speed > 0
    near = jnp.where(positive, behind, ahead)
    after = jnp.where(positive, ahead, behind)
    far = jnp.where(positive, far_behind, far_ahead)
    return jnp.abs(speed) * (2.0 * after + far + 3.0 * (centre - 2.0 * near))


def signs(part, parts, turns, directions, j):
    sin, cos = None, None
    for h in range(parts):
        angle = 2.0 * math.pi * (h * turns + j) / directions
        if h == 0:
            sin = jnp.full(part.shape, math.sin(angle), F32)
            cos = jnp.full(part.shape, math.cos(angle), F32)
        else:
            sin = jnp.where(part == h, math.sin(angle), sin)
            cos = jnp.where(part == h, math.cos(angle), cos)
    return sin, cos


def power_table(start, sign):
    lane = iota((SUBLANES, LANES), 1)
    table = jnp.full((SUBLANES, LANES), start, F32)
    for bit in range(7):
        factor = 2.0 ** (sign * 2**bit)
        table = jnp.where((lane & (1 << bit)) != 0, table * factor, table)
    return table


def arrange_kernel(x_ref, land_ref, after_ref, top_ref, bottom_ref, scratch):
    freqs, parts, step, rows, lon = x_ref.shape
    chunks = scratch.shape[1]
    tail = lon - (chunks - 1) * LANES
    filler = jnp.zeros((rows, LANES - tail), F32)
    lane = iota((SUBLANES * rows, LANES), 1)
    for j in range(step):
        for f in range(freqs):
            for h in range(parts):
                place = pl.ds(f * parts + h, rows, stride=SUBLANES)
                for k in range(chunks):
                    if k < chunks - 1:
                        piece = x_ref[f, h, j, :, k * LANES : (k + 1) * LANES].astype(F32)
                    else:
                        piece = x_ref[f, h, j, :, k * LANES : lon].astype(F32)
                        piece = jnp.concatenate([piece, filler], axis=1)
                    scratch[j, k, place, :] = piece
    initial = [None] * step
    for k in range(chunks):
        span = slice(k * LANES, (k + 1) * LANES)
        land = land_ref[:, k * LANES : min((k + 1) * LANES, lon)]
        if k == chunks - 1:
            land = jnp.concatenate([land, jnp.ones((rows, LANES - tail), I32)], axis=1)
        sea = (land == 0).astype(F32)
        sea = jnp.concatenate([jnp.broadcast_to(sea[r : r + 1], (SUBLANES, LANES)) for r in range(rows)], axis=0)
        for j in range(step):
            piece = scratch[j, k] * sea
            if k == 0:
                initial[j] = piece
            if k == chunks - 1:
                wrapped = jnp.where(
                    lane < tail + 2,
                    pltpu.roll(initial[j], tail, axis=1),
                    pltpu.roll(piece, LANES - tail, axis=1),
                )
                piece = jnp.where(lane < tail, piece, wrapped)
            piece = piece.astype(jnp.bfloat16)
            top_ref[j, :, span] = piece[: 2 * SUBLANES]
            bottom_ref[j, :, span] = piece[2 * SUBLANES :]


def index_kernel(land_ref, counts_ref, cells_ref, ranges_ref, flat):
    chunks = flat.shape[0]
    rows, lon = land_ref.shape
    per_row = chunks // rows
    tail = lon - (per_row - 1) * LANES
    flat[...] = jnp.ones(flat.shape, I32)
    for r in range(rows):
        for k in range(per_row):
            size = LANES if k < per_row - 1 else tail
            piece = land_ref[r : r + 1, k * LANES : k * LANES + size]
            flat[r * per_row + k : r * per_row + k + 1, :size] = piece
    groups, _, slots = cells_ref.shape
    spans = slots // LANES
    sea = (flat[...] == 0).astype(jnp.bfloat16)
    square = (LANES, LANES)
    ones_before = (iota(square, 1) <= iota(square, 0)).astype(jnp.bfloat16)
    ranks = lax.dot_general(ones_before, sea, (((1,), (1,)), ((), ())), preferred_element_type=F32)
    totals = jnp.dot(sea, jnp.ones(square, jnp.bfloat16), preferred_element_type=F32)
    chunk_square = (chunks, chunks)
    chunks_before = (iota(chunk_square, 1) <= iota(chunk_square, 0)).astype(jnp.bfloat16)
    through = jnp.dot(chunks_before, totals.astype(jnp.bfloat16), preferred_element_type=F32)
    through_column = through[:, :1]
    total_column = totals[:, :1]
    ranks = ranks.astype(jnp.bfloat16)
    chunk_ids = iota((chunks, slots), 0)
    slot_ids = iota((1, slots), 1)
    span_lane = iota((1, LANES), 1)
    start = jnp.int32(0)
    longest = jnp.zeros((1, 1), F32)
    for c in range(groups):
        count = counts_ref[0, c]
        number = (slot_ids + start).astype(F32)
        passed = (through_column <= number).astype(F32)
        chunk_of = jnp.sum(passed, axis=0, keepdims=True)
        before = jnp.sum(passed * total_column, axis=0, keepdims=True)
        chunk_of = chunk_of.astype(I32)
        chosen = (chunk_ids == chunk_of).astype(jnp.bfloat16)
        inside = jnp.dot(ranks, chosen, preferred_element_type=F32)
        lane = jnp.sum((inside <= number - before).astype(F32), axis=0, keepdims=True)
        valid = slot_ids < count
        found = jnp.where(valid, chunk_of * LANES + lane.astype(I32), -1)
        cells_ref[c] = jnp.broadcast_to(found, (SUBLANES, slots))
        bounds = jnp.zeros((1, LANES), I32)
        final = jnp.zeros((1, 1), F32)
        for m in range(spans):
            span = slice(m * LANES, (m + 1) * LANES)
            own = chunk_of[:, span].astype(F32)
            low = jnp.min(jnp.where(valid[:, span], own, float(chunks)), axis=1, keepdims=True)
            high = jnp.max(jnp.where(valid[:, span], own, -1.0), axis=1, keepdims=True)
            longest = jnp.maximum(longest, high - low + 1.0)
            final = jnp.maximum(final, high)
            bounds = jnp.where(span_lane == m, low.astype(I32), bounds)
            bounds = jnp.where(span_lane == m + spans, high.astype(I32), bounds)
        bounds = jnp.where(span_lane == 2 * spans, final.astype(I32), bounds)
        ranges_ref[c : c + 1, :] = bounds
        start = start + count
    ranges_ref[groups : groups + 1, :] = jnp.broadcast_to(longest.astype(I32), (1, LANES))


def advect_kernel(
    directions, stretch, top_ref, bottom_ref, speed_ref, depth_ref, current_ref, slope_ref, out_ref, coef_ref, scratch
):
    turns, _, padded = top_ref.shape
    rows, lon = depth_ref.shape
    chunks = padded // LANES
    tail = lon - (chunks - 1) * LANES
    total_freqs, depths = speed_ref.shape
    parts = directions // turns
    freqs = SUBLANES // parts
    comp, band = lax.axis_index("comp"), lax.axis_index("band")
    speeds = speed_ref[...]
    freq_ids = iota(speeds.shape, 0)
    table = []
    for f in range(freqs):
        row = jnp.sum(jnp.where(freq_ids == comp * freqs + f, speeds, 0.0), axis=0, keepdims=True)
        table.append(jnp.broadcast_to(row, (parts, depths)))
    table = jnp.concatenate(table, axis=0)
    table = jnp.concatenate([table, jnp.zeros((SUBLANES, LANES - depths), F32)], axis=1) * (1.0 / 6.0)
    shape = (SUBLANES, LANES)
    for r in range(rows):
        place = slice(r * SUBLANES, (r + 1) * SUBLANES)
        widening = jnp.float32(0.0)
        for b in range(len(stretch) // rows):
            widening = jnp.where(band == b, jnp.float32(stretch[b * rows + r]), widening)
        for k in range(chunks):
            span = slice(k * LANES, (k + 1) * LANES)

            def field(row):
                if k == chunks - 1:
                    row = jnp.concatenate([row[:, :tail], jnp.zeros((1, LANES - tail), row.dtype)], axis=1)
                return jnp.broadcast_to(row, shape)

            own = slice(k * LANES, min((k + 1) * LANES, lon))
            classes = field(depth_ref[r : r + 1, own])
            sixth = jnp.take_along_axis(table, classes, axis=1, mode="promise_in_bounds")
            coef_ref[0, place, span] = sixth
            coef_ref[1, place, span] = field(current_ref[1, r : r + 1, own]) * (1.0 / 6.0)
            coef_ref[2, place, span] = sixth * TURNING_SCALE * field(slope_ref[0, r : r + 1, own])
            coef_ref[3, place, span] = sixth * TURNING_SCALE * field(slope_ref[1, r : r + 1, own])
            scratch[0, place, span] = sixth * widening
            scratch[1, place, span] = field(current_ref[0, r : r + 1, own]) * (1.0 / 6.0)

    width = LANES * (4 if chunks % 4 == 0 else 1)

    def window(ref, j, low, high):
        parts = []
        if low < LANES:
            parts.append(ref[j, :, padded - LANES :])
            parts.append(ref[j, :, : min(high + LANES, padded)])
        else:
            parts.append(ref[j, :, low - LANES : min(high + LANES, padded)])
        if high + LANES > padded:
            parts.append(ref[j, :, :LANES])
        return jnp.concatenate([part.astype(F32) for part in parts], axis=1)

    turn_sin, turn_cos = math.sin(2.0 * math.pi / directions), math.cos(2.0 * math.pi / directions)

    def one_turn(j, carry):
        sin, cos = carry
        for low in range(0, padded, width):
            high = low + width
            centres, shifted = [], []
            for ref in (top_ref, bottom_ref):
                wide = window(ref, j, low, high)
                moved = [
                    pltpu.roll(wide, shift % wide.shape[1], axis=1)[:, LANES : LANES + width] for shift in (2, 1, -1, -2)
                ]
                for half in (slice(0, SUBLANES), slice(SUBLANES, 2 * SUBLANES)):
                    centres.append(wide[half, LANES : LANES + width])
                    shifted.append([one[half] for one in moved])
            for r in range(rows):
                place = slice(r * SUBLANES, (r + 1) * SUBLANES)
                span = slice(low, high)
                speed_x = scratch[0, place, span] * cos + scratch[1, place, span]
                speed_y = coef_ref[0, place, span] * sin + coef_ref[1, place, span]
                near = [centres[n] if 0 <= n < rows else 0.0 for n in range(r - 2, r + 3)]
                far_behind, behind, ahead, far_ahead = shifted[r]
                along = upwind(speed_x, far_behind, behind, centres[r], ahead, far_ahead)
                across = upwind(speed_y, *near)
                out_ref[j, place, span] = centres[r] - along - across
        return sin * turn_cos + cos * turn_sin, cos * turn_cos - sin * turn_sin

    part = iota((SUBLANES, 1), 0) % parts
    lax.fori_loop(0, turns, one_turn, signs(part, parts, turns, directions, 0))


def pack_kernel(directions, offsets, adv_ref, above_ref, below_ref, coef_ref, cells_ref, ranges_ref, after_ref, *refs):
    out_refs, (packed, turned_values, trig) = refs[:-3], refs[-3:]
    turns, height, padded = adv_ref.shape
    rows = height // SUBLANES
    chunks = padded // LANES
    parts = directions // turns
    units = turns // UNIT
    shape = (SUBLANES, LANES)
    part = iota(shape, 0) % parts
    scale = power_table(STEP_COUNT * 2.0**EXPONENT_ZERO, -1)
    together = turned_values.shape[0]
    for j in range(turns):
        trig[0, j], trig[1, j] = signs(part, parts, turns, directions, j)

    def turned(value, by):
        if by == 0:
            return value
        if by > 0:
            return jnp.where(
                part == parts - 1, pltpu.roll(value, parts - 1, axis=0), pltpu.roll(value, SUBLANES - 1, axis=0)
            )
        return jnp.where(part == 0, pltpu.roll(value, SUBLANES - parts + 1, axis=0), pltpu.roll(value, 1, axis=0))

    def refract(r, k, into):
        place = slice(r * SUBLANES, (r + 1) * SUBLANES)
        span = pl.ds(pl.multiple_of(k * LANES, LANES), LANES)
        sixth, current_y, turn_x, turn_y = [coef_ref[n, place, span] for n in range(4)]
        advected = []
        for j in range(turns):
            speed = sixth * trig[0, j] + current_y
            positive = speed > 0
            ref = above_ref if r < 2 else below_ref
            outer = ref[j, :, span].astype(F32)
            low, high = outer[:SUBLANES], outer[SUBLANES:]
            if r == 0:
                share = jnp.where(positive, low - 6.0 * high, 2.0 * high)
            elif r == 1:
                share = jnp.where(positive, high, 0.0)
            elif r == rows - 2:
                share = jnp.where(positive, 0.0, low)
            else:
                share = jnp.where(positive, 2.0 * low, high - 6.0 * low)
            advected.append(adv_ref[j, place, span] - jnp.abs(speed) * share)
        around = {j: turned(advected[j % turns], j // turns) for j in range(-2, turns + 2)}
        largest = [None] * units
        for j in range(turns):
            speed = trig[0, j] * turn_x - trig[1, j] * turn_y
            value = around[j] - upwind(speed, *[around[n] for n in range(j - 2, j + 3)])
            turned_values[into, j] = value
            size = jnp.abs(value)
            unit = j // UNIT
            largest[unit] = size if largest[unit] is None else jnp.maximum(largest[unit], size)
        return largest

    def code(chunk, come_from, unit, largest):
        level = jnp.ceil(jnp.log2(jnp.maximum(largest, 2.0**-98)))
        level = jnp.minimum(level, 28.0).astype(I32) + EXPONENT_ZERO
        level = jnp.maximum(level, 1)
        inverse = jnp.take_along_axis(scale, level, axis=1, mode="promise_in_bounds")
        codes = [
            (turned_values[come_from, unit * UNIT + n] * inverse + 65536.5).astype(I32) for n in range(UNIT)
        ]
        first = unit * WORDS
        rest = codes[8] | (level << 17)
        for n in range(4):
            even, odd = codes[2 * n], codes[2 * n + 1]
            packed[chunk, first + n] = even | (odd << 17)
            rest = rest | ((odd >> 15) << (24 + 2 * n))
        packed[chunk, first + 4] = rest

    half = len(offsets)
    _, words, slots = out_refs[0].shape
    words = words // SUBLANES
    spans = slots // LANES
    comp = lax.axis_index("comp")
    base = ((comp ^ offsets[0]) // half) * half
    first_set = ranges_ref[base, 0] // together
    last_set = ranges_ref[base + half - 1, 2 * spans] // together
    sets = chunks // together
    for r in range(rows):

        def some_chunks(i, carry):
            found = [refract(r, i * together + n, n) for n in range(together)]
            for n in range(together):
                for unit in range(units):
                    code(r * chunks + i * together + n, n, unit, found[n][unit])
            return carry

        low = jnp.clip(first_set - r * sets, 0, sets)
        high = jnp.clip(last_set + 1 - r * sets, 0, sets)
        lax.fori_loop(low, high, some_chunks, 0)

    last = rows * chunks - 1

    def merged(cells, chunk, sums):
        lane = cells - chunk * LANES
        here = (lane >= 0) & (lane < LANES)
        lane = lane & (LANES - 1)
        return tuple(
            jnp.where(
                here, jnp.take_along_axis(packed[chunk, n], lane, axis=1, mode="promise_in_bounds"), sums[n]
            )
            for n in range(words)
        )

    if len(out_refs) == half:
        places = [(comp ^ offset, out_ref, 0) for offset, out_ref in zip(offsets, out_refs)]
    else:
        places = [(base + n, out_refs[0], n) for n in range(half)]
    for block, out_ref, at in places:
        for m in range(spans):
            span = slice(m * LANES, (m + 1) * LANES)
            cells = cells_ref[block, :, span]
            low = ranges_ref[block, m]
            sums = tuple(jnp.zeros(shape, I32) for _ in range(words))
            for t in range(WINDOW):
                sums = merged(cells, jnp.minimum(low + t, last), sums)
            for n in range(words):
                out_ref[at, n * SUBLANES : (n + 1) * SUBLANES, span] = sums[n]

    @pl.when(ranges_ref[cells_ref.shape[0], 0] > WINDOW)
    def _():
        for block, out_ref, at in places:
            for m in range(spans):
                span = slice(m * LANES, (m + 1) * LANES)
                cells = cells_ref[block, :, span]
                low, high = ranges_ref[block, m], ranges_ref[block, m + spans]
                sums = tuple(out_ref[at, n * SUBLANES : (n + 1) * SUBLANES, span] for n in range(words))
                sums = lax.fori_loop(
                    low + WINDOW, high + 1, lambda chunk, sums: merged(cells, chunk, sums), sums
                )
                for n in range(words):
                    out_ref[at, n * SUBLANES : (n + 1) * SUBLANES, span] = sums[n]


def growth_rates(half, freqs, side):
    shape = (SUBLANES, LANES)
    freq = iota(shape, 0) // (SUBLANES // freqs)
    step = jnp.where(side == 0, jnp.float32(1.0), jnp.float32(1.1 ** (half * freqs)))
    rates = []
    for source in range(half):
        slope, threshold = jnp.zeros(shape, F32), jnp.zeros(shape, F32)
        for f in range(freqs):
            angular, ratio = frequency(source * freqs + f, 2 * half * freqs)
            slope = jnp.where(freq == f, GROWTH_RATE * ratio * angular / 9.81, slope)
            threshold = jnp.where(freq == f, GROWTH_RATE * ratio, threshold)
        rates.append((slope * (step * step), threshold * step))
    return rates


def grow_kernel(directions, wind_ref, cells_ref, ranges_ref, near_ref, slot_wind, flat):
    half, turns, _, slots = near_ref.shape
    rows, lon = wind_ref.shape[1:]
    chunks = flat.shape[0] // rows
    tail = lon - (chunks - 1) * LANES
    spans = slots // LANES
    parts = directions // turns
    freqs = SUBLANES // parts
    shape = (SUBLANES, LANES)
    part = iota(shape, 0) % parts
    comp = lax.axis_index("comp")
    for r in range(rows):
        for k in range(chunks):
            size = LANES if k < chunks - 1 else tail
            for n in range(2):
                flat[r * chunks + k, n : n + 1, :size] = wind_ref[n, r : r + 1, k * LANES : k * LANES + size]
    for m in range(spans):
        span = slice(m * LANES, (m + 1) * LANES)
        cells = cells_ref[comp, :, span]

        def merged(chunk, sums):
            lane = cells - chunk * LANES
            here = (lane >= 0) & (lane < LANES)
            lane = lane & (LANES - 1)
            return jnp.where(
                here, jnp.take_along_axis(flat[chunk], lane, axis=1, mode="promise_in_bounds"), sums
            )

        found = lax.fori_loop(
            ranges_ref[comp, m], ranges_ref[comp, m + spans] + 1, merged, jnp.zeros(shape, F32)
        )
        slot_wind[0, :, span] = jnp.broadcast_to(found[0:1], shape)
        slot_wind[1, :, span] = jnp.broadcast_to(found[1:2], shape)

    rates = growth_rates(half, freqs, comp // half)

    def one_span(m, carry):
        span = pl.ds(pl.multiple_of(m * LANES, LANES), LANES)
        east, north = slot_wind[0, :, span], slot_wind[1, :, span]
        for j in range(turns):
            sin, cos = signs(part, parts, turns, directions, j)
            along = east * cos + north * sin
            for source in range(half):
                slope, threshold = rates[source]
                near_ref[source, j, :, span] = jnp.exp(jnp.maximum(along * slope - threshold, 0.0))
        return carry

    lax.fori_loop(0, spans, one_span, 0)


def decode(arrived_refs, turns, scale, span, store):
    sums = [jnp.zeros((SUBLANES, LANES), F32) for _ in range(2)]
    for source, (arrived, at) in enumerate(arrived_refs):
        for unit in range(turns // UNIT):
            words = [
                arrived[(*at, slice(n * SUBLANES, (n + 1) * SUBLANES), span)]
                for n in range(unit * WORDS, (unit + 1) * WORDS)
            ]
            rest = words[4]
            level = lax.shift_right_logical(rest, 17) & 127
            size = jnp.take_along_axis(scale, level, axis=1, mode="promise_in_bounds")
            offset = size * 65536.0
            for n in range(UNIT):
                if n == 8:
                    coded = rest & 0x1FFFF
                elif n % 2 == 0:
                    coded = words[n // 2] & 0x1FFFF
                else:
                    coded = lax.shift_right_logical(words[n // 2], 17) | (
                        lax.shift_right_logical(rest, 9 + n - 1) & 0x18000
                    )
                value = coded.astype(F32) * size - offset
                sums[n % 2] = sums[n % 2] + value * value
                j = unit * UNIT + n
                store(source, j, value)
    return sums[0] + sums[1]


def early_kernel(directions, half, *refs):
    far_refs, (wind_ref, out_ref, sums_ref, buffer, arrivals) = refs[:half], refs[half:]
    copies = [pltpu.make_async_copy(ref, buffer.at[n], arrivals.at[n]) for n, ref in enumerate(far_refs)]
    for copy in copies:
        copy.start()
    _, turns, _, slots = out_ref.shape
    parts = directions // turns
    part = iota((SUBLANES, LANES), 0) % parts
    comp = lax.axis_index("comp")
    own = comp % half
    rates = growth_rates(half, SUBLANES // parts, (comp // half) ^ 1)
    scale = power_table(2.0**-EXPONENT_ZERO / STEP_COUNT, 1)
    spans = [slice(low, low + LANES) for low in range(0, slots, LANES)]
    for span in spans:
        east, north = wind_ref[0, :, span], wind_ref[1, :, span]
        for j in range(turns):
            sin, cos = signs(part, parts, turns, directions, j)
            along = east * cos + north * sin
            for source in range(half):
                slope, threshold = rates[source]
                out_ref[source, j, :, span] = jnp.exp(jnp.maximum(along * slope - threshold, 0.0))
    for copy in copies:
        copy.wait()
    for span in spans:

        def store(source, j, value):
            out_ref[own ^ source, j, :, span] = value * out_ref[own ^ source, j, :, span]

        sums_ref[:, span] = decode([(buffer, (n, 0)) for n in range(half)], turns, scale, span, store)


def finish_kernel(freqs, half, arrived_ref, grown_ref, early_ref, sums_ref, counts_ref, out_ref, values, ordered):
    arrived_refs = [(arrived_ref, (n,)) for n in range(half)]
    groups = 2 * half
    turns = values.shape[2]
    each = turns * SUBLANES
    shape = (SUBLANES, LANES)
    comp = lax.axis_index("comp")
    side = comp // half
    count = counts_ref[0, comp]
    scale = power_table(2.0**-EXPONENT_ZERO / STEP_COUNT, 1)
    freq = iota(shape, 0) // (SUBLANES // freqs)
    square = (LANES, LANES)
    unit_matrix = (iota(square, 0) == iota(square, 1)).astype(jnp.bfloat16)
    steps = [jnp.where(side ^ far == 0, jnp.float32(1.0), jnp.float32(1.1 ** (half * freqs))) for far in range(2)]
    for m in range(values.shape[0]):
        span = slice(m * LANES, (m + 1) * LANES)

        def store(source, j, value):
            values[m, source, j] = value * grown_ref[source, j, :, span]

        sums = decode(arrived_refs, turns, scale, span, store)
        mean_sq = jnp.sum(sums + sums_ref[:, span], axis=0, keepdims=True) / float(groups * each)
        strength = jnp.broadcast_to(jnp.sqrt(mean_sq + 1e-06), shape)
        occupied = (m * LANES + iota(shape, 1)) < count
        for far in range(2):
            for source in range(half):
                rate = jnp.zeros(shape, F32)
                for f in range(freqs):
                    rate = jnp.where(freq == f, DAMPING * frequency(source * freqs + f, groups * freqs)[1], rate)
                factor = jnp.exp(-(rate * steps[far] * strength))
                for j in range(turns):
                    value = early_ref[source, j, :, span] if far else values[m, source, j]
                    value = jnp.where(occupied, value * factor, 0.0)
                    ordered[m, side ^ far, pl.ds(source * each + j, SUBLANES, stride=turns), :] = value
        slots = slice(m * LANES, min((m + 1) * LANES, out_ref.shape[0]))
        for place in range(2):
            if place == 0:
                turned = lax.dot_general(
                    unit_matrix,
                    ordered[m, place].astype(jnp.bfloat16),
                    (((1,), (1,)), ((), ())),
                    preferred_element_type=F32,
                )
            else:
                turned = ordered[m, place].T
            out_ref[slots, place * half * each : (place + 1) * half * each] = turned[
                : slots.stop - slots.start
            ].astype(jnp.bfloat16)


def frequency(index, count):
    angular = 2.0 * math.pi * 0.0418 * 1.1**index
    return angular, 1.1 ** (index - (count - 1))


def body(spectra, depth_class, group_speed, current, depth_slope, wind, land_mask, block_counts):
    freqs, directions, rows, lon = spectra.shape
    total_freqs = group_speed.shape[1]
    groups = lax.axis_size("comp")
    bands = lax.axis_size("band")
    slot_count = rows * lon * 7 // (8 * groups)
    slots = -(-slot_count // LANES) * LANES
    parts = SUBLANES // freqs
    turns = directions // parts
    units = turns // UNIT
    chunks = -(-lon // LANES)
    padded = chunks * LANES
    height = rows * SUBLANES
    words = units * WORDS
    hbm = 2 * turns * height * padded
    latitude = (-60.0 + 120.0 * (np.arange(rows * bands) + 0.5) / (rows * bands)) * (math.pi / 180.0)
    stretch = [float(value) for value in 1.0 / np.cos(latitude)]
    smem = pl.BlockSpec(memory_space=pltpu.SMEM)
    vmem = pl.BlockSpec(memory_space=pltpu.VMEM)

    range_rows = 2 * SUBLANES if groups < 2 * SUBLANES else 3 * SUBLANES
    cells, ranges = call(
        index_kernel,
        [
            jax.ShapeDtypeStruct((groups, SUBLANES, slots), I32),
            jax.ShapeDtypeStruct((range_rows, LANES), I32),
        ],
        (100 * groups * slots, 8 * groups * slots),
        in_specs=[vmem, smem],
        out_specs=[vmem, vmem],
        scratch_shapes=[pltpu.VMEM((rows * chunks, LANES), I32)],
    )(land_mask, block_counts)

    step = 3
    half = jax.ShapeDtypeStruct((turns, height // 2, padded), jnp.bfloat16)
    half_spec = pl.BlockSpec((step, height // 2, padded), lambda i: (i, 0, 0))
    top, bottom = call(
        arrange_kernel,
        [half, half],
        (4 * hbm, 2 * hbm),
        grid=(turns // step,),
        in_specs=[
            pl.BlockSpec((freqs, parts, step, rows, lon), lambda i: (0, 0, i, 0, 0)),
            pl.BlockSpec((rows, lon), lambda i: (0, 0)),
            pl.BlockSpec(memory_space=pl.ANY),
        ],
        out_specs=[half_spec, half_spec],
        scratch_shapes=[pltpu.VMEM((step, chunks, height, LANES), F32)],
    )(spectra.reshape(freqs, parts, turns, rows, lon), land_mask, ranges)
    down = [(i, i + 1) for i in range(bands - 1)]
    above = lax.ppermute(bottom, "band", down)
    below = lax.ppermute(top, "band", [(j, i) for i, j in down])

    advected, coefs = call(
        functools.partial(advect_kernel, directions, stretch),
        [
            jax.ShapeDtypeStruct((turns, height, padded), F32),
            jax.ShapeDtypeStruct((4, height, padded), F32),
        ],
        (50 * hbm, 4 * hbm),
        in_specs=[vmem] * 6,
        out_specs=[vmem, vmem],
        scratch_shapes=[pltpu.VMEM((2, height, padded), F32)],
    )(top, bottom, group_speed.T, depth_class, current, depth_slope)

    half = groups // 2
    block = (words * SUBLANES, slots)
    after, shipped = ranges, []
    for offsets, outputs in ((range(half, groups), [(1,) + block] * half), (range(half), [(half,) + block])):
        shipped.append(
            call(
                functools.partial(pack_kernel, directions, tuple(offsets)),
                [jax.ShapeDtypeStruct(shape, I32) for shape in outputs],
                (25 * hbm, 3 * hbm) if len(outputs) > 1 else LITTLE,
                in_specs=[vmem] * 5 + [smem, pl.BlockSpec(memory_space=pl.ANY)],
                out_specs=[vmem] * len(outputs),
                scratch_shapes=[
                    pltpu.VMEM((rows * chunks, words, SUBLANES, LANES), I32),
                    pltpu.VMEM((6 if chunks % 6 == 0 else 1, turns, SUBLANES, LANES), F32),
                    pltpu.VMEM((2, turns, SUBLANES, LANES), F32),
                ],
            )(advected, above, below, coefs, cells, ranges, after)
        )
        after = shipped[0][0]
    far = [
        lax.ppermute(part, "comp", [(i, i ^ (half + n)) for i in range(groups)]) for n, part in enumerate(shipped[0])
    ]
    halves = [list(range(half)), list(range(half, groups))]
    near = lax.all_to_all(shipped[1][0], "comp", split_axis=0, concat_axis=0, axis_index_groups=halves, tiled=True)

    total = total_freqs * directions
    values = jax.ShapeDtypeStruct((half, turns, SUBLANES, slots), F32)
    grown, slot_wind = call(
        functools.partial(grow_kernel, directions),
        [values, jax.ShapeDtypeStruct((2, SUBLANES, slots), F32)],
        LITTLE,
        in_specs=[vmem, vmem, smem],
        out_specs=[vmem, vmem],
        scratch_shapes=[pltpu.VMEM((rows * chunks, SUBLANES, LANES), F32)],
    )(wind, cells, ranges)

    early, sums = call(
        functools.partial(early_kernel, directions, half),
        [values, jax.ShapeDtypeStruct((SUBLANES, slots), F32)],
        MUCH,
        in_specs=[pl.BlockSpec(memory_space=pltpu.HBM)] * half + [vmem],
        out_specs=[vmem, vmem],
        scratch_shapes=[pltpu.VMEM((half, 1) + block, I32), pltpu.SemaphoreType.DMA((half,))],
    )(*far, slot_wind)

    result = call(
        functools.partial(finish_kernel, freqs, half),
        jax.ShapeDtypeStruct((slot_count, total), jnp.bfloat16),
        (50 * total * slots, 6 * total * slots),
        vmem=FINISH_VMEM,
        in_specs=[vmem] * 4 + [smem],
        out_specs=vmem,
        scratch_shapes=[
            pltpu.VMEM((slots // LANES, half, turns, SUBLANES, LANES), F32),
            pltpu.VMEM((slots // LANES, 2, total // 2, LANES), F32),
        ],
    )(near, grown, early, sums, block_counts)
    return result.T


def solution(mesh):
    return jax.shard_map(
        body,
        mesh=mesh,
        in_specs=(
            P("comp", None, "band", None),
            P("band", None),
            P(),
            P(None, "band", None),
            P(None, "band", None),
            P(None, "band", None),
            P("band", None),
            P("band", None),
        ),
        out_specs=P(None, ("comp", "band")),
        check_vma=False,
    )
```

```python
import functools
import math

import jax
import jax.numpy as jnp
import numpy as np
from jax import lax
from jax.experimental import pallas as pl
from jax.experimental.pallas import tpu as pltpu
from jax.sharding import PartitionSpec as P

GROWTH_RATE = 0.05
DAMPING = 1.5
TURNING_SCALE = 0.5

LANES = 128
SUBLANES = 8
UNIT = 9
WORDS = 5
STEP_COUNT = 65500.0
EXPONENT_ZERO = 99
WINDOW = 4
VMEM_BYTES = 16 * 1024 * 1024
LITTLE = (1_000, 1_000)
MUCH = (200_000_000_000, 1_000_000)
WHOLE_VMEM = 62_000_000

F32 = jnp.float32
I32 = jnp.int32


def call(kernel, out_shape, cost, vmem=VMEM_BYTES, **options):
    flops, moved = cost
    return pl.pallas_call(
        kernel,
        out_shape=out_shape,
        cost_estimate=pl.CostEstimate(flops=flops, bytes_accessed=moved, transcendentals=0),
        compiler_params=pltpu.CompilerParams(vmem_limit_bytes=vmem),
        **options,
    )


def iota(shape, axis):
    return lax.broadcasted_iota(I32, shape, axis)


def upwind(speed, far_behind, behind, centre, ahead, far_ahead):
    positive = speed > 0
    near = jnp.where(positive, behind, ahead)
    after = jnp.where(positive, ahead, behind)
    far = jnp.where(positive, far_behind, far_ahead)
    return jnp.abs(speed) * (2.0 * after + far + 3.0 * (centre - 2.0 * near))


def signs(part, parts, turns, directions, j):
    sin, cos = None, None
    for h in range(parts):
        angle = 2.0 * math.pi * (h * turns + j) / directions
        if h == 0:
            sin = jnp.full(part.shape, math.sin(angle), F32)
            cos = jnp.full(part.shape, math.cos(angle), F32)
        else:
            sin = jnp.where(part == h, math.sin(angle), sin)
            cos = jnp.where(part == h, math.cos(angle), cos)
    return sin, cos


def power_table(start, sign):
    lane = iota((SUBLANES, LANES), 1)
    table = jnp.full((SUBLANES, LANES), start, F32)
    for bit in range(7):
        factor = 2.0 ** (sign * 2**bit)
        table = jnp.where((lane & (1 << bit)) != 0, table * factor, table)
    return table


def arrange_kernel(x_ref, land_ref, after_ref, top_ref, bottom_ref, scratch):
    freqs, parts, step, rows, lon = x_ref.shape
    chunks = scratch.shape[1]
    tail = lon - (chunks - 1) * LANES
    filler = jnp.zeros((rows, LANES - tail), F32)
    lane = iota((SUBLANES * rows, LANES), 1)
    for j in range(step):
        for f in range(freqs):
            for h in range(parts):
                place = pl.ds(f * parts + h, rows, stride=SUBLANES)
                for k in range(chunks):
                    if k < chunks - 1:
                        piece = x_ref[f, h, j, :, k * LANES : (k + 1) * LANES].astype(F32)
                    else:
                        piece = x_ref[f, h, j, :, k * LANES : lon].astype(F32)
                        piece = jnp.concatenate([piece, filler], axis=1)
                    scratch[j, k, place, :] = piece
    initial = [None] * step
    for k in range(chunks):
        span = slice(k * LANES, (k + 1) * LANES)
        land = land_ref[:, k * LANES : min((k + 1) * LANES, lon)]
        if k == chunks - 1:
            land = jnp.concatenate([land, jnp.ones((rows, LANES - tail), I32)], axis=1)
        sea = (land == 0).astype(F32)
        sea = jnp.concatenate([jnp.broadcast_to(sea[r : r + 1], (SUBLANES, LANES)) for r in range(rows)], axis=0)
        for j in range(step):
            piece = scratch[j, k] * sea
            if k == 0:
                initial[j] = piece
            if k == chunks - 1:
                wrapped = jnp.where(
                    lane < tail + 2,
                    pltpu.roll(initial[j], tail, axis=1),
                    pltpu.roll(piece, LANES - tail, axis=1),
                )
                piece = jnp.where(lane < tail, piece, wrapped)
            piece = piece.astype(jnp.bfloat16)
            top_ref[j, :, span] = piece[: 2 * SUBLANES]
            bottom_ref[j, :, span] = piece[2 * SUBLANES :]


def index_kernel(land_ref, counts_ref, cells_ref, ranges_ref, flat):
    chunks = flat.shape[0]
    rows, lon = land_ref.shape
    per_row = chunks // rows
    tail = lon - (per_row - 1) * LANES
    flat[...] = jnp.ones(flat.shape, I32)
    for r in range(rows):
        for k in range(per_row):
            size = LANES if k < per_row - 1 else tail
            piece = land_ref[r : r + 1, k * LANES : k * LANES + size]
            flat[r * per_row + k : r * per_row + k + 1, :size] = piece
    groups, _, slots = cells_ref.shape
    spans = slots // LANES
    sea = (flat[...] == 0).astype(jnp.bfloat16)
    square = (LANES, LANES)
    ones_before = (iota(square, 1) <= iota(square, 0)).astype(jnp.bfloat16)
    ranks = lax.dot_general(ones_before, sea, (((1,), (1,)), ((), ())), preferred_element_type=F32)
    totals = jnp.dot(sea, jnp.ones(square, jnp.bfloat16), preferred_element_type=F32)
    chunk_square = (chunks, chunks)
    chunks_before = (iota(chunk_square, 1) <= iota(chunk_square, 0)).astype(jnp.bfloat16)
    through = jnp.dot(chunks_before, totals.astype(jnp.bfloat16), preferred_element_type=F32)
    through_column = through[:, :1]
    total_column = totals[:, :1]
    ranks = ranks.astype(jnp.bfloat16)
    chunk_ids = iota((chunks, slots), 0)
    slot_ids = iota((1, slots), 1)
    span_lane = iota((1, LANES), 1)
    start = jnp.int32(0)
    longest = jnp.zeros((1, 1), F32)
    for c in range(groups):
        count = counts_ref[0, c]
        number = (slot_ids + start).astype(F32)
        passed = (through_column <= number).astype(F32)
        chunk_of = jnp.sum(passed, axis=0, keepdims=True)
        before = jnp.sum(passed * total_column, axis=0, keepdims=True)
        chunk_of = chunk_of.astype(I32)
        chosen = (chunk_ids == chunk_of).astype(jnp.bfloat16)
        inside = jnp.dot(ranks, chosen, preferred_element_type=F32)
        lane = jnp.sum((inside <= number - before).astype(F32), axis=0, keepdims=True)
        valid = slot_ids < count
        found = jnp.where(valid, chunk_of * LANES + lane.astype(I32), -1)
        cells_ref[c] = jnp.broadcast_to(found, (SUBLANES, slots))
        bounds = jnp.zeros((1, LANES), I32)
        final = jnp.zeros((1, 1), F32)
        for m in range(spans):
            span = slice(m * LANES, (m + 1) * LANES)
            own = chunk_of[:, span].astype(F32)
            low = jnp.min(jnp.where(valid[:, span], own, float(chunks)), axis=1, keepdims=True)
            high = jnp.max(jnp.where(valid[:, span], own, -1.0), axis=1, keepdims=True)
            longest = jnp.maximum(longest, high - low + 1.0)
            final = jnp.maximum(final, high)
            bounds = jnp.where(span_lane == m, low.astype(I32), bounds)
            bounds = jnp.where(span_lane == m + spans, high.astype(I32), bounds)
        bounds = jnp.where(span_lane == 2 * spans, final.astype(I32), bounds)
        ranges_ref[c : c + 1, :] = bounds
        start = start + count
    ranges_ref[groups : groups + 1, :] = jnp.broadcast_to(longest.astype(I32), (1, LANES))


def advect_kernel(
    directions,
    stretch,
    top_ref,
    bottom_ref,
    speed_ref,
    depth_ref,
    current_ref,
    slope_ref,
    out_ref,
    coef_ref,
    scratch,
    along,
    trig,
):
    turns, _, padded = top_ref.shape
    rows, lon = depth_ref.shape
    chunks = padded // LANES
    tail = lon - (chunks - 1) * LANES
    total_freqs, depths = speed_ref.shape
    parts = directions // turns
    freqs = SUBLANES // parts
    comp, band = lax.axis_index("comp"), lax.axis_index("band")
    speeds = speed_ref[...]
    freq_ids = iota(speeds.shape, 0)
    table = []
    for f in range(freqs):
        row = jnp.sum(jnp.where(freq_ids == comp * freqs + f, speeds, 0.0), axis=0, keepdims=True)
        table.append(jnp.broadcast_to(row, (parts, depths)))
    table = jnp.concatenate(table, axis=0)
    table = jnp.concatenate([table, jnp.zeros((SUBLANES, LANES - depths), F32)], axis=1) * (1.0 / 6.0)
    shape = (SUBLANES, LANES)
    for r in range(rows):
        place = slice(r * SUBLANES, (r + 1) * SUBLANES)
        widening = jnp.float32(0.0)
        for b in range(len(stretch) // rows):
            widening = jnp.where(band == b, jnp.float32(stretch[b * rows + r]), widening)
        for k in range(chunks):
            span = slice(k * LANES, (k + 1) * LANES)

            def field(row):
                if k == chunks - 1:
                    row = jnp.concatenate([row[:, :tail], jnp.zeros((1, LANES - tail), row.dtype)], axis=1)
                return jnp.broadcast_to(row, shape)

            own = slice(k * LANES, min((k + 1) * LANES, lon))
            classes = field(depth_ref[r : r + 1, own])
            sixth = jnp.take_along_axis(table, classes, axis=1, mode="promise_in_bounds")
            coef_ref[0, place, span] = sixth
            coef_ref[1, place, span] = field(current_ref[1, r : r + 1, own]) * (1.0 / 6.0)
            coef_ref[2, place, span] = sixth * TURNING_SCALE * field(slope_ref[0, r : r + 1, own])
            coef_ref[3, place, span] = sixth * TURNING_SCALE * field(slope_ref[1, r : r + 1, own])
            scratch[0, place, span] = sixth * widening
            scratch[1, place, span] = field(current_ref[0, r : r + 1, own]) * (1.0 / 6.0)

    source, target = iota((3 * LANES, 2 * LANES), 0), iota((3 * LANES, 2 * LANES), 1)
    distance = source - LANES - (target & (LANES - 1))
    odd = target < LANES
    weights = jnp.zeros(distance.shape, F32)
    for at, first, second in ((-2, 0.5, 0.5), (-1, -4.0, -2.0), (0, 0.0, 3.0), (1, 4.0, -2.0), (2, -0.5, 0.5)):
        weights = jnp.where(distance == at, jnp.where(odd, first, second), weights)
    weights = weights.astype(jnp.bfloat16)
    part = iota(shape, 0) % parts
    for j in range(turns):
        trig[0, j], trig[1, j] = signs(part, parts, turns, directions, j)

    def one_chunk(k, carry):
        span = pl.ds(pl.multiple_of(k * LANES, LANES), LANES)
        before = pl.ds(pl.multiple_of(((k + chunks - 1) % chunks) * LANES, LANES), LANES)
        after = pl.ds(pl.multiple_of(((k + 1) % chunks) * LANES, LANES), LANES)
        for n, ref in enumerate((top_ref, bottom_ref)):
            wide = jnp.concatenate([ref[:, :, before], ref[:, :, span], ref[:, :, after]], axis=2)
            wide = wide.reshape(turns * 2 * SUBLANES, 3 * LANES)
            product = jnp.dot(wide, weights, preferred_element_type=F32)
            along[n] = product.reshape(turns, 2 * SUBLANES, 2 * LANES)
        places = [slice(r * SUBLANES, (r + 1) * SUBLANES) for r in range(rows)]
        sixths = [coef_ref[0, place, span] for place in places]
        currents_y = [coef_ref[1, place, span] for place in places]
        widened = [scratch[0, place, span] for place in places]
        currents_x = [scratch[1, place, span] for place in places]
        for j in range(turns):
            sin, cos = trig[0, j], trig[1, j]
            centres = []
            for ref in (top_ref, bottom_ref):
                pair = ref[j, :, span].astype(F32)
                centres += [pair[:SUBLANES], pair[SUBLANES:]]
            for r in range(rows):
                at = slice((r % 2) * SUBLANES, (r % 2 + 1) * SUBLANES)
                speed_x = widened[r] * cos + currents_x[r]
                moved = speed_x * along[r // 2, j, at, :LANES] + jnp.abs(speed_x) * along[r // 2, j, at, LANES:]
                speed_y = sixths[r] * sin + currents_y[r]
                near = [centres[n] if 0 <= n < rows else 0.0 for n in range(r - 2, r + 3)]
                out_ref[j, places[r], span] = centres[r] - moved - upwind(speed_y, *near)
        return carry

    lax.fori_loop(0, chunks, one_chunk, 0)


def pack_kernel(directions, offsets, adv_ref, above_ref, below_ref, coef_ref, cells_ref, ranges_ref, after_ref, *refs):
    out_refs, (packed, turned_values, trig) = refs[:-3], refs[-3:]
    turns, height, padded = adv_ref.shape
    rows = height // SUBLANES
    chunks = padded // LANES
    parts = directions // turns
    units = turns // UNIT
    shape = (SUBLANES, LANES)
    part = iota(shape, 0) % parts
    scale = power_table(STEP_COUNT * 2.0**EXPONENT_ZERO, -1)
    together = turned_values.shape[0]
    for j in range(turns):
        trig[0, j], trig[1, j] = signs(part, parts, turns, directions, j)

    def turned(value, by):
        if by == 0:
            return value
        if by > 0:
            return jnp.where(
                part == parts - 1, pltpu.roll(value, parts - 1, axis=0), pltpu.roll(value, SUBLANES - 1, axis=0)
            )
        return jnp.where(part == 0, pltpu.roll(value, SUBLANES - parts + 1, axis=0), pltpu.roll(value, 1, axis=0))

    def refract(r, k, into):
        place = slice(r * SUBLANES, (r + 1) * SUBLANES)
        span = pl.ds(pl.multiple_of(k * LANES, LANES), LANES)
        sixth, current_y, turn_x, turn_y = [coef_ref[n, place, span] for n in range(4)]
        advected = []
        for j in range(turns):
            speed = sixth * trig[0, j] + current_y
            positive = speed > 0
            ref = above_ref if r < 2 else below_ref
            outer = ref[j, :, span].astype(F32)
            low, high = outer[:SUBLANES], outer[SUBLANES:]
            if r == 0:
                share = jnp.where(positive, low - 6.0 * high, 2.0 * high)
            elif r == 1:
                share = jnp.where(positive, high, 0.0)
            elif r == rows - 2:
                share = jnp.where(positive, 0.0, low)
            else:
                share = jnp.where(positive, 2.0 * low, high - 6.0 * low)
            advected.append(adv_ref[j, place, span] - jnp.abs(speed) * share)
        around = {j: turned(advected[j % turns], j // turns) for j in range(-2, turns + 2)}
        largest = [None] * units
        for j in range(turns):
            speed = trig[0, j] * turn_x - trig[1, j] * turn_y
            value = around[j] - upwind(speed, *[around[n] for n in range(j - 2, j + 3)])
            turned_values[into, j] = value
            size = jnp.abs(value)
            unit = j // UNIT
            largest[unit] = size if largest[unit] is None else jnp.maximum(largest[unit], size)
        return largest

    def code(chunk, come_from, unit, largest):
        level = jnp.ceil(jnp.log2(jnp.maximum(largest, 2.0**-98)))
        level = jnp.minimum(level, 28.0).astype(I32) + EXPONENT_ZERO
        level = jnp.maximum(level, 1)
        inverse = jnp.take_along_axis(scale, level, axis=1, mode="promise_in_bounds")
        codes = [
            (turned_values[come_from, unit * UNIT + n] * inverse + 65536.5).astype(I32) for n in range(UNIT)
        ]
        first = unit * WORDS
        rest = codes[8] | (level << 17)
        for n in range(4):
            even, odd = codes[2 * n], codes[2 * n + 1]
            packed[chunk, first + n] = even | (odd << 17)
            rest = rest | ((odd >> 15) << (24 + 2 * n))
        packed[chunk, first + 4] = rest

    half = len(offsets)
    _, words, slots = out_refs[0].shape
    words = words // SUBLANES
    spans = slots // LANES
    comp = lax.axis_index("comp")
    base = ((comp ^ offsets[0]) // half) * half
    first_set = ranges_ref[base, 0] // together
    last_set = ranges_ref[base + half - 1, 2 * spans] // together
    sets = chunks // together
    for r in range(rows):

        def some_chunks(i, carry):
            found = [refract(r, i * together + n, n) for n in range(together)]
            for n in range(together):
                for unit in range(units):
                    code(r * chunks + i * together + n, n, unit, found[n][unit])
            return carry

        low = jnp.clip(first_set - r * sets, 0, sets)
        high = jnp.clip(last_set + 1 - r * sets, 0, sets)
        lax.fori_loop(low, high, some_chunks, 0)

    last = rows * chunks - 1

    def merged(cells, chunk, sums):
        lane = cells - chunk * LANES
        here = (lane >= 0) & (lane < LANES)
        lane = lane & (LANES - 1)
        return tuple(
            jnp.where(
                here, jnp.take_along_axis(packed[chunk, n], lane, axis=1, mode="promise_in_bounds"), sums[n]
            )
            for n in range(words)
        )

    if len(out_refs) == half:
        places = [(comp ^ offset, out_ref, 0) for offset, out_ref in zip(offsets, out_refs)]
    else:
        places = [(base + n, out_refs[0], n) for n in range(half)]
    for block, out_ref, at in places:
        for m in range(spans):
            span = slice(m * LANES, (m + 1) * LANES)
            cells = cells_ref[block, :, span]
            low = ranges_ref[block, m]
            sums = tuple(jnp.zeros(shape, I32) for _ in range(words))
            for t in range(WINDOW):
                sums = merged(cells, jnp.minimum(low + t, last), sums)
            for n in range(words):
                out_ref[at, n * SUBLANES : (n + 1) * SUBLANES, span] = sums[n]

    @pl.when(ranges_ref[cells_ref.shape[0], 0] > WINDOW)
    def _():
        for block, out_ref, at in places:
            for m in range(spans):
                span = slice(m * LANES, (m + 1) * LANES)
                cells = cells_ref[block, :, span]
                low, high = ranges_ref[block, m], ranges_ref[block, m + spans]
                sums = tuple(out_ref[at, n * SUBLANES : (n + 1) * SUBLANES, span] for n in range(words))
                sums = lax.fori_loop(
                    low + WINDOW, high + 1, lambda chunk, sums: merged(cells, chunk, sums), sums
                )
                for n in range(words):
                    out_ref[at, n * SUBLANES : (n + 1) * SUBLANES, span] = sums[n]


def growth_rates(half, freqs, side):
    shape = (SUBLANES, LANES)
    freq = iota(shape, 0) // (SUBLANES // freqs)
    step = jnp.where(side == 0, jnp.float32(1.0), jnp.float32(1.1 ** (half * freqs)))
    rates = []
    for source in range(half):
        slope, threshold = jnp.zeros(shape, F32), jnp.zeros(shape, F32)
        for f in range(freqs):
            angular, ratio = frequency(source * freqs + f, 2 * half * freqs)
            slope = jnp.where(freq == f, GROWTH_RATE * ratio * angular / 9.81, slope)
            threshold = jnp.where(freq == f, GROWTH_RATE * ratio, threshold)
        rates.append((slope * (step * step), threshold * step))
    return rates


def grow_kernel(directions, wind_ref, cells_ref, ranges_ref, after_ref, near_ref, far_ref, flat, slot_wind):
    half, turns, _, slots = near_ref.shape
    rows, lon = wind_ref.shape[1:]
    chunks = flat.shape[0] // rows
    tail = lon - (chunks - 1) * LANES
    spans = slots // LANES
    parts = directions // turns
    freqs = SUBLANES // parts
    shape = (SUBLANES, LANES)
    part = iota(shape, 0) % parts
    comp = lax.axis_index("comp")
    for r in range(rows):
        for k in range(chunks):
            size = LANES if k < chunks - 1 else tail
            for n in range(2):
                flat[r * chunks + k, n : n + 1, :size] = wind_ref[n, r : r + 1, k * LANES : k * LANES + size]
    for m in range(spans):
        span = slice(m * LANES, (m + 1) * LANES)
        cells = cells_ref[comp, :, span]

        def merged(chunk, sums):
            lane = cells - chunk * LANES
            here = (lane >= 0) & (lane < LANES)
            lane = lane & (LANES - 1)
            return jnp.where(
                here, jnp.take_along_axis(flat[chunk], lane, axis=1, mode="promise_in_bounds"), sums
            )

        found = lax.fori_loop(
            ranges_ref[comp, m], ranges_ref[comp, m + spans] + 1, merged, jnp.zeros(shape, F32)
        )
        slot_wind[0, :, span] = jnp.broadcast_to(found[0:1], shape)
        slot_wind[1, :, span] = jnp.broadcast_to(found[1:2], shape)

    rates = growth_rates(half, freqs, comp // half) + growth_rates(half, freqs, (comp // half) ^ 1)

    def one_span(m, carry):
        span = pl.ds(pl.multiple_of(m * LANES, LANES), LANES)
        east, north = slot_wind[0, :, span], slot_wind[1, :, span]
        for j in range(turns):
            sin, cos = signs(part, parts, turns, directions, j)
            along = east * cos + north * sin
            for source in range(half):
                slope, threshold = rates[source]
                near_ref[source, j, :, span] = jnp.exp(jnp.maximum(along * slope - threshold, 0.0))
                slope, threshold = rates[half + source]
                far_ref[(comp % half) ^ source, j, :, span] = jnp.exp(jnp.maximum(along * slope - threshold, 0.0))
        return carry

    lax.fori_loop(0, spans, one_span, 0)


def decode(arrived, half, turns, scale, span, store):
    sums = [jnp.zeros((SUBLANES, LANES), F32) for _ in range(2)]
    for source in range(half):
        for unit in range(turns // UNIT):
            words = [
                arrived[source, n * SUBLANES : (n + 1) * SUBLANES, span]
                for n in range(unit * WORDS, (unit + 1) * WORDS)
            ]
            rest = words[4]
            level = lax.shift_right_logical(rest, 17) & 127
            size = jnp.take_along_axis(scale, level, axis=1, mode="promise_in_bounds")
            offset = size * 65536.0
            for n in range(UNIT):
                if n == 8:
                    coded = rest & 0x1FFFF
                elif n % 2 == 0:
                    coded = words[n // 2] & 0x1FFFF
                else:
                    coded = lax.shift_right_logical(words[n // 2], 17) | (
                        lax.shift_right_logical(rest, 9 + n - 1) & 0x18000
                    )
                value = coded.astype(F32) * size - offset
                sums[n % 2] = sums[n % 2] + value * value
                j = unit * UNIT + n
                store(source, j, value)
    return sums[0] + sums[1]


def gate_kernel(*refs):
    refs[-1][...] = jnp.zeros(refs[-1].shape, F32)


def finish_kernel(freqs, half, *refs):
    far_refs, refs = refs[:half], refs[half:]
    near_ref, grown_near_ref, grown_far_ref, _, counts_ref, out_ref = refs[:6]
    far_words, near_words, near_values, far_values, ordered, arrivals = refs[6:]
    groups = 2 * half
    turns = near_values.shape[1]
    each = turns * SUBLANES
    shape = (SUBLANES, LANES)
    comp = lax.axis_index("comp")
    side, own = comp // half, comp % half
    count = counts_ref[0, comp]
    spans = [slice(low, low + LANES) for low in range(0, near_values.shape[-1], LANES)]
    copies = []
    for m, span in enumerate(spans):
        pairs = [(ref.at[0, :, span], far_words.at[n, :, span]) for n, ref in enumerate(far_refs)]
        pairs.append((near_ref.at[:, :, span], near_words.at[:, :, span]))
        pairs.append((grown_far_ref.at[:, :, :, span], far_values.at[:, :, :, span]))
        pairs.append((grown_near_ref.at[:, :, :, span], near_values.at[:, :, :, span]))
        copies.append([pltpu.make_async_copy(*pair, arrivals.at[m, n]) for n, pair in enumerate(pairs)])
        for copy in copies[-1]:
            copy.start()
    scale = power_table(2.0**-EXPONENT_ZERO / STEP_COUNT, 1)
    freq = iota(shape, 0) // (SUBLANES // freqs)
    square = (LANES, LANES)
    unit_matrix = (iota(square, 0) == iota(square, 1)).astype(jnp.bfloat16)
    steps = [jnp.where(side ^ far == 0, jnp.float32(1.0), jnp.float32(1.1 ** (half * freqs))) for far in range(2)]
    for m, span in enumerate(spans):
        for copy in copies[m]:
            copy.wait()

        def store_far(source, j, value):
            far_values[source, j, :, span] = value * far_values[source, j, :, span]

        def store_near(source, j, value):
            near_values[source, j, :, span] = value * near_values[source, j, :, span]

        sums = decode(far_words, half, turns, scale, span, store_far)
        sums = sums + decode(near_words, half, turns, scale, span, store_near)
        mean_sq = jnp.sum(sums, axis=0, keepdims=True) / float(groups * each)
        strength = jnp.broadcast_to(jnp.sqrt(mean_sq + 1e-06), shape)
        occupied = (m * LANES + iota(shape, 1)) < count
        for far in range(2):
            for source in range(half):
                rate = jnp.zeros(shape, F32)
                for f in range(freqs):
                    rate = jnp.where(freq == f, DAMPING * frequency(source * freqs + f, groups * freqs)[1], rate)
                factor = jnp.exp(-(rate * steps[far] * strength))
                for j in range(turns):
                    value = far_values[own ^ source, j, :, span] if far else near_values[source, j, :, span]
                    value = jnp.where(occupied, value * factor, 0.0)
                    ordered[m, side ^ far, pl.ds(source * each + j, SUBLANES, stride=turns), :] = value
        slots = slice(m * LANES, min((m + 1) * LANES, out_ref.shape[0]))
        for place in range(2):
            if place == 0:
                turned = lax.dot_general(
                    unit_matrix,
                    ordered[m, place].astype(jnp.bfloat16),
                    (((1,), (1,)), ((), ())),
                    preferred_element_type=F32,
                )
            else:
                turned = ordered[m, place].T
            out_ref[slots, place * half * each : (place + 1) * half * each] = turned[
                : slots.stop - slots.start
            ].astype(jnp.bfloat16)


def frequency(index, count):
    angular = 2.0 * math.pi * 0.0418 * 1.1**index
    return angular, 1.1 ** (index - (count - 1))


def body(spectra, depth_class, group_speed, current, depth_slope, wind, land_mask, block_counts):
    freqs, directions, rows, lon = spectra.shape
    total_freqs = group_speed.shape[1]
    groups = lax.axis_size("comp")
    bands = lax.axis_size("band")
    slot_count = rows * lon * 7 // (8 * groups)
    slots = -(-slot_count // LANES) * LANES
    parts = SUBLANES // freqs
    turns = directions // parts
    units = turns // UNIT
    chunks = -(-lon // LANES)
    padded = chunks * LANES
    height = rows * SUBLANES
    words = units * WORDS
    hbm = 2 * turns * height * padded
    latitude = (-60.0 + 120.0 * (np.arange(rows * bands) + 0.5) / (rows * bands)) * (math.pi / 180.0)
    stretch = [float(value) for value in 1.0 / np.cos(latitude)]
    smem = pl.BlockSpec(memory_space=pltpu.SMEM)
    vmem = pl.BlockSpec(memory_space=pltpu.VMEM)
    anywhere = pl.BlockSpec(memory_space=pl.ANY)

    range_rows = 2 * SUBLANES if groups < 2 * SUBLANES else 3 * SUBLANES
    cells, ranges = call(
        index_kernel,
        [
            jax.ShapeDtypeStruct((groups, SUBLANES, slots), I32),
            jax.ShapeDtypeStruct((range_rows, LANES), I32),
        ],
        (400_000 * groups * slots, 8 * groups * slots),
        in_specs=[vmem, smem],
        out_specs=[vmem, vmem],
        scratch_shapes=[pltpu.VMEM((rows * chunks, LANES), I32)],
    )(land_mask, block_counts)

    step = 3
    half = jax.ShapeDtypeStruct((turns, height // 2, padded), jnp.bfloat16)
    half_spec = pl.BlockSpec((step, height // 2, padded), lambda i: (i, 0, 0))
    top, bottom = call(
        arrange_kernel,
        [half, half],
        (4 * hbm, 2 * hbm),
        grid=(turns // step,),
        in_specs=[
            pl.BlockSpec((freqs, parts, step, rows, lon), lambda i: (0, 0, i, 0, 0)),
            pl.BlockSpec((rows, lon), lambda i: (0, 0)),
            anywhere,
        ],
        out_specs=[half_spec, half_spec],
        scratch_shapes=[pltpu.VMEM((step, chunks, height, LANES), F32)],
    )(spectra.reshape(freqs, parts, turns, rows, lon), land_mask, ranges)
    down = [(i, i + 1) for i in range(bands - 1)]
    above = lax.ppermute(bottom, "band", down)
    below = lax.ppermute(top, "band", [(j, i) for i, j in down])

    advected, coefs = call(
        functools.partial(advect_kernel, directions, stretch),
        [
            jax.ShapeDtypeStruct((turns, height, padded), F32),
            jax.ShapeDtypeStruct((4, height, padded), F32),
        ],
        (50 * hbm, 4 * hbm),
        in_specs=[vmem] * 6,
        out_specs=[vmem, vmem],
        scratch_shapes=[
            pltpu.VMEM((2, height, padded), F32),
            pltpu.VMEM((rows // 2, turns, 2 * SUBLANES, 2 * LANES), F32),
            pltpu.VMEM((2, turns, SUBLANES, LANES), F32),
        ],
    )(top, bottom, group_speed.T, depth_class, current, depth_slope)

    half = groups // 2
    block = (words * SUBLANES, slots)
    after, shipped = ranges, []
    for offsets, outputs in ((range(half, groups), [(1,) + block] * half), (range(half), [(half,) + block])):
        shipped.append(
            call(
                functools.partial(pack_kernel, directions, tuple(offsets)),
                [jax.ShapeDtypeStruct(shape, I32) for shape in outputs],
                (25 * hbm, 3 * hbm) if len(outputs) > 1 else LITTLE,
                in_specs=[vmem] * 5 + [smem, anywhere],
                out_specs=[vmem] * len(outputs),
                scratch_shapes=[
                    pltpu.VMEM((rows * chunks, words, SUBLANES, LANES), I32),
                    pltpu.VMEM((6 if chunks % 6 == 0 else 1, turns, SUBLANES, LANES), F32),
                    pltpu.VMEM((2, turns, SUBLANES, LANES), F32),
                ],
            )(advected, above, below, coefs, cells, ranges, after)
        )
        after = shipped[0][0]
    far = [
        lax.ppermute(part, "comp", [(i, i ^ (half + n)) for i in range(groups)]) for n, part in enumerate(shipped[0])
    ]
    halves = [list(range(half)), list(range(half, groups))]
    near = lax.all_to_all(shipped[1][0], "comp", split_axis=0, concat_axis=0, axis_index_groups=halves, tiled=True)

    total = total_freqs * directions
    values = jax.ShapeDtypeStruct((half, turns, SUBLANES, slots), F32)
    grown_near, grown_far = call(
        functools.partial(grow_kernel, directions),
        [values, values],
        LITTLE,
        vmem=WHOLE_VMEM,
        in_specs=[vmem, vmem, smem, anywhere],
        out_specs=[vmem, vmem],
        scratch_shapes=[
            pltpu.VMEM((rows * chunks, SUBLANES, LANES), F32),
            pltpu.VMEM((2, SUBLANES, slots), F32),
        ],
    )(wind, cells, ranges, shipped[1][0])

    gate = call(
        gate_kernel,
        jax.ShapeDtypeStruct((SUBLANES, LANES), F32),
        MUCH,
        vmem=WHOLE_VMEM,
        in_specs=[anywhere] * half,
        out_specs=vmem,
    )(*far)

    result = call(
        functools.partial(finish_kernel, freqs, half),
        jax.ShapeDtypeStruct((slot_count, total), jnp.bfloat16),
        (50 * total * slots, 6 * total * slots),
        vmem=WHOLE_VMEM,
        in_specs=[anywhere] * (half + 4) + [smem],
        out_specs=vmem,
        scratch_shapes=[
            pltpu.VMEM((half,) + block, I32),
            pltpu.VMEM((half,) + block, I32),
            pltpu.VMEM((half, turns, SUBLANES, slots), F32),
            pltpu.VMEM((half, turns, SUBLANES, slots), F32),
            pltpu.VMEM((slots // LANES, 2, total // 2, LANES), F32),
            pltpu.SemaphoreType.DMA((slots // LANES, half + 3)),
        ],
    )(*far, near, grown_near, grown_far, gate, block_counts)
    return result.T


def solution(mesh):
    return jax.shard_map(
        body,
        mesh=mesh,
        in_specs=(
            P("comp", None, "band", None),
            P("band", None),
            P(),
            P(None, "band", None),
            P(None, "band", None),
            P(None, "band", None),
            P("band", None),
            P("band", None),
        ),
        out_specs=P(None, ("comp", "band")),
        check_vma=False,
    )
```

```python
import functools
import math

import jax
import jax.numpy as jnp
import numpy as np
from jax import lax
from jax.experimental import pallas as pl
from jax.experimental.pallas import tpu as pltpu
from jax.sharding import PartitionSpec as P

GROWTH_RATE = 0.05
DAMPING = 1.5
TURNING_SCALE = 0.5

LANES = 128
SUBLANES = 8
UNIT = 9
WORDS = 5
STEP_COUNT = 65500.0
EXPONENT_ZERO = 99
WINDOW = 4
VMEM_BYTES = 16 * 1024 * 1024
LITTLE = (1_000, 1_000)
MUCH = (200_000_000_000, 1_000_000)
WHOLE_VMEM = 62_000_000

F32 = jnp.float32
I32 = jnp.int32


def call(kernel, out_shape, cost, vmem=VMEM_BYTES, **options):
    flops, moved = cost
    return pl.pallas_call(
        kernel,
        out_shape=out_shape,
        cost_estimate=pl.CostEstimate(flops=flops, bytes_accessed=moved, transcendentals=0),
        compiler_params=pltpu.CompilerParams(vmem_limit_bytes=vmem),
        **options,
    )


def iota(shape, axis):
    return lax.broadcasted_iota(I32, shape, axis)


def upwind(speed, far_behind, behind, centre, ahead, far_ahead):
    positive = speed > 0
    near = jnp.where(positive, behind, ahead)
    after = jnp.where(positive, ahead, behind)
    far = jnp.where(positive, far_behind, far_ahead)
    return jnp.abs(speed) * (2.0 * after + far + 3.0 * (centre - 2.0 * near))


def signs(part, parts, turns, directions, j):
    sin, cos = None, None
    for h in range(parts):
        angle = 2.0 * math.pi * (h * turns + j) / directions
        if h == 0:
            sin = jnp.full(part.shape, math.sin(angle), F32)
            cos = jnp.full(part.shape, math.cos(angle), F32)
        else:
            sin = jnp.where(part == h, math.sin(angle), sin)
            cos = jnp.where(part == h, math.cos(angle), cos)
    return sin, cos


def power_table(start, sign):
    lane = iota((SUBLANES, LANES), 1)
    table = jnp.full((SUBLANES, LANES), start, F32)
    for bit in range(7):
        factor = 2.0 ** (sign * 2**bit)
        table = jnp.where((lane & (1 << bit)) != 0, table * factor, table)
    return table


def arrange_kernel(x_ref, land_ref, after_ref, top_ref, bottom_ref, scratch):
    freqs, parts, step, rows, lon = x_ref.shape
    chunks = scratch.shape[1]
    tail = lon - (chunks - 1) * LANES
    filler = jnp.zeros((rows, LANES - tail), F32)
    lane = iota((SUBLANES * rows, LANES), 1)
    for j in range(step):
        for f in range(freqs):
            for h in range(parts):
                place = pl.ds(f * parts + h, rows, stride=SUBLANES)
                for k in range(chunks):
                    if k < chunks - 1:
                        piece = x_ref[f, h, j, :, k * LANES : (k + 1) * LANES].astype(F32)
                    else:
                        piece = x_ref[f, h, j, :, k * LANES : lon].astype(F32)
                        piece = jnp.concatenate([piece, filler], axis=1)
                    scratch[j, k, place, :] = piece
    initial = [None] * step
    for k in range(chunks):
        span = slice(k * LANES, (k + 1) * LANES)
        land = land_ref[:, k * LANES : min((k + 1) * LANES, lon)]
        if k == chunks - 1:
            land = jnp.concatenate([land, jnp.ones((rows, LANES - tail), I32)], axis=1)
        sea = (land == 0).astype(F32)
        sea = jnp.concatenate([jnp.broadcast_to(sea[r : r + 1], (SUBLANES, LANES)) for r in range(rows)], axis=0)
        for j in range(step):
            piece = scratch[j, k] * sea
            if k == 0:
                initial[j] = piece
            if k == chunks - 1:
                wrapped = jnp.where(
                    lane < tail + 2,
                    pltpu.roll(initial[j], tail, axis=1),
                    pltpu.roll(piece, LANES - tail, axis=1),
                )
                piece = jnp.where(lane < tail, piece, wrapped)
            piece = piece.astype(jnp.bfloat16)
            top_ref[j, :, span] = piece[: 2 * SUBLANES]
            bottom_ref[j, :, span] = piece[2 * SUBLANES :]


def index_kernel(land_ref, cells_ref, ranges_ref, flat):
    chunks = flat.shape[0]
    rows, lon = land_ref.shape[0] - 1, land_ref.shape[1]
    per_row = chunks // rows
    tail = lon - (per_row - 1) * LANES
    flat[...] = jnp.ones(flat.shape, I32)
    for r in range(rows):
        for k in range(per_row):
            size = LANES if k < per_row - 1 else tail
            piece = land_ref[r : r + 1, k * LANES : k * LANES + size]
            flat[r * per_row + k : r * per_row + k + 1, :size] = piece
    groups, _, slots = cells_ref.shape
    spans = slots // LANES
    sea = (flat[...] == 0).astype(jnp.bfloat16)
    square = (LANES, LANES)
    ones_before = (iota(square, 1) <= iota(square, 0)).astype(jnp.bfloat16)
    ranks = lax.dot_general(ones_before, sea, (((1,), (1,)), ((), ())), preferred_element_type=F32)
    totals = jnp.dot(sea, jnp.ones(square, jnp.bfloat16), preferred_element_type=F32)
    chunk_square = (chunks, chunks)
    chunks_before = (iota(chunk_square, 1) <= iota(chunk_square, 0)).astype(jnp.bfloat16)
    through = jnp.dot(chunks_before, totals.astype(jnp.bfloat16), preferred_element_type=F32)
    through_column = through[:, :1]
    total_column = totals[:, :1]
    ranks = ranks.astype(jnp.bfloat16)
    chunk_ids = iota((chunks, slots), 0)
    slot_ids = iota((1, slots), 1)
    span_lane = iota((1, LANES), 1)
    start = jnp.zeros((1, 1), I32)
    longest = jnp.zeros((1, 1), F32)
    for c in range(groups):
        count = land_ref[rows : rows + 1, c : c + 1]
        number = (slot_ids + start).astype(F32)
        passed = (through_column <= number).astype(F32)
        chunk_of = jnp.sum(passed, axis=0, keepdims=True)
        before = jnp.sum(passed * total_column, axis=0, keepdims=True)
        chunk_of = chunk_of.astype(I32)
        chosen = (chunk_ids == chunk_of).astype(jnp.bfloat16)
        inside = jnp.dot(ranks, chosen, preferred_element_type=F32)
        lane = jnp.sum((inside <= number - before).astype(F32), axis=0, keepdims=True)
        valid = slot_ids < count
        found = jnp.where(valid, chunk_of * LANES + lane.astype(I32), -1)
        cells_ref[c] = jnp.broadcast_to(found, (SUBLANES, slots))
        bounds = jnp.zeros((1, LANES), I32)
        final = jnp.zeros((1, 1), F32)
        for m in range(spans):
            span = slice(m * LANES, (m + 1) * LANES)
            own = chunk_of[:, span].astype(F32)
            low = jnp.min(jnp.where(valid[:, span], own, float(chunks)), axis=1, keepdims=True)
            high = jnp.max(jnp.where(valid[:, span], own, -1.0), axis=1, keepdims=True)
            longest = jnp.maximum(longest, high - low + 1.0)
            final = jnp.maximum(final, high)
            bounds = jnp.where(span_lane == m, low.astype(I32), bounds)
            bounds = jnp.where(span_lane == m + spans, high.astype(I32), bounds)
        bounds = jnp.where(span_lane == 2 * spans, final.astype(I32), bounds)
        ranges_ref[c : c + 1, :] = bounds
        start = start + count
    ranges_ref[groups : groups + 1, :] = jnp.broadcast_to(longest.astype(I32), (1, LANES))


def advect_kernel(
    directions,
    stretch,
    top_ref,
    bottom_ref,
    speed_ref,
    depth_ref,
    current_ref,
    slope_ref,
    out_ref,
    coef_ref,
    scratch,
    along,
    trig,
):
    turns, _, padded = top_ref.shape
    rows, lon = depth_ref.shape
    chunks = padded // LANES
    tail = lon - (chunks - 1) * LANES
    total_freqs, depths = speed_ref.shape
    parts = directions // turns
    freqs = SUBLANES // parts
    comp, band = lax.axis_index("comp"), lax.axis_index("band")
    speeds = speed_ref[...]
    freq_ids = iota(speeds.shape, 0)
    table = []
    for f in range(freqs):
        row = jnp.sum(jnp.where(freq_ids == comp * freqs + f, speeds, 0.0), axis=0, keepdims=True)
        table.append(jnp.broadcast_to(row, (parts, depths)))
    table = jnp.concatenate(table, axis=0)
    table = jnp.concatenate([table, jnp.zeros((SUBLANES, LANES - depths), F32)], axis=1) * (1.0 / 6.0)
    shape = (SUBLANES, LANES)
    for r in range(rows):
        place = slice(r * SUBLANES, (r + 1) * SUBLANES)
        widening = jnp.float32(0.0)
        for b in range(len(stretch) // rows):
            widening = jnp.where(band == b, jnp.float32(stretch[b * rows + r]), widening)
        for k in range(chunks):
            span = slice(k * LANES, (k + 1) * LANES)

            def field(row):
                if k == chunks - 1:
                    row = jnp.concatenate([row[:, :tail], jnp.zeros((1, LANES - tail), row.dtype)], axis=1)
                return jnp.broadcast_to(row, shape)

            own = slice(k * LANES, min((k + 1) * LANES, lon))
            classes = field(depth_ref[r : r + 1, own])
            sixth = jnp.take_along_axis(table, classes, axis=1, mode="promise_in_bounds")
            coef_ref[0, place, span] = sixth
            coef_ref[1, place, span] = field(current_ref[1, r : r + 1, own]) * (1.0 / 6.0)
            coef_ref[2, place, span] = sixth * TURNING_SCALE * field(slope_ref[0, r : r + 1, own])
            coef_ref[3, place, span] = sixth * TURNING_SCALE * field(slope_ref[1, r : r + 1, own])
            scratch[0, place, span] = sixth * widening
            scratch[1, place, span] = field(current_ref[0, r : r + 1, own]) * (1.0 / 6.0)

    source, target = iota((3 * LANES, 2 * LANES), 0), iota((3 * LANES, 2 * LANES), 1)
    distance = source - LANES - (target & (LANES - 1))
    odd = target < LANES
    weights = jnp.zeros(distance.shape, F32)
    for at, first, second in ((-2, 0.5, 0.5), (-1, -4.0, -2.0), (0, 0.0, 3.0), (1, 4.0, -2.0), (2, -0.5, 0.5)):
        weights = jnp.where(distance == at, jnp.where(odd, first, second), weights)
    weights = weights.astype(jnp.bfloat16)
    part = iota(shape, 0) % parts
    for j in range(turns):
        trig[0, j], trig[1, j] = signs(part, parts, turns, directions, j)

    together = along.shape[0]

    def lanes(k):
        return pl.ds(pl.multiple_of(k * LANES, LANES), LANES)

    def some_chunks(i, carry):
        for at in range(together):
            k = i * together + at
            before, span, after = lanes((k + chunks - 1) % chunks), lanes(k), lanes((k + 1) % chunks)
            for n, ref in enumerate((top_ref, bottom_ref)):
                wide = jnp.concatenate([ref[:, :, before], ref[:, :, span], ref[:, :, after]], axis=2)
                wide = wide.reshape(turns * 2 * SUBLANES, 3 * LANES)
                product = jnp.dot(wide, weights, preferred_element_type=F32)
                along[at, n] = product.reshape(turns, 2 * SUBLANES, 2 * LANES)
        for at in range(together):
            one_chunk(lanes(i * together + at), at)
        return carry

    def one_chunk(span, at):
        places = [slice(r * SUBLANES, (r + 1) * SUBLANES) for r in range(rows)]
        sixths = [coef_ref[0, place, span] for place in places]
        currents_y = [coef_ref[1, place, span] for place in places]
        widened = [scratch[0, place, span] for place in places]
        currents_x = [scratch[1, place, span] for place in places]
        for j in range(turns):
            sin, cos = trig[0, j], trig[1, j]
            centres = []
            for ref in (top_ref, bottom_ref):
                pair = ref[j, :, span].astype(F32)
                centres += [pair[:SUBLANES], pair[SUBLANES:]]
            for r in range(rows):
                row = slice((r % 2) * SUBLANES, (r % 2 + 1) * SUBLANES)
                odd, even = along[at, r // 2, j, row, :LANES], along[at, r // 2, j, row, LANES:]
                speed_x = widened[r] * cos + currents_x[r]
                moved = speed_x * odd + jnp.abs(speed_x) * even
                speed_y = sixths[r] * sin + currents_y[r]
                near = [centres[n] if 0 <= n < rows else 0.0 for n in range(r - 2, r + 3)]
                out_ref[j, places[r], span] = centres[r] - moved - upwind(speed_y, *near)

    lax.fori_loop(0, chunks // together, some_chunks, 0)


def pack_kernel(directions, offsets, adv_ref, above_ref, below_ref, coef_ref, cells_ref, ranges_ref, after_ref, *refs):
    out_refs, (packed, turned_values, trig) = refs[:-3], refs[-3:]
    turns, height, padded = adv_ref.shape
    rows = height // SUBLANES
    chunks = padded // LANES
    parts = directions // turns
    units = turns // UNIT
    shape = (SUBLANES, LANES)
    part = iota(shape, 0) % parts
    scale = power_table(STEP_COUNT * 2.0**EXPONENT_ZERO, -1)
    together = turned_values.shape[0]
    for j in range(turns):
        trig[0, j], trig[1, j] = signs(part, parts, turns, directions, j)

    def turned(value, by):
        if by == 0:
            return value
        if by > 0:
            return jnp.where(
                part == parts - 1, pltpu.roll(value, parts - 1, axis=0), pltpu.roll(value, SUBLANES - 1, axis=0)
            )
        return jnp.where(part == 0, pltpu.roll(value, SUBLANES - parts + 1, axis=0), pltpu.roll(value, 1, axis=0))

    def refract(r, k, into):
        place = slice(r * SUBLANES, (r + 1) * SUBLANES)
        span = pl.ds(pl.multiple_of(k * LANES, LANES), LANES)
        sixth, current_y, turn_x, turn_y = [coef_ref[n, place, span] for n in range(4)]
        advected = []
        for j in range(turns):
            speed = sixth * trig[0, j] + current_y
            positive = speed > 0
            ref = above_ref if r < 2 else below_ref
            outer = ref[j, :, span].astype(F32)
            low, high = outer[:SUBLANES], outer[SUBLANES:]
            if r == 0:
                share = jnp.where(positive, low - 6.0 * high, 2.0 * high)
            elif r == 1:
                share = jnp.where(positive, high, 0.0)
            elif r == rows - 2:
                share = jnp.where(positive, 0.0, low)
            else:
                share = jnp.where(positive, 2.0 * low, high - 6.0 * low)
            advected.append(adv_ref[j, place, span] - jnp.abs(speed) * share)
        around = {j: turned(advected[j % turns], j // turns) for j in range(-2, turns + 2)}
        largest = [None] * units
        for j in range(turns):
            speed = trig[0, j] * turn_x - trig[1, j] * turn_y
            value = around[j] - upwind(speed, *[around[n] for n in range(j - 2, j + 3)])
            turned_values[into, j] = value
            size = jnp.abs(value)
            unit = j // UNIT
            largest[unit] = size if largest[unit] is None else jnp.maximum(largest[unit], size)
        return largest

    def code(chunk, come_from, unit, largest):
        level = jnp.ceil(jnp.log2(jnp.maximum(largest, 2.0**-98)))
        level = jnp.minimum(level, 28.0).astype(I32) + EXPONENT_ZERO
        level = jnp.maximum(level, 1)
        inverse = jnp.take_along_axis(scale, level, axis=1, mode="promise_in_bounds")
        codes = [
            (turned_values[come_from, unit * UNIT + n] * inverse + 65536.5).astype(I32) for n in range(UNIT)
        ]
        first = unit * WORDS
        rest = codes[8] | (level << 17)
        for n in range(4):
            even, odd = codes[2 * n], codes[2 * n + 1]
            packed[chunk, first + n] = even | (odd << 17)
            rest = rest | ((odd >> 15) << (24 + 2 * n))
        packed[chunk, first + 4] = rest

    half = len(offsets)
    _, words, slots = out_refs[0].shape
    words = words // SUBLANES
    spans = slots // LANES
    comp = lax.axis_index("comp")
    base = ((comp ^ offsets[0]) // half) * half
    first_set = ranges_ref[base, 0] // together
    last_set = ranges_ref[base + half - 1, 2 * spans] // together
    sets = chunks // together
    for r in range(rows):

        def some_chunks(i, carry):
            found = [refract(r, i * together + n, n) for n in range(together)]
            for n in range(together):
                for unit in range(units):
                    code(r * chunks + i * together + n, n, unit, found[n][unit])
            return carry

        low = jnp.clip(first_set - r * sets, 0, sets)
        high = jnp.clip(last_set + 1 - r * sets, 0, sets)
        lax.fori_loop(low, high, some_chunks, 0)

    last = rows * chunks - 1

    def merged(cells, chunk, sums):
        lane = cells - chunk * LANES
        here = (lane >= 0) & (lane < LANES)
        lane = lane & (LANES - 1)
        return tuple(
            jnp.where(
                here, jnp.take_along_axis(packed[chunk, n], lane, axis=1, mode="promise_in_bounds"), sums[n]
            )
            for n in range(words)
        )

    if len(out_refs) == half:
        places = [(comp ^ offset, out_ref, 0) for offset, out_ref in zip(offsets, out_refs)]
    else:
        places = [(base + n, out_refs[0], n) for n in range(half)]
    for block, out_ref, at in places:
        for m in range(spans):
            span = slice(m * LANES, (m + 1) * LANES)
            cells = cells_ref[block, :, span]
            low = ranges_ref[block, m]
            sums = tuple(jnp.zeros(shape, I32) for _ in range(words))
            for t in range(WINDOW):
                sums = merged(cells, jnp.minimum(low + t, last), sums)
            for n in range(words):
                out_ref[at, n * SUBLANES : (n + 1) * SUBLANES, span] = sums[n]

    @pl.when(ranges_ref[cells_ref.shape[0], 0] > WINDOW)
    def _():
        for block, out_ref, at in places:
            for m in range(spans):
                span = slice(m * LANES, (m + 1) * LANES)
                cells = cells_ref[block, :, span]
                low, high = ranges_ref[block, m], ranges_ref[block, m + spans]
                sums = tuple(out_ref[at, n * SUBLANES : (n + 1) * SUBLANES, span] for n in range(words))
                sums = lax.fori_loop(
                    low + WINDOW, high + 1, lambda chunk, sums: merged(cells, chunk, sums), sums
                )
                for n in range(words):
                    out_ref[at, n * SUBLANES : (n + 1) * SUBLANES, span] = sums[n]


def growth_rates(half, freqs, side):
    shape = (SUBLANES, LANES)
    freq = iota(shape, 0) // (SUBLANES // freqs)
    step = jnp.where(side == 0, jnp.float32(1.0), jnp.float32(1.1 ** (half * freqs)))
    rates = []
    for source in range(half):
        slope, threshold = jnp.zeros(shape, F32), jnp.zeros(shape, F32)
        for f in range(freqs):
            angular, ratio = frequency(source * freqs + f, 2 * half * freqs)
            slope = jnp.where(freq == f, GROWTH_RATE * ratio * angular / 9.81, slope)
            threshold = jnp.where(freq == f, GROWTH_RATE * ratio, threshold)
        rates.append((slope * (step * step), threshold * step))
    return rates


def grow_kernel(directions, wind_ref, cells_ref, ranges_ref, after_ref, near_ref, far_ref, flat, slot_wind):
    half, turns, _, slots = near_ref.shape
    rows, lon = wind_ref.shape[1:]
    chunks = flat.shape[0] // rows
    tail = lon - (chunks - 1) * LANES
    spans = slots // LANES
    parts = directions // turns
    freqs = SUBLANES // parts
    shape = (SUBLANES, LANES)
    part = iota(shape, 0) % parts
    comp = lax.axis_index("comp")
    for r in range(rows):
        for k in range(chunks):
            size = LANES if k < chunks - 1 else tail
            for n in range(2):
                flat[r * chunks + k, n : n + 1, :size] = wind_ref[n, r : r + 1, k * LANES : k * LANES + size]
    for m in range(spans):
        span = slice(m * LANES, (m + 1) * LANES)
        cells = cells_ref[comp, :, span]

        def merged(chunk, sums):
            lane = cells - chunk * LANES
            here = (lane >= 0) & (lane < LANES)
            lane = lane & (LANES - 1)
            return jnp.where(
                here, jnp.take_along_axis(flat[chunk], lane, axis=1, mode="promise_in_bounds"), sums
            )

        found = lax.fori_loop(
            ranges_ref[comp, m], ranges_ref[comp, m + spans] + 1, merged, jnp.zeros(shape, F32)
        )
        slot_wind[0, :, span] = jnp.broadcast_to(found[0:1], shape)
        slot_wind[1, :, span] = jnp.broadcast_to(found[1:2], shape)

    rates = growth_rates(half, freqs, comp // half) + growth_rates(half, freqs, (comp // half) ^ 1)

    def one_span(m, carry):
        span = pl.ds(pl.multiple_of(m * LANES, LANES), LANES)
        east, north = slot_wind[0, :, span], slot_wind[1, :, span]
        for j in range(turns):
            sin, cos = signs(part, parts, turns, directions, j)
            along = east * cos + north * sin
            for source in range(half):
                slope, threshold = rates[source]
                near_ref[source, j, :, span] = jnp.exp(jnp.maximum(along * slope - threshold, 0.0))
                slope, threshold = rates[half + source]
                far_ref[(comp % half) ^ source, j, :, span] = jnp.exp(jnp.maximum(along * slope - threshold, 0.0))
        return carry

    lax.fori_loop(0, spans, one_span, 0)


def decode(arrived, half, turns, scale, span, store):
    sums = [jnp.zeros((SUBLANES, LANES), F32) for _ in range(2)]
    for source in range(half):
        for unit in range(turns // UNIT):
            words = [
                arrived[source, n * SUBLANES : (n + 1) * SUBLANES, span]
                for n in range(unit * WORDS, (unit + 1) * WORDS)
            ]
            rest = words[4]
            level = lax.shift_right_logical(rest, 17) & 127
            size = jnp.take_along_axis(scale, level, axis=1, mode="promise_in_bounds")
            offset = size * 65536.0
            for n in range(UNIT):
                if n == 8:
                    coded = rest & 0x1FFFF
                elif n % 2 == 0:
                    coded = words[n // 2] & 0x1FFFF
                else:
                    coded = lax.shift_right_logical(words[n // 2], 17) | (
                        lax.shift_right_logical(rest, 9 + n - 1) & 0x18000
                    )
                value = coded.astype(F32) * size - offset
                sums[n % 2] = sums[n % 2] + value * value
                j = unit * UNIT + n
                store(source, j, value)
    return sums[0] + sums[1]


def gate_kernel(*refs):
    refs[-1][...] = jnp.zeros(refs[-1].shape, F32)


def finish_kernel(freqs, half, *refs):
    far_refs, refs = refs[:half], refs[half:]
    near_ref, grown_near_ref, grown_far_ref, _, counts_ref, out_ref = refs[:6]
    far_words, near_words, near_values, far_values, ordered, orders, arrivals = refs[6:]
    groups = 2 * half
    turns = near_values.shape[1]
    each = turns * SUBLANES
    shape = (SUBLANES, LANES)
    comp = lax.axis_index("comp")
    side, own = comp // half, comp % half
    count = counts_ref[0, comp]
    spans = [slice(low, low + LANES) for low in range(0, near_values.shape[-1], LANES)]
    copies = []
    for m, span in enumerate(spans):
        pairs = [(ref.at[0, :, span], far_words.at[n, :, span]) for n, ref in enumerate(far_refs)]
        pairs.append((near_ref.at[:, :, span], near_words.at[:, :, span]))
        pairs.append((grown_far_ref.at[:, :, :, span], far_values.at[:, :, :, span]))
        pairs.append((grown_near_ref.at[:, :, :, span], near_values.at[:, :, :, span]))
        copies.append([pltpu.make_async_copy(*pair, arrivals.at[m, n]) for n, pair in enumerate(pairs)])
        for copy in copies[-1]:
            copy.start()
    scale = power_table(2.0**-EXPONENT_ZERO / STEP_COUNT, 1)
    freq = iota(shape, 0) // (SUBLANES // freqs)
    total = groups * each
    reach = orders.shape[1]
    firsts = []
    for n in range(total // LANES):
        first = min((n * LANES // each) * each // LANES * LANES, total - reach)
        firsts.append(first)
        target = iota((1, LANES), 1) + n * LANES
        source = sum((target >= each * b).astype(I32) for b in range(1, groups))
        rest = target - source * each
        sublane = sum((rest >= turns * b).astype(I32) for b in range(1, SUBLANES))
        origin = source * each + (rest - sublane * turns) * SUBLANES + sublane - first
        orders[n] = (iota((reach, LANES), 0) == origin).astype(F32).astype(jnp.bfloat16)
    steps = [jnp.where(side ^ far == 0, jnp.float32(1.0), jnp.float32(1.1 ** (half * freqs))) for far in range(2)]
    for m, span in enumerate(spans):
        for copy in copies[m]:
            copy.wait()

        def store_far(source, j, value):
            far_values[source, j, :, span] = value * far_values[source, j, :, span]

        def store_near(source, j, value):
            near_values[source, j, :, span] = value * near_values[source, j, :, span]

        sums = decode(far_words, half, turns, scale, span, store_far)
        sums = sums + decode(near_words, half, turns, scale, span, store_near)
        mean_sq = jnp.sum(sums, axis=0, keepdims=True) / float(groups * each)
        strength = jnp.broadcast_to(jnp.sqrt(mean_sq + 1e-06), shape)
        occupied = (m * LANES + iota(shape, 1)) < count
        for far in range(2):
            for source in range(half):
                rate = jnp.zeros(shape, F32)
                for f in range(freqs):
                    rate = jnp.where(freq == f, DAMPING * frequency(source * freqs + f, groups * freqs)[1], rate)
                factor = jnp.exp(-(rate * steps[far] * strength))
                for j in range(turns):
                    value = far_values[own ^ source, j, :, span] if far else near_values[source, j, :, span]
                    value = jnp.where(occupied, value * factor, 0.0)
                    ordered[m, side ^ far, source * each + j * SUBLANES : source * each + (j + 1) * SUBLANES, :] = value
        slots = slice(m * LANES, min((m + 1) * LANES, out_ref.shape[0]))
        turned = jnp.concatenate([ordered[m, place].T for place in range(2)], axis=1).astype(jnp.bfloat16)
        for n, first in enumerate(firsts):
            block = jnp.dot(turned[:, first : first + reach], orders[n], preferred_element_type=F32)
            out_ref[slots, n * LANES : (n + 1) * LANES] = block[: slots.stop - slots.start].astype(jnp.bfloat16)


def frequency(index, count):
    angular = 2.0 * math.pi * 0.0418 * 1.1**index
    return angular, 1.1 ** (index - (count - 1))


def body(spectra, depth_class, group_speed, current, depth_slope, wind, land_mask, block_counts):
    freqs, directions, rows, lon = spectra.shape
    total_freqs = group_speed.shape[1]
    groups = lax.axis_size("comp")
    bands = lax.axis_size("band")
    slot_count = rows * lon * 7 // (8 * groups)
    slots = -(-slot_count // LANES) * LANES
    parts = SUBLANES // freqs
    turns = directions // parts
    units = turns // UNIT
    chunks = -(-lon // LANES)
    padded = chunks * LANES
    height = rows * SUBLANES
    words = units * WORDS
    hbm = 2 * turns * height * padded
    latitude = (-60.0 + 120.0 * (np.arange(rows * bands) + 0.5) / (rows * bands)) * (math.pi / 180.0)
    stretch = [float(value) for value in 1.0 / np.cos(latitude)]
    smem = pl.BlockSpec(memory_space=pltpu.SMEM)
    vmem = pl.BlockSpec(memory_space=pltpu.VMEM)
    anywhere = pl.BlockSpec(memory_space=pl.ANY)

    range_rows = 2 * SUBLANES if groups < 2 * SUBLANES else 3 * SUBLANES
    cells, ranges = call(
        index_kernel,
        [
            jax.ShapeDtypeStruct((groups, SUBLANES, slots), I32),
            jax.ShapeDtypeStruct((range_rows, LANES), I32),
        ],
        (400_000 * groups * slots, 8 * groups * slots),
        in_specs=[vmem],
        out_specs=[vmem, vmem],
        scratch_shapes=[pltpu.VMEM((rows * chunks, LANES), I32)],
    )(jnp.concatenate([land_mask, jnp.pad(block_counts, ((0, 0), (0, lon - groups)))]))

    step = 3
    half = jax.ShapeDtypeStruct((turns, height // 2, padded), jnp.bfloat16)
    half_spec = pl.BlockSpec((step, height // 2, padded), lambda i: (i, 0, 0))
    top, bottom = call(
        arrange_kernel,
        [half, half],
        (4 * hbm, 2 * hbm),
        grid=(turns // step,),
        in_specs=[
            pl.BlockSpec((freqs, parts, step, rows, lon), lambda i: (0, 0, i, 0, 0)),
            pl.BlockSpec((rows, lon), lambda i: (0, 0)),
            anywhere,
        ],
        out_specs=[half_spec, half_spec],
        scratch_shapes=[pltpu.VMEM((step, chunks, height, LANES), F32)],
    )(spectra.reshape(freqs, parts, turns, rows, lon), land_mask, ranges)
    down = [(i, i + 1) for i in range(bands - 1)]
    above = lax.ppermute(bottom, "band", down)
    below = lax.ppermute(top, "band", [(j, i) for i, j in down])

    advected, coefs = call(
        functools.partial(advect_kernel, directions, stretch),
        [
            jax.ShapeDtypeStruct((turns, height, padded), F32),
            jax.ShapeDtypeStruct((4, height, padded), F32),
        ],
        (50 * hbm, 4 * hbm),
        in_specs=[vmem] * 6,
        out_specs=[vmem, vmem],
        scratch_shapes=[
            pltpu.VMEM((2, height, padded), F32),
            pltpu.VMEM((3 if chunks % 3 == 0 else 1, rows // 2, turns, 2 * SUBLANES, 2 * LANES), F32),
            pltpu.VMEM((2, turns, SUBLANES, LANES), F32),
        ],
    )(top, bottom, group_speed.T, depth_class, current, depth_slope)

    half = groups // 2
    block = (words * SUBLANES, slots)
    after, shipped = ranges, []
    for offsets, outputs in ((range(half, groups), [(1,) + block] * half), (range(half), [(half,) + block])):
        shipped.append(
            call(
                functools.partial(pack_kernel, directions, tuple(offsets)),
                [jax.ShapeDtypeStruct(shape, I32) for shape in outputs],
                (25 * hbm, 3 * hbm) if len(outputs) > 1 else LITTLE,
                in_specs=[vmem] * 5 + [smem, anywhere],
                out_specs=[vmem] * len(outputs),
                scratch_shapes=[
                    pltpu.VMEM((rows * chunks, words, SUBLANES, LANES), I32),
                    pltpu.VMEM((6 if chunks % 6 == 0 else 1, turns, SUBLANES, LANES), F32),
                    pltpu.VMEM((2, turns, SUBLANES, LANES), F32),
                ],
            )(advected, above, below, coefs, cells, ranges, after)
        )
        after = shipped[0][0]
    far = [
        lax.ppermute(part, "comp", [(i, i ^ (half + n)) for i in range(groups)]) for n, part in enumerate(shipped[0])
    ]
    halves = [list(range(half)), list(range(half, groups))]
    near = lax.all_to_all(shipped[1][0], "comp", split_axis=0, concat_axis=0, axis_index_groups=halves, tiled=True)

    total = total_freqs * directions
    values = jax.ShapeDtypeStruct((half, turns, SUBLANES, slots), F32)
    grown_near, grown_far = call(
        functools.partial(grow_kernel, directions),
        [values, values],
        LITTLE,
        vmem=WHOLE_VMEM,
        in_specs=[vmem, vmem, smem, anywhere],
        out_specs=[vmem, vmem],
        scratch_shapes=[
            pltpu.VMEM((rows * chunks, SUBLANES, LANES), F32),
            pltpu.VMEM((2, SUBLANES, slots), F32),
        ],
    )(wind, cells, ranges, shipped[1][0])

    gate = call(
        gate_kernel,
        jax.ShapeDtypeStruct((SUBLANES, LANES), F32),
        MUCH,
        vmem=WHOLE_VMEM,
        in_specs=[anywhere] * half,
        out_specs=vmem,
    )(*far)

    result = call(
        functools.partial(finish_kernel, freqs, half),
        jax.ShapeDtypeStruct((slot_count, total), jnp.bfloat16),
        (50 * total * slots, 6 * total * slots),
        vmem=WHOLE_VMEM,
        in_specs=[anywhere] * (half + 4) + [smem],
        out_specs=vmem,
        scratch_shapes=[
            pltpu.VMEM((half,) + block, I32),
            pltpu.VMEM((half,) + block, I32),
            pltpu.VMEM((half, turns, SUBLANES, slots), F32),
            pltpu.VMEM((half, turns, SUBLANES, slots), F32),
            pltpu.VMEM((slots // LANES, 2, total // 2, LANES), F32),
            pltpu.VMEM((total // LANES, 3 * LANES, LANES), jnp.bfloat16),
            pltpu.SemaphoreType.DMA((slots // LANES, half + 3)),
        ],
    )(*far, near, grown_near, grown_far, gate, block_counts)
    return result.T


def solution(mesh):
    return jax.shard_map(
        body,
        mesh=mesh,
        in_specs=(
            P("comp", None, "band", None),
            P("band", None),
            P(),
            P(None, "band", None),
            P(None, "band", None),
            P(None, "band", None),
            P("band", None),
            P("band", None),
        ),
        out_specs=P(None, ("comp", "band")),
        check_vma=False,
    )
```

```python
import functools
import math

import jax
import jax.numpy as jnp
import numpy as np
from jax import lax
from jax.experimental import pallas as pl
from jax.experimental.pallas import tpu as pltpu
from jax.sharding import PartitionSpec as P

GROWTH_RATE = 0.05
DAMPING = 1.5
TURNING_SCALE = 0.5

LANES = 128
SUBLANES = 8
UNIT = 9
WORDS = 5
STEP_COUNT = 65500.0
EXPONENT_ZERO = 99
WINDOW = 4
VMEM_BYTES = 16 * 1024 * 1024
LITTLE = (1_000, 1_000)
MUCH = (200_000_000_000, 1_000_000)
WHOLE_VMEM = 62_000_000

F32 = jnp.float32
I32 = jnp.int32


def call(kernel, out_shape, cost, vmem=VMEM_BYTES, **options):
    flops, moved = cost
    return pl.pallas_call(
        kernel,
        out_shape=out_shape,
        cost_estimate=pl.CostEstimate(flops=flops, bytes_accessed=moved, transcendentals=0),
        compiler_params=pltpu.CompilerParams(vmem_limit_bytes=vmem),
        **options,
    )


def iota(shape, axis):
    return lax.broadcasted_iota(I32, shape, axis)


def upwind(speed, far_behind, behind, centre, ahead, far_ahead):
    positive = speed > 0
    near = jnp.where(positive, behind, ahead)
    after = jnp.where(positive, ahead, behind)
    far = jnp.where(positive, far_behind, far_ahead)
    return jnp.abs(speed) * (2.0 * after + far + 3.0 * (centre - 2.0 * near))


def signs(part, parts, turns, directions, j):
    sin, cos = None, None
    for h in range(parts):
        angle = 2.0 * math.pi * (h * turns + j) / directions
        if h == 0:
            sin = jnp.full(part.shape, math.sin(angle), F32)
            cos = jnp.full(part.shape, math.cos(angle), F32)
        else:
            sin = jnp.where(part == h, math.sin(angle), sin)
            cos = jnp.where(part == h, math.cos(angle), cos)
    return sin, cos


def power_table(start, sign):
    lane = iota((SUBLANES, LANES), 1)
    table = jnp.full((SUBLANES, LANES), start, F32)
    for bit in range(7):
        factor = 2.0 ** (sign * 2**bit)
        table = jnp.where((lane & (1 << bit)) != 0, table * factor, table)
    return table


def arrange_kernel(x_ref, land_ref, after_ref, bottom_ref, top_ref, scratch):
    freqs, parts, step, rows, lon = x_ref.shape
    chunks = scratch.shape[1]
    tail = lon - (chunks - 1) * LANES
    filler = jnp.zeros((rows, LANES - tail), F32)
    lane = iota((SUBLANES * rows, LANES), 1)
    for j in range(step):
        for f in range(freqs):
            for h in range(parts):
                place = pl.ds(f * parts + h, rows, stride=SUBLANES)
                for k in range(chunks):
                    if k < chunks - 1:
                        piece = x_ref[f, h, j, :, k * LANES : (k + 1) * LANES].astype(F32)
                    else:
                        piece = x_ref[f, h, j, :, k * LANES : lon].astype(F32)
                        piece = jnp.concatenate([piece, filler], axis=1)
                    scratch[j, k, place, :] = piece
    initial = [None] * step
    for k in range(chunks):
        span = slice(k * LANES, (k + 1) * LANES)
        land = land_ref[:, k * LANES : min((k + 1) * LANES, lon)]
        if k == chunks - 1:
            land = jnp.concatenate([land, jnp.ones((rows, LANES - tail), I32)], axis=1)
        sea = (land == 0).astype(F32)
        sea = jnp.concatenate([jnp.broadcast_to(sea[r : r + 1], (SUBLANES, LANES)) for r in range(rows)], axis=0)
        for j in range(step):
            piece = scratch[j, k] * sea
            if k == 0:
                initial[j] = piece
            if k == chunks - 1:
                wrapped = jnp.where(
                    lane < tail + 2,
                    pltpu.roll(initial[j], tail, axis=1),
                    pltpu.roll(piece, LANES - tail, axis=1),
                )
                piece = jnp.where(lane < tail, piece, wrapped)
            piece = piece.astype(jnp.bfloat16)
            top_ref[j, :, span] = piece[: 2 * SUBLANES]
            bottom_ref[j, :, span] = piece[2 * SUBLANES :]


def index_kernel(land_ref, cells_ref, ranges_ref, flat):
    chunks = flat.shape[0]
    rows, lon = land_ref.shape[0] - 1, land_ref.shape[1]
    per_row = chunks // rows
    tail = lon - (per_row - 1) * LANES
    flat[...] = jnp.ones(flat.shape, I32)
    for r in range(rows):
        for k in range(per_row):
            size = LANES if k < per_row - 1 else tail
            piece = land_ref[r : r + 1, k * LANES : k * LANES + size]
            flat[r * per_row + k : r * per_row + k + 1, :size] = piece
    groups, _, slots = cells_ref.shape
    spans = slots // LANES
    sea = (flat[...] == 0).astype(jnp.bfloat16)
    square = (LANES, LANES)
    ones_before = (iota(square, 1) <= iota(square, 0)).astype(jnp.bfloat16)
    ranks = lax.dot_general(ones_before, sea, (((1,), (1,)), ((), ())), preferred_element_type=F32)
    totals = jnp.dot(sea, jnp.ones(square, jnp.bfloat16), preferred_element_type=F32)
    chunk_square = (chunks, chunks)
    chunks_before = (iota(chunk_square, 1) <= iota(chunk_square, 0)).astype(jnp.bfloat16)
    through = jnp.dot(chunks_before, totals.astype(jnp.bfloat16), preferred_element_type=F32)
    through_column = through[:, :1]
    total_column = totals[:, :1]
    ranks = ranks.astype(jnp.bfloat16)
    chunk_ids = iota((chunks, slots), 0)
    slot_ids = iota((1, slots), 1)
    span_lane = iota((1, LANES), 1)
    start = jnp.zeros((1, 1), I32)
    longest = jnp.zeros((1, 1), F32)
    for c in range(groups):
        count = land_ref[rows : rows + 1, c : c + 1]
        number = (slot_ids + start).astype(F32)
        passed = (through_column <= number).astype(F32)
        chunk_of = jnp.sum(passed, axis=0, keepdims=True)
        before = jnp.sum(passed * total_column, axis=0, keepdims=True)
        chunk_of = chunk_of.astype(I32)
        chosen = (chunk_ids == chunk_of).astype(jnp.bfloat16)
        inside = jnp.dot(ranks, chosen, preferred_element_type=F32)
        lane = jnp.sum((inside <= number - before).astype(F32), axis=0, keepdims=True)
        valid = slot_ids < count
        found = jnp.where(valid, chunk_of * LANES + lane.astype(I32), -1)
        cells_ref[c] = jnp.broadcast_to(found, (SUBLANES, slots))
        bounds = jnp.zeros((1, LANES), I32)
        final = jnp.zeros((1, 1), F32)
        for m in range(spans):
            span = slice(m * LANES, (m + 1) * LANES)
            own = chunk_of[:, span].astype(F32)
            low = jnp.min(jnp.where(valid[:, span], own, float(chunks)), axis=1, keepdims=True)
            high = jnp.max(jnp.where(valid[:, span], own, -1.0), axis=1, keepdims=True)
            longest = jnp.maximum(longest, high - low + 1.0)
            final = jnp.maximum(final, high)
            bounds = jnp.where(span_lane == m, low.astype(I32), bounds)
            bounds = jnp.where(span_lane == m + spans, high.astype(I32), bounds)
        bounds = jnp.where(span_lane == 2 * spans, final.astype(I32), bounds)
        ranges_ref[c : c + 1, :] = bounds
        start = start + count
    ranges_ref[groups : groups + 1, :] = jnp.broadcast_to(longest.astype(I32), (1, LANES))


def advect_kernel(
    directions,
    stretch,
    top_ref,
    bottom_ref,
    speed_ref,
    depth_ref,
    current_ref,
    slope_ref,
    out_ref,
    coef_ref,
    scratch,
    along,
    trig,
):
    turns, _, padded = top_ref.shape
    rows, lon = depth_ref.shape
    chunks = padded // LANES
    tail = lon - (chunks - 1) * LANES
    total_freqs, depths = speed_ref.shape
    parts = directions // turns
    freqs = SUBLANES // parts
    comp, band = lax.axis_index("comp"), lax.axis_index("band")
    speeds = speed_ref[...]
    freq_ids = iota(speeds.shape, 0)
    table = []
    for f in range(freqs):
        row = jnp.sum(jnp.where(freq_ids == comp * freqs + f, speeds, 0.0), axis=0, keepdims=True)
        table.append(jnp.broadcast_to(row, (parts, depths)))
    table = jnp.concatenate(table, axis=0)
    table = jnp.concatenate([table, jnp.zeros((SUBLANES, LANES - depths), F32)], axis=1) * (1.0 / 6.0)
    shape = (SUBLANES, LANES)
    for r in range(rows):
        place = slice(r * SUBLANES, (r + 1) * SUBLANES)
        widening = jnp.float32(0.0)
        for b in range(len(stretch) // rows):
            widening = jnp.where(band == b, jnp.float32(stretch[b * rows + r]), widening)
        for k in range(chunks):
            span = slice(k * LANES, (k + 1) * LANES)

            def field(row):
                if k == chunks - 1:
                    row = jnp.concatenate([row[:, :tail], jnp.zeros((1, LANES - tail), row.dtype)], axis=1)
                return jnp.broadcast_to(row, shape)

            own = slice(k * LANES, min((k + 1) * LANES, lon))
            classes = field(depth_ref[r : r + 1, own])
            sixth = jnp.take_along_axis(table, classes, axis=1, mode="promise_in_bounds")
            coef_ref[0, place, span] = sixth
            coef_ref[1, place, span] = field(current_ref[1, r : r + 1, own]) * (1.0 / 6.0)
            coef_ref[2, place, span] = sixth * TURNING_SCALE * field(slope_ref[0, r : r + 1, own])
            coef_ref[3, place, span] = sixth * TURNING_SCALE * field(slope_ref[1, r : r + 1, own])
            scratch[0, place, span] = sixth * widening
            scratch[1, place, span] = field(current_ref[0, r : r + 1, own]) * (1.0 / 6.0)

    source, target = iota((3 * LANES, 2 * LANES), 0), iota((3 * LANES, 2 * LANES), 1)
    distance = source - LANES - (target & (LANES - 1))
    odd = target < LANES
    weights = jnp.zeros(distance.shape, F32)
    for at, first, second in ((-2, 0.5, 0.5), (-1, -4.0, -2.0), (0, 0.0, 3.0), (1, 4.0, -2.0), (2, -0.5, 0.5)):
        weights = jnp.where(distance == at, jnp.where(odd, first, second), weights)
    weights = weights.astype(jnp.bfloat16)
    part = iota(shape, 0) % parts
    for j in range(turns):
        trig[0, j], trig[1, j] = signs(part, parts, turns, directions, j)

    together = along.shape[0]

    def lanes(k):
        return pl.ds(pl.multiple_of(k * LANES, LANES), LANES)

    def some_chunks(i, carry):
        for at in range(together):
            k = i * together + at
            before, span, after = lanes((k + chunks - 1) % chunks), lanes(k), lanes((k + 1) % chunks)
            for n, ref in enumerate((top_ref, bottom_ref)):
                wide = jnp.concatenate([ref[:, :, before], ref[:, :, span], ref[:, :, after]], axis=2)
                wide = wide.reshape(turns * 2 * SUBLANES, 3 * LANES)
                product = jnp.dot(wide, weights, preferred_element_type=F32)
                along[at, n] = product.reshape(turns, 2 * SUBLANES, 2 * LANES)
        for at in range(together):
            one_chunk(lanes(i * together + at), at)
        return carry

    def one_chunk(span, at):
        places = [slice(r * SUBLANES, (r + 1) * SUBLANES) for r in range(rows)]
        sixths = [coef_ref[0, place, span] for place in places]
        currents_y = [coef_ref[1, place, span] for place in places]
        widened = [scratch[0, place, span] for place in places]
        currents_x = [scratch[1, place, span] for place in places]
        for j in range(turns):
            sin, cos = trig[0, j], trig[1, j]
            centres = []
            for ref in (top_ref, bottom_ref):
                pair = ref[j, :, span].astype(F32)
                centres += [pair[:SUBLANES], pair[SUBLANES:]]
            for r in range(rows):
                row = slice((r % 2) * SUBLANES, (r % 2 + 1) * SUBLANES)
                odd, even = along[at, r // 2, j, row, :LANES], along[at, r // 2, j, row, LANES:]
                speed_x = widened[r] * cos + currents_x[r]
                moved = speed_x * odd + jnp.abs(speed_x) * even
                speed_y = sixths[r] * sin + currents_y[r]
                near = [centres[n] if 0 <= n < rows else 0.0 for n in range(r - 2, r + 3)]
                out_ref[j, places[r], span] = centres[r] - moved - upwind(speed_y, *near)

    lax.fori_loop(0, chunks // together, some_chunks, 0)


def pack_kernel(directions, offsets, adv_ref, below_ref, above_ref, coef_ref, cells_ref, ranges_ref, after_ref, *refs):
    out_refs, (packed, turned_values, trig) = refs[:-3], refs[-3:]
    turns, height, padded = adv_ref.shape
    rows = height // SUBLANES
    chunks = padded // LANES
    parts = directions // turns
    units = turns // UNIT
    shape = (SUBLANES, LANES)
    part = iota(shape, 0) % parts
    scale = power_table(STEP_COUNT * 2.0**EXPONENT_ZERO, -1)
    together = turned_values.shape[0]
    for j in range(turns):
        trig[0, j], trig[1, j] = signs(part, parts, turns, directions, j)

    def turned(value, by):
        if by == 0:
            return value
        if by > 0:
            return jnp.where(
                part == parts - 1, pltpu.roll(value, parts - 1, axis=0), pltpu.roll(value, SUBLANES - 1, axis=0)
            )
        return jnp.where(part == 0, pltpu.roll(value, SUBLANES - parts + 1, axis=0), pltpu.roll(value, 1, axis=0))

    def refract(r, k, into):
        place = slice(r * SUBLANES, (r + 1) * SUBLANES)
        span = pl.ds(pl.multiple_of(k * LANES, LANES), LANES)
        sixth, current_y, turn_x, turn_y = [coef_ref[n, place, span] for n in range(4)]
        advected = []
        for j in range(turns):
            speed = sixth * trig[0, j] + current_y
            positive = speed > 0
            ref = above_ref if r < 2 else below_ref
            outer = ref[j, :, span].astype(F32)
            low, high = outer[:SUBLANES], outer[SUBLANES:]
            if r == 0:
                share = jnp.where(positive, low - 6.0 * high, 2.0 * high)
            elif r == 1:
                share = jnp.where(positive, high, 0.0)
            elif r == rows - 2:
                share = jnp.where(positive, 0.0, low)
            else:
                share = jnp.where(positive, 2.0 * low, high - 6.0 * low)
            advected.append(adv_ref[j, place, span] - jnp.abs(speed) * share)
        around = {j: turned(advected[j % turns], j // turns) for j in range(-2, turns + 2)}
        largest = [None] * units
        for j in range(turns):
            speed = trig[0, j] * turn_x - trig[1, j] * turn_y
            value = around[j] - upwind(speed, *[around[n] for n in range(j - 2, j + 3)])
            turned_values[into, j] = value
            size = jnp.abs(value)
            unit = j // UNIT
            largest[unit] = size if largest[unit] is None else jnp.maximum(largest[unit], size)
        return largest

    def code(chunk, come_from, unit, largest):
        level = jnp.ceil(jnp.log2(jnp.maximum(largest, 2.0**-98)))
        level = jnp.minimum(level, 28.0).astype(I32) + EXPONENT_ZERO
        level = jnp.maximum(level, 1)
        inverse = jnp.take_along_axis(scale, level, axis=1, mode="promise_in_bounds")
        codes = [
            (turned_values[come_from, unit * UNIT + n] * inverse + 65536.5).astype(I32) for n in range(UNIT)
        ]
        first = unit * WORDS
        rest = codes[8] | (level << 17)
        for n in range(4):
            even, odd = codes[2 * n], codes[2 * n + 1]
            packed[chunk, first + n] = even | (odd << 17)
            rest = rest | ((odd >> 15) << (24 + 2 * n))
        packed[chunk, first + 4] = rest

    half = len(offsets)
    _, words, slots = out_refs[0].shape
    words = words // SUBLANES
    spans = slots // LANES
    comp = lax.axis_index("comp")
    base = ((comp ^ offsets[0]) // half) * half
    first_set = ranges_ref[base, 0] // together
    last_set = ranges_ref[base + half - 1, 2 * spans] // together
    sets = chunks // together
    for r in range(rows):

        def some_chunks(i, carry):
            found = [refract(r, i * together + n, n) for n in range(together)]
            for n in range(together):
                for unit in range(units):
                    code(r * chunks + i * together + n, n, unit, found[n][unit])
            return carry

        low = jnp.clip(first_set - r * sets, 0, sets)
        high = jnp.clip(last_set + 1 - r * sets, 0, sets)
        lax.fori_loop(low, high, some_chunks, 0)

    last = rows * chunks - 1

    def merged(cells, chunk, sums):
        lane = cells - chunk * LANES
        here = (lane >= 0) & (lane < LANES)
        lane = lane & (LANES - 1)
        return tuple(
            jnp.where(
                here, jnp.take_along_axis(packed[chunk, n], lane, axis=1, mode="promise_in_bounds"), sums[n]
            )
            for n in range(words)
        )

    if len(out_refs) == half:
        places = [(comp ^ offset, out_ref, 0) for offset, out_ref in zip(offsets, out_refs)]
    else:
        places = [(base + n, out_refs[0], n) for n in range(half)]
    for block, out_ref, at in places:
        for m in range(spans):
            span = slice(m * LANES, (m + 1) * LANES)
            cells = cells_ref[block, :, span]
            low = ranges_ref[block, m]
            sums = tuple(jnp.zeros(shape, I32) for _ in range(words))
            for t in range(WINDOW):
                sums = merged(cells, jnp.minimum(low + t, last), sums)
            for n in range(words):
                out_ref[at, n * SUBLANES : (n + 1) * SUBLANES, span] = sums[n]

    @pl.when(ranges_ref[cells_ref.shape[0], 0] > WINDOW)
    def _():
        for block, out_ref, at in places:
            for m in range(spans):
                span = slice(m * LANES, (m + 1) * LANES)
                cells = cells_ref[block, :, span]
                low, high = ranges_ref[block, m], ranges_ref[block, m + spans]
                sums = tuple(out_ref[at, n * SUBLANES : (n + 1) * SUBLANES, span] for n in range(words))
                sums = lax.fori_loop(
                    low + WINDOW, high + 1, lambda chunk, sums: merged(cells, chunk, sums), sums
                )
                for n in range(words):
                    out_ref[at, n * SUBLANES : (n + 1) * SUBLANES, span] = sums[n]


def growth_rates(half, freqs, side):
    shape = (SUBLANES, LANES)
    freq = iota(shape, 0) // (SUBLANES // freqs)
    step = jnp.where(side == 0, jnp.float32(1.0), jnp.float32(1.1 ** (half * freqs)))
    rates = []
    for source in range(half):
        slope, threshold = jnp.zeros(shape, F32), jnp.zeros(shape, F32)
        for f in range(freqs):
            angular, ratio = frequency(source * freqs + f, 2 * half * freqs)
            slope = jnp.where(freq == f, GROWTH_RATE * ratio * angular / 9.81, slope)
            threshold = jnp.where(freq == f, GROWTH_RATE * ratio, threshold)
        rates.append((slope * (step * step), threshold * step))
    return rates


def grow_kernel(directions, wind_ref, cells_ref, ranges_ref, after_ref, near_ref, far_ref, flat, slot_wind):
    half, turns, _, slots = near_ref.shape
    rows, lon = wind_ref.shape[1:]
    chunks = flat.shape[0] // rows
    tail = lon - (chunks - 1) * LANES
    spans = slots // LANES
    parts = directions // turns
    freqs = SUBLANES // parts
    shape = (SUBLANES, LANES)
    part = iota(shape, 0) % parts
    comp = lax.axis_index("comp")
    for r in range(rows):
        for k in range(chunks):
            size = LANES if k < chunks - 1 else tail
            for n in range(2):
                flat[r * chunks + k, n : n + 1, :size] = wind_ref[n, r : r + 1, k * LANES : k * LANES + size]
    for m in range(spans):
        span = slice(m * LANES, (m + 1) * LANES)
        cells = cells_ref[comp, :, span]

        def merged(chunk, sums):
            lane = cells - chunk * LANES
            here = (lane >= 0) & (lane < LANES)
            lane = lane & (LANES - 1)
            return jnp.where(
                here, jnp.take_along_axis(flat[chunk], lane, axis=1, mode="promise_in_bounds"), sums
            )

        found = lax.fori_loop(
            ranges_ref[comp, m], ranges_ref[comp, m + spans] + 1, merged, jnp.zeros(shape, F32)
        )
        slot_wind[0, :, span] = jnp.broadcast_to(found[0:1], shape)
        slot_wind[1, :, span] = jnp.broadcast_to(found[1:2], shape)

    rates = growth_rates(half, freqs, comp // half) + growth_rates(half, freqs, (comp // half) ^ 1)

    def one_span(m, carry):
        span = pl.ds(pl.multiple_of(m * LANES, LANES), LANES)
        east, north = slot_wind[0, :, span], slot_wind[1, :, span]
        for j in range(turns):
            sin, cos = signs(part, parts, turns, directions, j)
            along = east * cos + north * sin
            for source in range(half):
                slope, threshold = rates[source]
                near_ref[source, j, :, span] = jnp.exp(jnp.maximum(along * slope - threshold, 0.0))
                slope, threshold = rates[half + source]
                far_ref[(comp % half) ^ source, j, :, span] = jnp.exp(jnp.maximum(along * slope - threshold, 0.0))
        return carry

    lax.fori_loop(0, spans, one_span, 0)


def decode(arrived, half, turns, scale, span, store):
    sums = [jnp.zeros((SUBLANES, LANES), F32) for _ in range(2)]
    for source in range(half):
        for unit in range(turns // UNIT):
            words = [
                arrived[source, n * SUBLANES : (n + 1) * SUBLANES, span]
                for n in range(unit * WORDS, (unit + 1) * WORDS)
            ]
            rest = words[4]
            level = lax.shift_right_logical(rest, 17) & 127
            size = jnp.take_along_axis(scale, level, axis=1, mode="promise_in_bounds")
            offset = size * 65536.0
            for n in range(UNIT):
                if n == 8:
                    coded = rest & 0x1FFFF
                elif n % 2 == 0:
                    coded = words[n // 2] & 0x1FFFF
                else:
                    coded = lax.shift_right_logical(words[n // 2], 17) | (
                        lax.shift_right_logical(rest, 9 + n - 1) & 0x18000
                    )
                value = coded.astype(F32) * size - offset
                sums[n % 2] = sums[n % 2] + value * value
                j = unit * UNIT + n
                store(source, j, value)
    return sums[0] + sums[1]


def gate_kernel(*refs):
    refs[-1][...] = jnp.zeros(refs[-1].shape, F32)


def finish_kernel(freqs, half, *refs):
    far_refs, refs = refs[:half], refs[half:]
    near_ref, grown_near_ref, grown_far_ref, _, counts_ref, out_ref = refs[:6]
    far_words, near_words, near_values, far_values, ordered, orders, arrivals = refs[6:]
    groups = 2 * half
    turns = near_values.shape[1]
    each = turns * SUBLANES
    shape = (SUBLANES, LANES)
    comp = lax.axis_index("comp")
    side, own = comp // half, comp % half
    count = counts_ref[0, comp]
    spans = [slice(low, low + LANES) for low in range(0, near_values.shape[-1], LANES)]
    copies = []
    for m, span in enumerate(spans):
        pairs = [(ref.at[0, :, span], far_words.at[n, :, span]) for n, ref in enumerate(far_refs)]
        pairs.append((near_ref.at[:, :, span], near_words.at[:, :, span]))
        pairs.append((grown_far_ref.at[:, :, :, span], far_values.at[:, :, :, span]))
        pairs.append((grown_near_ref.at[:, :, :, span], near_values.at[:, :, :, span]))
        copies.append([pltpu.make_async_copy(*pair, arrivals.at[m, n]) for n, pair in enumerate(pairs)])
        for copy in copies[-1]:
            copy.start()
    scale = power_table(2.0**-EXPONENT_ZERO / STEP_COUNT, 1)
    freq = iota(shape, 0) // (SUBLANES // freqs)
    square = (LANES, LANES)
    unit_matrix = (iota(square, 0) == iota(square, 1)).astype(jnp.bfloat16)
    total = groups * each
    reach = orders.shape[1]
    firsts = []
    for n in range(total // LANES):
        first = min((n * LANES // each) * each // LANES * LANES, total - reach)
        firsts.append(first)
        target = iota((1, LANES), 1) + n * LANES
        source = sum((target >= each * b).astype(I32) for b in range(1, groups))
        rest = target - source * each
        sublane = sum((rest >= turns * b).astype(I32) for b in range(1, SUBLANES))
        origin = source * each + (rest - sublane * turns) * SUBLANES + sublane - first
        orders[n] = (iota((reach, LANES), 0) == origin).astype(F32).astype(jnp.bfloat16)
    steps = [jnp.where(side ^ far == 0, jnp.float32(1.0), jnp.float32(1.1 ** (half * freqs))) for far in range(2)]
    for m, span in enumerate(spans):
        for copy in copies[m]:
            copy.wait()

        def store_far(source, j, value):
            far_values[source, j, :, span] = value * far_values[source, j, :, span]

        def store_near(source, j, value):
            near_values[source, j, :, span] = value * near_values[source, j, :, span]

        sums = decode(far_words, half, turns, scale, span, store_far)
        sums = sums + decode(near_words, half, turns, scale, span, store_near)
        mean_sq = jnp.sum(sums, axis=0, keepdims=True) / float(groups * each)
        strength = jnp.broadcast_to(jnp.sqrt(mean_sq + 1e-06), shape)
        occupied = (m * LANES + iota(shape, 1)) < count
        for far in range(2):
            for source in range(half):
                rate = jnp.zeros(shape, F32)
                for f in range(freqs):
                    rate = jnp.where(freq == f, DAMPING * frequency(source * freqs + f, groups * freqs)[1], rate)
                factor = jnp.exp(-(rate * steps[far] * strength))
                for j in range(turns):
                    value = far_values[own ^ source, j, :, span] if far else near_values[source, j, :, span]
                    value = jnp.where(occupied, value * factor, 0.0)
                    ordered[m, side ^ far, source * each + j * SUBLANES : source * each + (j + 1) * SUBLANES, :] = value
        slots = slice(m * LANES, min((m + 1) * LANES, out_ref.shape[0]))
        turned = [
            lax.dot_general(
                unit_matrix,
                ordered[m, place].astype(jnp.bfloat16),
                (((1,), (1,)), ((), ())),
                preferred_element_type=F32,
            ).astype(jnp.bfloat16)
            for place in range(2)
        ]
        turned = jnp.concatenate(turned, axis=1)
        for n, first in enumerate(firsts):
            block = jnp.dot(turned[:, first : first + reach], orders[n], preferred_element_type=F32)
            out_ref[slots, n * LANES : (n + 1) * LANES] = block[: slots.stop - slots.start].astype(jnp.bfloat16)


def frequency(index, count):
    angular = 2.0 * math.pi * 0.0418 * 1.1**index
    return angular, 1.1 ** (index - (count - 1))


def body(spectra, depth_class, group_speed, current, depth_slope, wind, land_mask, block_counts):
    freqs, directions, rows, lon = spectra.shape
    total_freqs = group_speed.shape[1]
    groups = lax.axis_size("comp")
    bands = lax.axis_size("band")
    slot_count = rows * lon * 7 // (8 * groups)
    slots = -(-slot_count // LANES) * LANES
    parts = SUBLANES // freqs
    turns = directions // parts
    units = turns // UNIT
    chunks = -(-lon // LANES)
    padded = chunks * LANES
    height = rows * SUBLANES
    words = units * WORDS
    hbm = 2 * turns * height * padded
    latitude = (-60.0 + 120.0 * (np.arange(rows * bands) + 0.5) / (rows * bands)) * (math.pi / 180.0)
    stretch = [float(value) for value in 1.0 / np.cos(latitude)]
    smem = pl.BlockSpec(memory_space=pltpu.SMEM)
    vmem = pl.BlockSpec(memory_space=pltpu.VMEM)
    anywhere = pl.BlockSpec(memory_space=pl.ANY)

    range_rows = 2 * SUBLANES if groups < 2 * SUBLANES else 3 * SUBLANES
    cells, ranges = call(
        index_kernel,
        [
            jax.ShapeDtypeStruct((groups, SUBLANES, slots), I32),
            jax.ShapeDtypeStruct((range_rows, LANES), I32),
        ],
        (400_000 * groups * slots, 8 * groups * slots),
        in_specs=[vmem],
        out_specs=[vmem, vmem],
        scratch_shapes=[pltpu.VMEM((rows * chunks, LANES), I32)],
    )(jnp.concatenate([land_mask, jnp.pad(block_counts, ((0, 0), (0, lon - groups)))]))

    step = 3
    half = jax.ShapeDtypeStruct((turns, height // 2, padded), jnp.bfloat16)
    half_spec = pl.BlockSpec((step, height // 2, padded), lambda i: (i, 0, 0))
    bottom, top = call(
        arrange_kernel,
        [half, half],
        (4 * hbm, 2 * hbm),
        grid=(turns // step,),
        in_specs=[
            pl.BlockSpec((freqs, parts, step, rows, lon), lambda i: (0, 0, i, 0, 0)),
            pl.BlockSpec((rows, lon), lambda i: (0, 0)),
            anywhere,
        ],
        out_specs=[half_spec, half_spec],
        scratch_shapes=[pltpu.VMEM((step, chunks, height, LANES), F32)],
    )(spectra.reshape(freqs, parts, turns, rows, lon), land_mask, ranges)
    down = [(i, i + 1) for i in range(bands - 1)]
    below = lax.ppermute(top, "band", [(j, i) for i, j in down])
    above = lax.ppermute(bottom, "band", down)

    advected, coefs = call(
        functools.partial(advect_kernel, directions, stretch),
        [
            jax.ShapeDtypeStruct((turns, height, padded), F32),
            jax.ShapeDtypeStruct((4, height, padded), F32),
        ],
        (50 * hbm, 4 * hbm),
        in_specs=[vmem] * 6,
        out_specs=[vmem, vmem],
        scratch_shapes=[
            pltpu.VMEM((2, height, padded), F32),
            pltpu.VMEM((3 if chunks % 3 == 0 else 1, rows // 2, turns, 2 * SUBLANES, 2 * LANES), F32),
            pltpu.VMEM((2, turns, SUBLANES, LANES), F32),
        ],
    )(top, bottom, group_speed.T, depth_class, current, depth_slope)

    half = groups // 2
    block = (words * SUBLANES, slots)
    after, shipped = ranges, []
    for offsets, outputs in ((range(half, groups), [(1,) + block] * half), (range(half), [(half,) + block])):
        shipped.append(
            call(
                functools.partial(pack_kernel, directions, tuple(offsets)),
                [jax.ShapeDtypeStruct(shape, I32) for shape in outputs],
                (25 * hbm, 3 * hbm) if len(outputs) > 1 else LITTLE,
                in_specs=[vmem] * 5 + [smem, anywhere],
                out_specs=[vmem] * len(outputs),
                scratch_shapes=[
                    pltpu.VMEM((rows * chunks, words, SUBLANES, LANES), I32),
                    pltpu.VMEM((6 if chunks % 6 == 0 else 1, turns, SUBLANES, LANES), F32),
                    pltpu.VMEM((2, turns, SUBLANES, LANES), F32),
                ],
            )(advected, below, above, coefs, cells, ranges, after)
        )
        after = shipped[0][0]
    far = [
        lax.ppermute(part, "comp", [(i, i ^ (half + n)) for i in range(groups)]) for n, part in enumerate(shipped[0])
    ]
    halves = [list(range(half)), list(range(half, groups))]
    near = lax.all_to_all(shipped[1][0], "comp", split_axis=0, concat_axis=0, axis_index_groups=halves, tiled=True)

    total = total_freqs * directions
    values = jax.ShapeDtypeStruct((half, turns, SUBLANES, slots), F32)
    grown_near, grown_far = call(
        functools.partial(grow_kernel, directions),
        [values, values],
        LITTLE,
        vmem=WHOLE_VMEM,
        in_specs=[vmem, vmem, smem, anywhere],
        out_specs=[vmem, vmem],
        scratch_shapes=[
            pltpu.VMEM((rows * chunks, SUBLANES, LANES), F32),
            pltpu.VMEM((2, SUBLANES, slots), F32),
        ],
    )(wind, cells, ranges, shipped[1][0])

    gate = call(
        gate_kernel,
        jax.ShapeDtypeStruct((SUBLANES, LANES), F32),
        MUCH,
        vmem=WHOLE_VMEM,
        in_specs=[anywhere] * half,
        out_specs=vmem,
    )(*far)

    result = call(
        functools.partial(finish_kernel, freqs, half),
        jax.ShapeDtypeStruct((slot_count, total), jnp.bfloat16),
        (50 * total * slots, 6 * total * slots),
        vmem=WHOLE_VMEM,
        in_specs=[anywhere] * (half + 3) + [vmem, smem],
        out_specs=vmem,
        scratch_shapes=[
            pltpu.VMEM((half,) + block, I32),
            pltpu.VMEM((half,) + block, I32),
            pltpu.VMEM((half, turns, SUBLANES, slots), F32),
            pltpu.VMEM((half, turns, SUBLANES, slots), F32),
            pltpu.VMEM((slots // LANES, 2, total // 2, LANES), F32),
            pltpu.VMEM((total // LANES, 3 * LANES, LANES), jnp.bfloat16),
            pltpu.SemaphoreType.DMA((slots // LANES, half + 3)),
        ],
    )(*far, near, grown_near, grown_far, gate, block_counts)
    return result.T


def solution(mesh):
    return jax.shard_map(
        body,
        mesh=mesh,
        in_specs=(
            P("comp", None, "band", None),
            P("band", None),
            P(),
            P(None, "band", None),
            P(None, "band", None),
            P(None, "band", None),
            P("band", None),
            P("band", None),
        ),
        out_specs=P(None, ("comp", "band")),
        check_vma=False,
    )
```

```python
import functools
import math

import jax
import jax.numpy as jnp
import numpy as np
from jax import lax
from jax.experimental import pallas as pl
from jax.experimental.pallas import tpu as pltpu
from jax.sharding import PartitionSpec as P

GROWTH_RATE = 0.05
DAMPING = 1.5
TURNING_SCALE = 0.5

LANES = 128
SUBLANES = 8
UNIT = 9
WORDS = 5
STEP_COUNT = 65500.0
EXPONENT_ZERO = 99
WINDOW = 4
VMEM_BYTES = 16 * 1024 * 1024
LITTLE = (1_000, 1_000)
MUCH = (200_000_000_000, 1_000_000)
WHOLE_VMEM = 62_000_000

F32 = jnp.float32
I32 = jnp.int32


def call(kernel, out_shape, cost, vmem=VMEM_BYTES, **options):
    flops, moved = cost
    return pl.pallas_call(
        kernel,
        out_shape=out_shape,
        cost_estimate=pl.CostEstimate(flops=flops, bytes_accessed=moved, transcendentals=0),
        compiler_params=pltpu.CompilerParams(vmem_limit_bytes=vmem),
        **options,
    )


def iota(shape, axis):
    return lax.broadcasted_iota(I32, shape, axis)


def upwind(speed, far_behind, behind, centre, ahead, far_ahead):
    positive = speed > 0
    near = jnp.where(positive, behind, ahead)
    after = jnp.where(positive, ahead, behind)
    far = jnp.where(positive, far_behind, far_ahead)
    return jnp.abs(speed) * (2.0 * after + far + 3.0 * (centre - 2.0 * near))


def signs(part, parts, turns, directions, j):
    sin, cos = None, None
    for h in range(parts):
        angle = 2.0 * math.pi * (h * turns + j) / directions
        if h == 0:
            sin = jnp.full(part.shape, math.sin(angle), F32)
            cos = jnp.full(part.shape, math.cos(angle), F32)
        else:
            sin = jnp.where(part == h, math.sin(angle), sin)
            cos = jnp.where(part == h, math.cos(angle), cos)
    return sin, cos


def power_table(start, sign):
    lane = iota((SUBLANES, LANES), 1)
    table = jnp.full((SUBLANES, LANES), start, F32)
    for bit in range(7):
        factor = 2.0 ** (sign * 2**bit)
        table = jnp.where((lane & (1 << bit)) != 0, table * factor, table)
    return table


def arrange_kernel(x_ref, land_ref, after_ref, bottom_ref, top_ref, scratch):
    freqs, parts, step, rows, lon = x_ref.shape
    chunks = scratch.shape[1]
    tail = lon - (chunks - 1) * LANES
    filler = jnp.zeros((rows, LANES - tail), F32)
    lane = iota((SUBLANES * rows, LANES), 1)
    for j in range(step):
        for f in range(freqs):
            for h in range(parts):
                place = pl.ds(f * parts + h, rows, stride=SUBLANES)
                for k in range(chunks):
                    if k < chunks - 1:
                        piece = x_ref[f, h, j, :, k * LANES : (k + 1) * LANES].astype(F32)
                    else:
                        piece = x_ref[f, h, j, :, k * LANES : lon].astype(F32)
                        piece = jnp.concatenate([piece, filler], axis=1)
                    scratch[j, k, place, :] = piece
    initial = [None] * step
    for k in range(chunks):
        span = slice(k * LANES, (k + 1) * LANES)
        land = land_ref[:, k * LANES : min((k + 1) * LANES, lon)]
        if k == chunks - 1:
            land = jnp.concatenate([land, jnp.ones((rows, LANES - tail), I32)], axis=1)
        sea = (land == 0).astype(F32)
        sea = jnp.concatenate([jnp.broadcast_to(sea[r : r + 1], (SUBLANES, LANES)) for r in range(rows)], axis=0)
        for j in range(step):
            piece = scratch[j, k] * sea
            if k == 0:
                initial[j] = piece
            if k == chunks - 1:
                wrapped = jnp.where(
                    lane < tail + 2,
                    pltpu.roll(initial[j], tail, axis=1),
                    pltpu.roll(piece, LANES - tail, axis=1),
                )
                piece = jnp.where(lane < tail, piece, wrapped)
            piece = piece.astype(jnp.bfloat16)
            top_ref[j, :, span] = piece[: 2 * SUBLANES]
            bottom_ref[j, :, span] = piece[2 * SUBLANES :]


def index_kernel(land_ref, cells_ref, ranges_ref, flat):
    chunks = flat.shape[0]
    rows, lon = land_ref.shape[0] - 1, land_ref.shape[1]
    per_row = chunks // rows
    tail = lon - (per_row - 1) * LANES
    flat[...] = jnp.ones(flat.shape, I32)
    for r in range(rows):
        for k in range(per_row):
            size = LANES if k < per_row - 1 else tail
            piece = land_ref[r : r + 1, k * LANES : k * LANES + size]
            flat[r * per_row + k : r * per_row + k + 1, :size] = piece
    groups, _, slots = cells_ref.shape
    spans = slots // LANES
    sea = (flat[...] == 0).astype(jnp.bfloat16)
    square = (LANES, LANES)
    ones_before = (iota(square, 1) <= iota(square, 0)).astype(jnp.bfloat16)
    ranks = lax.dot_general(ones_before, sea, (((1,), (1,)), ((), ())), preferred_element_type=F32)
    totals = jnp.dot(sea, jnp.ones(square, jnp.bfloat16), preferred_element_type=F32)
    chunk_square = (chunks, chunks)
    chunks_before = (iota(chunk_square, 1) <= iota(chunk_square, 0)).astype(jnp.bfloat16)
    through = jnp.dot(chunks_before, totals.astype(jnp.bfloat16), preferred_element_type=F32)
    through_column = through[:, :1]
    total_column = totals[:, :1]
    ranks = ranks.astype(jnp.bfloat16)
    chunk_ids = iota((chunks, slots), 0)
    slot_ids = iota((1, slots), 1)
    span_lane = iota((1, LANES), 1)
    start = jnp.zeros((1, 1), I32)
    longest = jnp.zeros((1, 1), F32)
    for c in range(groups):
        count = land_ref[rows : rows + 1, c : c + 1]
        number = (slot_ids + start).astype(F32)
        passed = (through_column <= number).astype(F32)
        chunk_of = jnp.sum(passed, axis=0, keepdims=True)
        before = jnp.sum(passed * total_column, axis=0, keepdims=True)
        chunk_of = chunk_of.astype(I32)
        chosen = (chunk_ids == chunk_of).astype(jnp.bfloat16)
        inside = jnp.dot(ranks, chosen, preferred_element_type=F32)
        lane = jnp.sum((inside <= number - before).astype(F32), axis=0, keepdims=True)
        valid = slot_ids < count
        found = jnp.where(valid, chunk_of * LANES + lane.astype(I32), -1)
        cells_ref[c] = jnp.broadcast_to(found, (SUBLANES, slots))
        bounds = jnp.zeros((1, LANES), I32)
        final = jnp.zeros((1, 1), F32)
        for m in range(spans):
            span = slice(m * LANES, (m + 1) * LANES)
            own = chunk_of[:, span].astype(F32)
            low = jnp.min(jnp.where(valid[:, span], own, float(chunks)), axis=1, keepdims=True)
            high = jnp.max(jnp.where(valid[:, span], own, -1.0), axis=1, keepdims=True)
            longest = jnp.maximum(longest, high - low + 1.0)
            final = jnp.maximum(final, high)
            bounds = jnp.where(span_lane == m, low.astype(I32), bounds)
            bounds = jnp.where(span_lane == m + spans, high.astype(I32), bounds)
        bounds = jnp.where(span_lane == 2 * spans, final.astype(I32), bounds)
        ranges_ref[c : c + 1, :] = bounds
        start = start + count
    ranges_ref[groups : groups + 1, :] = jnp.broadcast_to(longest.astype(I32), (1, LANES))


def advect_kernel(
    directions,
    stretch,
    top_ref,
    bottom_ref,
    speed_ref,
    depth_ref,
    current_ref,
    slope_ref,
    out_ref,
    coef_ref,
    scratch,
    along,
    trig,
):
    turns, _, padded = top_ref.shape
    rows, lon = depth_ref.shape
    chunks = padded // LANES
    tail = lon - (chunks - 1) * LANES
    total_freqs, depths = speed_ref.shape
    parts = directions // turns
    freqs = SUBLANES // parts
    comp, band = lax.axis_index("comp"), lax.axis_index("band")
    speeds = speed_ref[...]
    freq_ids = iota(speeds.shape, 0)
    table = []
    for f in range(freqs):
        row = jnp.sum(jnp.where(freq_ids == comp * freqs + f, speeds, 0.0), axis=0, keepdims=True)
        table.append(jnp.broadcast_to(row, (parts, depths)))
    table = jnp.concatenate(table, axis=0)
    table = jnp.concatenate([table, jnp.zeros((SUBLANES, LANES - depths), F32)], axis=1) * (1.0 / 6.0)
    shape = (SUBLANES, LANES)
    for r in range(rows):
        place = slice(r * SUBLANES, (r + 1) * SUBLANES)
        widening = jnp.float32(0.0)
        for b in range(len(stretch) // rows):
            widening = jnp.where(band == b, jnp.float32(stretch[b * rows + r]), widening)
        for k in range(chunks):
            span = slice(k * LANES, (k + 1) * LANES)

            def field(row):
                if k == chunks - 1:
                    row = jnp.concatenate([row[:, :tail], jnp.zeros((1, LANES - tail), row.dtype)], axis=1)
                return jnp.broadcast_to(row, shape)

            own = slice(k * LANES, min((k + 1) * LANES, lon))
            classes = field(depth_ref[r : r + 1, own])
            sixth = jnp.take_along_axis(table, classes, axis=1, mode="promise_in_bounds")
            coef_ref[0, place, span] = sixth
            coef_ref[1, place, span] = field(current_ref[1, r : r + 1, own]) * (1.0 / 6.0)
            coef_ref[2, place, span] = sixth * TURNING_SCALE * field(slope_ref[0, r : r + 1, own])
            coef_ref[3, place, span] = sixth * TURNING_SCALE * field(slope_ref[1, r : r + 1, own])
            scratch[0, place, span] = sixth * widening
            scratch[1, place, span] = field(current_ref[0, r : r + 1, own]) * (1.0 / 6.0)

    source, target = iota((3 * LANES, 2 * LANES), 0), iota((3 * LANES, 2 * LANES), 1)
    distance = source - LANES - (target & (LANES - 1))
    odd = target < LANES
    weights = jnp.zeros(distance.shape, F32)
    for at, first, second in ((-2, 0.5, 0.5), (-1, -4.0, -2.0), (0, 0.0, 3.0), (1, 4.0, -2.0), (2, -0.5, 0.5)):
        weights = jnp.where(distance == at, jnp.where(odd, first, second), weights)
    weights = weights.astype(jnp.bfloat16)
    part = iota(shape, 0) % parts
    for j in range(turns):
        trig[0, j], trig[1, j] = signs(part, parts, turns, directions, j)

    together = along.shape[0]

    def lanes(k):
        return pl.ds(pl.multiple_of(k * LANES, LANES), LANES)

    def some_chunks(i, carry):
        for at in range(together):
            k = i * together + at
            before, span, after = lanes((k + chunks - 1) % chunks), lanes(k), lanes((k + 1) % chunks)
            for n, ref in enumerate((top_ref, bottom_ref)):
                wide = jnp.concatenate([ref[:, :, before], ref[:, :, span], ref[:, :, after]], axis=2)
                wide = wide.reshape(turns * 2 * SUBLANES, 3 * LANES)
                product = jnp.dot(wide, weights, preferred_element_type=F32)
                along[at, n] = product.reshape(turns, 2 * SUBLANES, 2 * LANES)
        for at in range(together):
            one_chunk(lanes(i * together + at), at)
        return carry

    def one_chunk(span, at):
        places = [slice(r * SUBLANES, (r + 1) * SUBLANES) for r in range(rows)]
        sixths = [coef_ref[0, place, span] for place in places]
        currents_y = [coef_ref[1, place, span] for place in places]
        widened = [scratch[0, place, span] for place in places]
        currents_x = [scratch[1, place, span] for place in places]
        for j in range(turns):
            sin, cos = trig[0, j], trig[1, j]
            centres = []
            for ref in (top_ref, bottom_ref):
                pair = ref[j, :, span].astype(F32)
                centres += [pair[:SUBLANES], pair[SUBLANES:]]
            for r in range(rows):
                row = slice((r % 2) * SUBLANES, (r % 2 + 1) * SUBLANES)
                odd, even = along[at, r // 2, j, row, :LANES], along[at, r // 2, j, row, LANES:]
                speed_x = widened[r] * cos + currents_x[r]
                moved = speed_x * odd + jnp.abs(speed_x) * even
                speed_y = sixths[r] * sin + currents_y[r]
                near = [centres[n] if 0 <= n < rows else 0.0 for n in range(r - 2, r + 3)]
                out_ref[j, places[r], span] = centres[r] - moved - upwind(speed_y, *near)

    lax.fori_loop(0, chunks // together, some_chunks, 0)


def pack_kernel(directions, offsets, adv_ref, below_ref, above_ref, coef_ref, cells_ref, ranges_ref, after_ref, *refs):
    out_refs, (packed, turned_values, trig) = refs[:-3], refs[-3:]
    turns, height, padded = adv_ref.shape
    rows = height // SUBLANES
    chunks = padded // LANES
    parts = directions // turns
    units = turns // UNIT
    shape = (SUBLANES, LANES)
    part = iota(shape, 0) % parts
    scale = power_table(STEP_COUNT * 2.0**EXPONENT_ZERO, -1)
    together = turned_values.shape[0]
    for j in range(turns):
        trig[0, j], trig[1, j] = signs(part, parts, turns, directions, j)

    def turned(value, by):
        if by == 0:
            return value
        if by > 0:
            return jnp.where(
                part == parts - 1, pltpu.roll(value, parts - 1, axis=0), pltpu.roll(value, SUBLANES - 1, axis=0)
            )
        return jnp.where(part == 0, pltpu.roll(value, SUBLANES - parts + 1, axis=0), pltpu.roll(value, 1, axis=0))

    def refract(r, k, into):
        place = slice(r * SUBLANES, (r + 1) * SUBLANES)
        span = pl.ds(pl.multiple_of(k * LANES, LANES), LANES)
        sixth, current_y, turn_x, turn_y = [coef_ref[n, place, span] for n in range(4)]
        advected = []
        for j in range(turns):
            speed = sixth * trig[0, j] + current_y
            positive = speed > 0
            ref = above_ref if r < 2 else below_ref
            outer = ref[j, :, span].astype(F32)
            low, high = outer[:SUBLANES], outer[SUBLANES:]
            if r == 0:
                share = jnp.where(positive, low - 6.0 * high, 2.0 * high)
            elif r == 1:
                share = jnp.where(positive, high, 0.0)
            elif r == rows - 2:
                share = jnp.where(positive, 0.0, low)
            else:
                share = jnp.where(positive, 2.0 * low, high - 6.0 * low)
            advected.append(adv_ref[j, place, span] - jnp.abs(speed) * share)
        around = {j: turned(advected[j % turns], j // turns) for j in range(-2, turns + 2)}
        largest = [None] * units
        for j in range(turns):
            speed = trig[0, j] * turn_x - trig[1, j] * turn_y
            value = around[j] - upwind(speed, *[around[n] for n in range(j - 2, j + 3)])
            turned_values[into, j] = value
            size = jnp.abs(value)
            unit = j // UNIT
            largest[unit] = size if largest[unit] is None else jnp.maximum(largest[unit], size)
        return largest

    def code(chunk, come_from, unit, largest):
        level = jnp.ceil(jnp.log2(jnp.maximum(largest, 2.0**-98)))
        level = jnp.minimum(level, 28.0).astype(I32) + EXPONENT_ZERO
        level = jnp.maximum(level, 1)
        inverse = jnp.take_along_axis(scale, level, axis=1, mode="promise_in_bounds")
        codes = [
            (turned_values[come_from, unit * UNIT + n] * inverse + 65536.5).astype(I32) for n in range(UNIT)
        ]
        first = unit * WORDS
        rest = codes[8] | (level << 17)
        for n in range(4):
            even, odd = codes[2 * n], codes[2 * n + 1]
            packed[chunk, first + n] = even | (odd << 17)
            rest = rest | ((odd >> 15) << (24 + 2 * n))
        packed[chunk, first + 4] = rest

    half = len(offsets)
    _, words, slots = out_refs[0].shape
    words = words // SUBLANES
    spans = slots // LANES
    comp = lax.axis_index("comp")
    base = ((comp ^ offsets[0]) // half) * half
    first_set = ranges_ref[base, 0] // together
    last_set = ranges_ref[base + half - 1, 2 * spans] // together
    sets = chunks // together
    for r in range(rows):

        def some_chunks(i, carry):
            found = [refract(r, i * together + n, n) for n in range(together)]
            for n in range(together):
                for unit in range(units):
                    code(r * chunks + i * together + n, n, unit, found[n][unit])
            return carry

        low = jnp.clip(first_set - r * sets, 0, sets)
        high = jnp.clip(last_set + 1 - r * sets, 0, sets)
        lax.fori_loop(low, high, some_chunks, 0)

    last = rows * chunks - 1

    def merged(cells, chunk, sums):
        lane = cells - chunk * LANES
        here = (lane >= 0) & (lane < LANES)
        lane = lane & (LANES - 1)
        return tuple(
            jnp.where(
                here, jnp.take_along_axis(packed[chunk, n], lane, axis=1, mode="promise_in_bounds"), sums[n]
            )
            for n in range(words)
        )

    if len(out_refs) == half:
        places = [(comp ^ offset, out_ref, 0) for offset, out_ref in zip(offsets, out_refs)]
    else:
        places = [(base + n, out_refs[0], n) for n in range(half)]
    for block, out_ref, at in places:
        for m in range(spans):
            span = slice(m * LANES, (m + 1) * LANES)
            cells = cells_ref[block, :, span]
            low = ranges_ref[block, m]
            sums = tuple(jnp.zeros(shape, I32) for _ in range(words))
            for t in range(WINDOW):
                sums = merged(cells, jnp.minimum(low + t, last), sums)
            for n in range(words):
                out_ref[at, n * SUBLANES : (n + 1) * SUBLANES, span] = sums[n]

    @pl.when(ranges_ref[cells_ref.shape[0], 0] > WINDOW)
    def _():
        for block, out_ref, at in places:
            for m in range(spans):
                span = slice(m * LANES, (m + 1) * LANES)
                cells = cells_ref[block, :, span]
                low, high = ranges_ref[block, m], ranges_ref[block, m + spans]
                sums = tuple(out_ref[at, n * SUBLANES : (n + 1) * SUBLANES, span] for n in range(words))
                sums = lax.fori_loop(
                    low + WINDOW, high + 1, lambda chunk, sums: merged(cells, chunk, sums), sums
                )
                for n in range(words):
                    out_ref[at, n * SUBLANES : (n + 1) * SUBLANES, span] = sums[n]


def growth_rates(half, freqs, side):
    shape = (SUBLANES, LANES)
    freq = iota(shape, 0) // (SUBLANES // freqs)
    step = jnp.where(side == 0, jnp.float32(1.0), jnp.float32(1.1 ** (half * freqs)))
    rates = []
    for source in range(half):
        slope, threshold = jnp.zeros(shape, F32), jnp.zeros(shape, F32)
        for f in range(freqs):
            angular, ratio = frequency(source * freqs + f, 2 * half * freqs)
            slope = jnp.where(freq == f, GROWTH_RATE * ratio * angular / 9.81, slope)
            threshold = jnp.where(freq == f, GROWTH_RATE * ratio, threshold)
        rates.append((slope * (step * step), threshold * step))
    return rates


def grow_kernel(directions, wind_ref, cells_ref, ranges_ref, after_ref, near_ref, far_ref, flat, slot_wind):
    half, turns, _, slots = near_ref.shape
    rows, lon = wind_ref.shape[1:]
    chunks = flat.shape[0] // rows
    tail = lon - (chunks - 1) * LANES
    spans = slots // LANES
    parts = directions // turns
    freqs = SUBLANES // parts
    shape = (SUBLANES, LANES)
    part = iota(shape, 0) % parts
    comp = lax.axis_index("comp")
    for r in range(rows):
        for k in range(chunks):
            size = LANES if k < chunks - 1 else tail
            for n in range(2):
                flat[r * chunks + k, n : n + 1, :size] = wind_ref[n, r : r + 1, k * LANES : k * LANES + size]
    for m in range(spans):
        span = slice(m * LANES, (m + 1) * LANES)
        cells = cells_ref[comp, :, span]

        def merged(chunk, sums):
            lane = cells - chunk * LANES
            here = (lane >= 0) & (lane < LANES)
            lane = lane & (LANES - 1)
            return jnp.where(
                here, jnp.take_along_axis(flat[chunk], lane, axis=1, mode="promise_in_bounds"), sums
            )

        found = lax.fori_loop(
            ranges_ref[comp, m], ranges_ref[comp, m + spans] + 1, merged, jnp.zeros(shape, F32)
        )
        slot_wind[0, :, span] = jnp.broadcast_to(found[0:1], shape)
        slot_wind[1, :, span] = jnp.broadcast_to(found[1:2], shape)

    rates = growth_rates(half, freqs, comp // half) + growth_rates(half, freqs, (comp // half) ^ 1)

    def one_span(m, carry):
        span = pl.ds(pl.multiple_of(m * LANES, LANES), LANES)
        east, north = slot_wind[0, :, span], slot_wind[1, :, span]
        for j in range(turns):
            sin, cos = signs(part, parts, turns, directions, j)
            along = east * cos + north * sin
            for source in range(half):
                slope, threshold = rates[source]
                near_ref[source, j, :, span] = jnp.exp(jnp.maximum(along * slope - threshold, 0.0))
                slope, threshold = rates[half + source]
                far_ref[(comp % half) ^ source, j, :, span] = jnp.exp(jnp.maximum(along * slope - threshold, 0.0))
        return carry

    lax.fori_loop(0, spans, one_span, 0)


def decode(arrived, half, turns, scale, span, store):
    sums = [jnp.zeros((SUBLANES, LANES), F32) for _ in range(2)]
    for source in range(half):
        for unit in range(turns // UNIT):
            words = [
                arrived[source, n * SUBLANES : (n + 1) * SUBLANES, span]
                for n in range(unit * WORDS, (unit + 1) * WORDS)
            ]
            rest = words[4]
            level = lax.shift_right_logical(rest, 17) & 127
            size = jnp.take_along_axis(scale, level, axis=1, mode="promise_in_bounds")
            offset = size * 65536.0
            for n in range(UNIT):
                if n == 8:
                    coded = rest & 0x1FFFF
                elif n % 2 == 0:
                    coded = words[n // 2] & 0x1FFFF
                else:
                    coded = lax.shift_right_logical(words[n // 2], 17) | (
                        lax.shift_right_logical(rest, 9 + n - 1) & 0x18000
                    )
                value = coded.astype(F32) * size - offset
                sums[n % 2] = sums[n % 2] + value * value
                j = unit * UNIT + n
                store(source, j, value)
    return sums[0] + sums[1]


def gate_kernel(*refs):
    refs[-1][...] = jnp.zeros(refs[-1].shape, F32)


def finish_kernel(freqs, half, *refs):
    far_refs, refs = refs[:half], refs[half:]
    near_ref, grown_near_ref, grown_far_ref, _, counts_ref, out_ref = refs[:6]
    far_words, near_words, near_values, far_values, ordered, arrivals = refs[6:]
    groups = 2 * half
    turns = near_values.shape[1]
    each = turns * SUBLANES
    shape = (SUBLANES, LANES)
    comp = lax.axis_index("comp")
    side, own = comp // half, comp % half
    count = counts_ref[0, comp]
    spans = [slice(low, low + LANES) for low in range(0, near_values.shape[-1], LANES)]
    copies = []
    for m, span in enumerate(spans):
        pairs = [(ref.at[0, :, span], far_words.at[n, :, span]) for n, ref in enumerate(far_refs)]
        pairs.append((near_ref.at[:, :, span], near_words.at[:, :, span]))
        pairs.append((grown_far_ref.at[:, :, :, span], far_values.at[:, :, :, span]))
        pairs.append((grown_near_ref.at[:, :, :, span], near_values.at[:, :, :, span]))
        copies.append([pltpu.make_async_copy(*pair, arrivals.at[m, n]) for n, pair in enumerate(pairs)])
        for copy in copies[-1]:
            copy.start()
    scale = power_table(2.0**-EXPONENT_ZERO / STEP_COUNT, 1)
    freq = iota(shape, 0) // (SUBLANES // freqs)
    square = (LANES, LANES)
    unit_matrix = (iota(square, 0) == iota(square, 1)).astype(jnp.bfloat16)
    steps = [jnp.where(side ^ far == 0, jnp.float32(1.0), jnp.float32(1.1 ** (half * freqs))) for far in range(2)]
    for m, span in enumerate(spans):
        for copy in copies[m]:
            copy.wait()

        def store_far(source, j, value):
            far_values[source, j, :, span] = value * far_values[source, j, :, span]

        def store_near(source, j, value):
            near_values[source, j, :, span] = value * near_values[source, j, :, span]

        sums = decode(far_words, half, turns, scale, span, store_far)
        sums = sums + decode(near_words, half, turns, scale, span, store_near)
        mean_sq = jnp.sum(sums, axis=0, keepdims=True) / float(groups * each)
        strength = jnp.broadcast_to(jnp.sqrt(mean_sq + 1e-06), shape)
        occupied = (m * LANES + iota(shape, 1)) < count
        for far in range(2):
            for source in range(half):
                rate = jnp.zeros(shape, F32)
                for f in range(freqs):
                    rate = jnp.where(freq == f, DAMPING * frequency(source * freqs + f, groups * freqs)[1], rate)
                factor = jnp.exp(-(rate * steps[far] * strength))
                for j in range(turns):
                    value = far_values[own ^ source, j, :, span] if far else near_values[source, j, :, span]
                    value = jnp.where(occupied, value * factor, 0.0)
                    ordered[m, side ^ far, pl.ds(source * each + j, SUBLANES, stride=turns), :] = value
        slots = slice(m * LANES, min((m + 1) * LANES, out_ref.shape[0]))
        for place in range(2):
            if place == 0:
                turned = lax.dot_general(
                    unit_matrix,
                    ordered[m, place].astype(jnp.bfloat16),
                    (((1,), (1,)), ((), ())),
                    preferred_element_type=F32,
                )
            else:
                turned = ordered[m, place].T
            out_ref[slots, place * half * each : (place + 1) * half * each] = turned[
                : slots.stop - slots.start
            ].astype(jnp.bfloat16)


def frequency(index, count):
    angular = 2.0 * math.pi * 0.0418 * 1.1**index
    return angular, 1.1 ** (index - (count - 1))


def body(spectra, depth_class, group_speed, current, depth_slope, wind, land_mask, block_counts):
    freqs, directions, rows, lon = spectra.shape
    total_freqs = group_speed.shape[1]
    groups = lax.axis_size("comp")
    bands = lax.axis_size("band")
    slot_count = rows * lon * 7 // (8 * groups)
    slots = -(-slot_count // LANES) * LANES
    parts = SUBLANES // freqs
    turns = directions // parts
    units = turns // UNIT
    chunks = -(-lon // LANES)
    padded = chunks * LANES
    height = rows * SUBLANES
    words = units * WORDS
    hbm = 2 * turns * height * padded
    latitude = (-60.0 + 120.0 * (np.arange(rows * bands) + 0.5) / (rows * bands)) * (math.pi / 180.0)
    stretch = [float(value) for value in 1.0 / np.cos(latitude)]
    smem = pl.BlockSpec(memory_space=pltpu.SMEM)
    vmem = pl.BlockSpec(memory_space=pltpu.VMEM)
    anywhere = pl.BlockSpec(memory_space=pl.ANY)

    range_rows = 2 * SUBLANES if groups < 2 * SUBLANES else 3 * SUBLANES
    cells, ranges = call(
        index_kernel,
        [
            jax.ShapeDtypeStruct((groups, SUBLANES, slots), I32),
            jax.ShapeDtypeStruct((range_rows, LANES), I32),
        ],
        (400_000 * groups * slots, 8 * groups * slots),
        in_specs=[vmem],
        out_specs=[vmem, vmem],
        scratch_shapes=[pltpu.VMEM((rows * chunks, LANES), I32)],
    )(jnp.concatenate([land_mask, jnp.pad(block_counts, ((0, 0), (0, lon - groups)))]))

    step = 3
    half = jax.ShapeDtypeStruct((turns, height // 2, padded), jnp.bfloat16)
    half_spec = pl.BlockSpec((step, height // 2, padded), lambda i: (i, 0, 0))
    bottom, top = call(
        arrange_kernel,
        [half, half],
        (4 * hbm, 2 * hbm),
        grid=(turns // step,),
        in_specs=[
            pl.BlockSpec((freqs, parts, step, rows, lon), lambda i: (0, 0, i, 0, 0)),
            pl.BlockSpec((rows, lon), lambda i: (0, 0)),
            anywhere,
        ],
        out_specs=[half_spec, half_spec],
        scratch_shapes=[pltpu.VMEM((step, chunks, height, LANES), F32)],
    )(spectra.reshape(freqs, parts, turns, rows, lon), land_mask, ranges)
    down = [(i, i + 1) for i in range(bands - 1)]
    below = lax.ppermute(top, "band", [(j, i) for i, j in down])
    above = lax.ppermute(bottom, "band", down)

    advected, coefs = call(
        functools.partial(advect_kernel, directions, stretch),
        [
            jax.ShapeDtypeStruct((turns, height, padded), F32),
            jax.ShapeDtypeStruct((4, height, padded), F32),
        ],
        (50 * hbm, 4 * hbm),
        in_specs=[vmem] * 6,
        out_specs=[vmem, vmem],
        scratch_shapes=[
            pltpu.VMEM((2, height, padded), F32),
            pltpu.VMEM((3 if chunks % 3 == 0 else 1, rows // 2, turns, 2 * SUBLANES, 2 * LANES), F32),
            pltpu.VMEM((2, turns, SUBLANES, LANES), F32),
        ],
    )(top, bottom, group_speed.T, depth_class, current, depth_slope)

    half = groups // 2
    block = (words * SUBLANES, slots)
    after, shipped = ranges, []
    for offsets, outputs in ((range(half, groups), [(1,) + block] * half), (range(half), [(half,) + block])):
        shipped.append(
            call(
                functools.partial(pack_kernel, directions, tuple(offsets)),
                [jax.ShapeDtypeStruct(shape, I32) for shape in outputs],
                (25 * hbm, 3 * hbm) if len(outputs) > 1 else LITTLE,
                in_specs=[vmem] * 5 + [smem, anywhere],
                out_specs=[vmem] * len(outputs),
                scratch_shapes=[
                    pltpu.VMEM((rows * chunks, words, SUBLANES, LANES), I32),
                    pltpu.VMEM((6 if chunks % 6 == 0 else 1, turns, SUBLANES, LANES), F32),
                    pltpu.VMEM((2, turns, SUBLANES, LANES), F32),
                ],
            )(advected, below, above, coefs, cells, ranges, after)
        )
        after = shipped[0][0]
    far = [
        lax.ppermute(part, "comp", [(i, i ^ (half + n)) for i in range(groups)]) for n, part in enumerate(shipped[0])
    ]
    halves = [list(range(half)), list(range(half, groups))]
    near = lax.all_to_all(shipped[1][0], "comp", split_axis=0, concat_axis=0, axis_index_groups=halves, tiled=True)

    total = total_freqs * directions
    values = jax.ShapeDtypeStruct((half, turns, SUBLANES, slots), F32)
    grown_near, grown_far = call(
        functools.partial(grow_kernel, directions),
        [values, values],
        LITTLE,
        vmem=WHOLE_VMEM,
        in_specs=[vmem, vmem, smem, anywhere],
        out_specs=[vmem, vmem],
        scratch_shapes=[
            pltpu.VMEM((rows * chunks, SUBLANES, LANES), F32),
            pltpu.VMEM((2, SUBLANES, slots), F32),
        ],
    )(wind, cells, ranges, shipped[1][0])

    gate = call(
        gate_kernel,
        jax.ShapeDtypeStruct((SUBLANES, LANES), F32),
        MUCH,
        vmem=WHOLE_VMEM,
        in_specs=[anywhere] * half,
        out_specs=vmem,
    )(*far)

    result = call(
        functools.partial(finish_kernel, freqs, half),
        jax.ShapeDtypeStruct((slot_count, total), jnp.bfloat16),
        (50 * total * slots, 6 * total * slots),
        vmem=WHOLE_VMEM,
        in_specs=[anywhere] * (half + 3) + [vmem, smem],
        out_specs=vmem,
        scratch_shapes=[
            pltpu.VMEM((half,) + block, I32),
            pltpu.VMEM((half,) + block, I32),
            pltpu.VMEM((half, turns, SUBLANES, slots), F32),
            pltpu.VMEM((half, turns, SUBLANES, slots), F32),
            pltpu.VMEM((slots // LANES, 2, total // 2, LANES), F32),
            pltpu.SemaphoreType.DMA((slots // LANES, half + 3)),
        ],
    )(*far, near, grown_near, grown_far, gate, block_counts)
    return result.T


def solution(mesh):
    return jax.shard_map(
        body,
        mesh=mesh,
        in_specs=(
            P("comp", None, "band", None),
            P("band", None),
            P(),
            P(None, "band", None),
            P(None, "band", None),
            P(None, "band", None),
            P("band", None),
            P("band", None),
        ),
        out_specs=P(None, ("comp", "band")),
        check_vma=False,
    )
```

```python
import functools
import math

import jax
import jax.numpy as jnp
import numpy as np
from jax import lax
from jax.experimental import pallas as pl
from jax.experimental.pallas import tpu as pltpu
from jax.sharding import PartitionSpec as P

GROWTH_RATE = 0.05
DAMPING = 1.5
TURNING_SCALE = 0.5

LANES = 128
SUBLANES = 8
UNIT = 9
WORDS = 5
STEP_COUNT = 65500.0
EXPONENT_ZERO = 99
WINDOW = 4
VMEM_BYTES = 16 * 1024 * 1024
LITTLE = (1_000, 1_000)
MUCH = (200_000_000_000, 1_000_000)
WHOLE_VMEM = 62_000_000

F32 = jnp.float32
I32 = jnp.int32


def call(kernel, out_shape, cost, vmem=VMEM_BYTES, **options):
    flops, moved = cost
    return pl.pallas_call(
        kernel,
        out_shape=out_shape,
        cost_estimate=pl.CostEstimate(flops=flops, bytes_accessed=moved, transcendentals=0),
        compiler_params=pltpu.CompilerParams(vmem_limit_bytes=vmem),
        **options,
    )


def iota(shape, axis):
    return lax.broadcasted_iota(I32, shape, axis)


def upwind(speed, far_behind, behind, centre, ahead, far_ahead):
    positive = speed > 0
    near = jnp.where(positive, behind, ahead)
    after = jnp.where(positive, ahead, behind)
    far = jnp.where(positive, far_behind, far_ahead)
    return jnp.abs(speed) * (2.0 * after + far + 3.0 * (centre - 2.0 * near))


def signs(part, parts, turns, directions, j):
    sin, cos = None, None
    for h in range(parts):
        angle = 2.0 * math.pi * (h * turns + j) / directions
        if h == 0:
            sin = jnp.full(part.shape, math.sin(angle), F32)
            cos = jnp.full(part.shape, math.cos(angle), F32)
        else:
            sin = jnp.where(part == h, math.sin(angle), sin)
            cos = jnp.where(part == h, math.cos(angle), cos)
    return sin, cos


def power_table(start, sign):
    lane = iota((SUBLANES, LANES), 1)
    table = jnp.full((SUBLANES, LANES), start, F32)
    for bit in range(7):
        factor = 2.0 ** (sign * 2**bit)
        table = jnp.where((lane & (1 << bit)) != 0, table * factor, table)
    return table


def arrange_kernel(x_ref, land_ref, after_ref, bottom_ref, top_ref, scratch):
    freqs, parts, step, rows, lon = x_ref.shape
    chunks = scratch.shape[1]
    tail = lon - (chunks - 1) * LANES
    filler = jnp.zeros((rows, LANES - tail), F32)
    lane = iota((SUBLANES * rows, LANES), 1)
    for j in range(step):
        for f in range(freqs):
            for h in range(parts):
                place = pl.ds(f * parts + h, rows, stride=SUBLANES)
                for k in range(chunks):
                    if k < chunks - 1:
                        piece = x_ref[f, h, j, :, k * LANES : (k + 1) * LANES].astype(F32)
                    else:
                        piece = x_ref[f, h, j, :, k * LANES : lon].astype(F32)
                        piece = jnp.concatenate([piece, filler], axis=1)
                    scratch[j, k, place, :] = piece
    initial = [None] * step
    for k in range(chunks):
        span = slice(k * LANES, (k + 1) * LANES)
        land = land_ref[:, k * LANES : min((k + 1) * LANES, lon)]
        if k == chunks - 1:
            land = jnp.concatenate([land, jnp.ones((rows, LANES - tail), I32)], axis=1)
        sea = (land == 0).astype(F32)
        sea = jnp.concatenate([jnp.broadcast_to(sea[r : r + 1], (SUBLANES, LANES)) for r in range(rows)], axis=0)
        for j in range(step):
            piece = scratch[j, k] * sea
            if k == 0:
                initial[j] = piece
            if k == chunks - 1:
                wrapped = jnp.where(
                    lane < tail + 2,
                    pltpu.roll(initial[j], tail, axis=1),
                    pltpu.roll(piece, LANES - tail, axis=1),
                )
                piece = jnp.where(lane < tail, piece, wrapped)
            piece = piece.astype(jnp.bfloat16)
            top_ref[j, :, span] = piece[: 2 * SUBLANES]
            bottom_ref[j, :, span] = piece[2 * SUBLANES :]


def index_kernel(land_ref, cells_ref, ranges_ref, flat):
    chunks = flat.shape[0]
    rows, lon = land_ref.shape[0] - 1, land_ref.shape[1]
    per_row = chunks // rows
    tail = lon - (per_row - 1) * LANES
    flat[...] = jnp.ones(flat.shape, I32)
    for r in range(rows):
        for k in range(per_row):
            size = LANES if k < per_row - 1 else tail
            piece = land_ref[r : r + 1, k * LANES : k * LANES + size]
            flat[r * per_row + k : r * per_row + k + 1, :size] = piece
    groups, _, slots = cells_ref.shape
    spans = slots // LANES
    sea = (flat[...] == 0).astype(jnp.bfloat16)
    square = (LANES, LANES)
    ones_before = (iota(square, 1) <= iota(square, 0)).astype(jnp.bfloat16)
    ranks = lax.dot_general(ones_before, sea, (((1,), (1,)), ((), ())), preferred_element_type=F32)
    totals = jnp.dot(sea, jnp.ones(square, jnp.bfloat16), preferred_element_type=F32)
    chunk_square = (chunks, chunks)
    chunks_before = (iota(chunk_square, 1) <= iota(chunk_square, 0)).astype(jnp.bfloat16)
    through = jnp.dot(chunks_before, totals.astype(jnp.bfloat16), preferred_element_type=F32)
    through_column = through[:, :1]
    total_column = totals[:, :1]
    ranks = ranks.astype(jnp.bfloat16)
    chunk_ids = iota((chunks, slots), 0)
    slot_ids = iota((1, slots), 1)
    span_lane = iota((1, LANES), 1)
    start = jnp.zeros((1, 1), I32)
    longest = jnp.zeros((1, 1), F32)
    for c in range(groups):
        count = land_ref[rows : rows + 1, c : c + 1]
        number = (slot_ids + start).astype(F32)
        passed = (through_column <= number).astype(F32)
        chunk_of = jnp.sum(passed, axis=0, keepdims=True)
        before = jnp.sum(passed * total_column, axis=0, keepdims=True)
        chunk_of = chunk_of.astype(I32)
        chosen = (chunk_ids == chunk_of).astype(jnp.bfloat16)
        inside = jnp.dot(ranks, chosen, preferred_element_type=F32)
        lane = jnp.sum((inside <= number - before).astype(F32), axis=0, keepdims=True)
        valid = slot_ids < count
        found = jnp.where(valid, chunk_of * LANES + lane.astype(I32), -1)
        cells_ref[c] = jnp.broadcast_to(found, (SUBLANES, slots))
        bounds = jnp.zeros((1, LANES), I32)
        final = jnp.zeros((1, 1), F32)
        for m in range(spans):
            span = slice(m * LANES, (m + 1) * LANES)
            own = chunk_of[:, span].astype(F32)
            low = jnp.min(jnp.where(valid[:, span], own, float(chunks)), axis=1, keepdims=True)
            high = jnp.max(jnp.where(valid[:, span], own, -1.0), axis=1, keepdims=True)
            longest = jnp.maximum(longest, high - low + 1.0)
            final = jnp.maximum(final, high)
            bounds = jnp.where(span_lane == m, low.astype(I32), bounds)
            bounds = jnp.where(span_lane == m + spans, high.astype(I32), bounds)
        bounds = jnp.where(span_lane == 2 * spans, final.astype(I32), bounds)
        ranges_ref[c : c + 1, :] = bounds
        start = start + count
    ranges_ref[groups : groups + 1, :] = jnp.broadcast_to(longest.astype(I32), (1, LANES))


def advect_kernel(
    directions,
    stretch,
    top_ref,
    bottom_ref,
    speed_ref,
    depth_ref,
    current_ref,
    slope_ref,
    out_ref,
    coef_ref,
    scratch,
    along,
    trig,
):
    turns, _, padded = top_ref.shape
    rows, lon = depth_ref.shape
    chunks = padded // LANES
    tail = lon - (chunks - 1) * LANES
    total_freqs, depths = speed_ref.shape
    parts = directions // turns
    freqs = SUBLANES // parts
    comp, band = lax.axis_index("comp"), lax.axis_index("band")
    speeds = speed_ref[...]
    freq_ids = iota(speeds.shape, 0)
    table = []
    for f in range(freqs):
        row = jnp.sum(jnp.where(freq_ids == comp * freqs + f, speeds, 0.0), axis=0, keepdims=True)
        table.append(jnp.broadcast_to(row, (parts, depths)))
    table = jnp.concatenate(table, axis=0)
    table = jnp.concatenate([table, jnp.zeros((SUBLANES, LANES - depths), F32)], axis=1) * (1.0 / 6.0)
    shape = (SUBLANES, LANES)
    for r in range(rows):
        place = slice(r * SUBLANES, (r + 1) * SUBLANES)
        widening = jnp.float32(0.0)
        for b in range(len(stretch) // rows):
            widening = jnp.where(band == b, jnp.float32(stretch[b * rows + r]), widening)
        for k in range(chunks):
            span = slice(k * LANES, (k + 1) * LANES)

            def field(row):
                if k == chunks - 1:
                    row = jnp.concatenate([row[:, :tail], jnp.zeros((1, LANES - tail), row.dtype)], axis=1)
                return jnp.broadcast_to(row, shape)

            own = slice(k * LANES, min((k + 1) * LANES, lon))
            classes = field(depth_ref[r : r + 1, own])
            sixth = jnp.take_along_axis(table, classes, axis=1, mode="promise_in_bounds")
            coef_ref[0, place, span] = sixth
            coef_ref[1, place, span] = field(current_ref[1, r : r + 1, own]) * (1.0 / 6.0)
            coef_ref[2, place, span] = sixth * TURNING_SCALE * field(slope_ref[0, r : r + 1, own])
            coef_ref[3, place, span] = sixth * TURNING_SCALE * field(slope_ref[1, r : r + 1, own])
            scratch[0, place, span] = sixth * widening
            scratch[1, place, span] = field(current_ref[0, r : r + 1, own]) * (1.0 / 6.0)

    source, target = iota((3 * LANES, 2 * LANES), 0), iota((3 * LANES, 2 * LANES), 1)
    distance = source - LANES - (target & (LANES - 1))
    odd = target < LANES
    weights = jnp.zeros(distance.shape, F32)
    for at, first, second in ((-2, 0.5, 0.5), (-1, -4.0, -2.0), (0, 0.0, 3.0), (1, 4.0, -2.0), (2, -0.5, 0.5)):
        weights = jnp.where(distance == at, jnp.where(odd, first, second), weights)
    weights = weights.astype(jnp.bfloat16)
    part = iota(shape, 0) % parts
    for j in range(turns):
        trig[0, j], trig[1, j] = signs(part, parts, turns, directions, j)

    together = along.shape[0]

    def lanes(k):
        return pl.ds(pl.multiple_of(k * LANES, LANES), LANES)

    def some_chunks(i, carry):
        for at in range(together):
            k = i * together + at
            before, span, after = lanes((k + chunks - 1) % chunks), lanes(k), lanes((k + 1) % chunks)
            for n, ref in enumerate((top_ref, bottom_ref)):
                wide = jnp.concatenate([ref[:, :, before], ref[:, :, span], ref[:, :, after]], axis=2)
                wide = wide.reshape(turns * 2 * SUBLANES, 3 * LANES)
                product = jnp.dot(wide, weights, preferred_element_type=F32)
                along[at, n] = product.reshape(turns, 2 * SUBLANES, 2 * LANES)
        for at in range(together):
            one_chunk(lanes(i * together + at), at)
        return carry

    def one_chunk(span, at):
        places = [slice(r * SUBLANES, (r + 1) * SUBLANES) for r in range(rows)]
        sixths = [coef_ref[0, place, span] for place in places]
        currents_y = [coef_ref[1, place, span] for place in places]
        widened = [scratch[0, place, span] for place in places]
        currents_x = [scratch[1, place, span] for place in places]
        for j in range(turns):
            sin, cos = trig[0, j], trig[1, j]
            centres = []
            for ref in (top_ref, bottom_ref):
                pair = ref[j, :, span].astype(F32)
                centres += [pair[:SUBLANES], pair[SUBLANES:]]
            for r in range(rows):
                row = slice((r % 2) * SUBLANES, (r % 2 + 1) * SUBLANES)
                odd, even = along[at, r // 2, j, row, :LANES], along[at, r // 2, j, row, LANES:]
                speed_x = widened[r] * cos + currents_x[r]
                moved = speed_x * odd + jnp.abs(speed_x) * even
                speed_y = sixths[r] * sin + currents_y[r]
                near = [centres[n] if 0 <= n < rows else 0.0 for n in range(r - 2, r + 3)]
                out_ref[j, places[r], span] = centres[r] - moved - upwind(speed_y, *near)

    lax.fori_loop(0, chunks // together, some_chunks, 0)


def pack_kernel(directions, offsets, adv_ref, below_ref, above_ref, coef_ref, cells_ref, ranges_ref, after_ref, *refs):
    out_refs, (packed, turned_values, trig) = refs[:-3], refs[-3:]
    turns, height, padded = adv_ref.shape
    rows = height // SUBLANES
    chunks = padded // LANES
    parts = directions // turns
    units = turns // UNIT
    shape = (SUBLANES, LANES)
    part = iota(shape, 0) % parts
    scale = power_table(STEP_COUNT * 2.0**EXPONENT_ZERO, -1)
    together = turned_values.shape[0]
    for j in range(turns):
        trig[0, j], trig[1, j] = signs(part, parts, turns, directions, j)

    def turned(value, by):
        if by == 0:
            return value
        if by > 0:
            return jnp.where(
                part == parts - 1, pltpu.roll(value, parts - 1, axis=0), pltpu.roll(value, SUBLANES - 1, axis=0)
            )
        return jnp.where(part == 0, pltpu.roll(value, SUBLANES - parts + 1, axis=0), pltpu.roll(value, 1, axis=0))

    def refract(r, k, into):
        place = slice(r * SUBLANES, (r + 1) * SUBLANES)
        span = pl.ds(pl.multiple_of(k * LANES, LANES), LANES)
        sixth, current_y, turn_x, turn_y = [coef_ref[n, place, span] for n in range(4)]
        advected = []
        for j in range(turns):
            speed = sixth * trig[0, j] + current_y
            positive = speed > 0
            ref = above_ref if r < 2 else below_ref
            outer = ref[j, :, span].astype(F32)
            low, high = outer[:SUBLANES], outer[SUBLANES:]
            if r == 0:
                share = jnp.where(positive, low - 6.0 * high, 2.0 * high)
            elif r == 1:
                share = jnp.where(positive, high, 0.0)
            elif r == rows - 2:
                share = jnp.where(positive, 0.0, low)
            else:
                share = jnp.where(positive, 2.0 * low, high - 6.0 * low)
            advected.append(adv_ref[j, place, span] - jnp.abs(speed) * share)
        around = {j: turned(advected[j % turns], j // turns) for j in range(-2, turns + 2)}
        largest = [None] * units
        for j in range(turns):
            speed = trig[0, j] * turn_x - trig[1, j] * turn_y
            value = around[j] - upwind(speed, *[around[n] for n in range(j - 2, j + 3)])
            turned_values[into, j] = value
            size = jnp.abs(value)
            unit = j // UNIT
            largest[unit] = size if largest[unit] is None else jnp.maximum(largest[unit], size)
        return largest

    def code(chunk, come_from, unit, largest):
        level = jnp.ceil(jnp.log2(jnp.maximum(largest, 2.0**-98)))
        level = jnp.minimum(level, 28.0).astype(I32) + EXPONENT_ZERO
        level = jnp.maximum(level, 1)
        inverse = jnp.take_along_axis(scale, level, axis=1, mode="promise_in_bounds")
        codes = [
            (turned_values[come_from, unit * UNIT + n] * inverse + 65536.5).astype(I32) for n in range(UNIT)
        ]
        first = unit * WORDS
        rest = codes[8] | (level << 17)
        for n in range(4):
            even, odd = codes[2 * n], codes[2 * n + 1]
            packed[chunk, first + n] = even | (odd << 17)
            rest = rest | ((odd >> 15) << (24 + 2 * n))
        packed[chunk, first + 4] = rest

    half = len(offsets)
    _, words, slots = out_refs[0].shape
    words = words // SUBLANES
    spans = slots // LANES
    comp = lax.axis_index("comp")
    base = ((comp ^ offsets[0]) // half) * half
    first_set = ranges_ref[base, 0] // together
    last_set = ranges_ref[base + half - 1, 2 * spans] // together
    sets = chunks // together
    for r in range(rows):

        def some_chunks(i, carry):
            found = [refract(r, i * together + n, n) for n in range(together)]
            for n in range(together):
                for unit in range(units):
                    code(r * chunks + i * together + n, n, unit, found[n][unit])
            return carry

        low = jnp.clip(first_set - r * sets, 0, sets)
        high = jnp.clip(last_set + 1 - r * sets, 0, sets)
        lax.fori_loop(low, high, some_chunks, 0)

    last = rows * chunks - 1

    def merged(cells, chunk, sums):
        lane = cells - chunk * LANES
        here = (lane >= 0) & (lane < LANES)
        lane = lane & (LANES - 1)
        return tuple(
            jnp.where(
                here, jnp.take_along_axis(packed[chunk, n], lane, axis=1, mode="promise_in_bounds"), sums[n]
            )
            for n in range(words)
        )

    if len(out_refs) == half:
        places = [(comp ^ offset, out_ref, 0) for offset, out_ref in zip(offsets, out_refs)]
    else:
        places = [(base + n, out_refs[0], n) for n in range(half)]
    for block, out_ref, at in places:
        for m in range(spans):
            span = slice(m * LANES, (m + 1) * LANES)
            cells = cells_ref[block, :, span]
            low = ranges_ref[block, m]
            sums = tuple(jnp.zeros(shape, I32) for _ in range(words))
            for t in range(WINDOW):
                sums = merged(cells, jnp.minimum(low + t, last), sums)
            for n in range(words):
                out_ref[at, n * SUBLANES : (n + 1) * SUBLANES, span] = sums[n]

    @pl.when(ranges_ref[cells_ref.shape[0], 0] > WINDOW)
    def _():
        for block, out_ref, at in places:
            for m in range(spans):
                span = slice(m * LANES, (m + 1) * LANES)
                cells = cells_ref[block, :, span]
                low, high = ranges_ref[block, m], ranges_ref[block, m + spans]
                sums = tuple(out_ref[at, n * SUBLANES : (n + 1) * SUBLANES, span] for n in range(words))
                sums = lax.fori_loop(
                    low + WINDOW, high + 1, lambda chunk, sums: merged(cells, chunk, sums), sums
                )
                for n in range(words):
                    out_ref[at, n * SUBLANES : (n + 1) * SUBLANES, span] = sums[n]


def growth_rates(half, freqs, side):
    shape = (SUBLANES, LANES)
    freq = iota(shape, 0) // (SUBLANES // freqs)
    step = jnp.where(side == 0, jnp.float32(1.0), jnp.float32(1.1 ** (half * freqs)))
    rates = []
    for source in range(half):
        slope, threshold = jnp.zeros(shape, F32), jnp.zeros(shape, F32)
        for f in range(freqs):
            angular, ratio = frequency(source * freqs + f, 2 * half * freqs)
            slope = jnp.where(freq == f, GROWTH_RATE * ratio * angular / 9.81, slope)
            threshold = jnp.where(freq == f, GROWTH_RATE * ratio, threshold)
        rates.append((slope * (step * step), threshold * step))
    return rates


def grow_kernel(directions, wind_ref, cells_ref, ranges_ref, after_ref, near_ref, far_ref, flat, slot_wind):
    half, turns, _, slots = near_ref.shape
    rows, lon = wind_ref.shape[1:]
    chunks = flat.shape[0] // rows
    tail = lon - (chunks - 1) * LANES
    spans = slots // LANES
    parts = directions // turns
    freqs = SUBLANES // parts
    shape = (SUBLANES, LANES)
    part = iota(shape, 0) % parts
    comp = lax.axis_index("comp")
    for r in range(rows):
        for k in range(chunks):
            size = LANES if k < chunks - 1 else tail
            for n in range(2):
                flat[r * chunks + k, n : n + 1, :size] = wind_ref[n, r : r + 1, k * LANES : k * LANES + size]
    for m in range(spans):
        span = slice(m * LANES, (m + 1) * LANES)
        cells = cells_ref[comp, :, span]

        def merged(chunk, sums):
            lane = cells - chunk * LANES
            here = (lane >= 0) & (lane < LANES)
            lane = lane & (LANES - 1)
            return jnp.where(
                here, jnp.take_along_axis(flat[chunk], lane, axis=1, mode="promise_in_bounds"), sums
            )

        found = lax.fori_loop(
            ranges_ref[comp, m], ranges_ref[comp, m + spans] + 1, merged, jnp.zeros(shape, F32)
        )
        slot_wind[0, :, span] = jnp.broadcast_to(found[0:1], shape)
        slot_wind[1, :, span] = jnp.broadcast_to(found[1:2], shape)

    rates = growth_rates(half, freqs, comp // half) + growth_rates(half, freqs, (comp // half) ^ 1)

    def one_span(m, carry):
        span = pl.ds(pl.multiple_of(m * LANES, LANES), LANES)
        east, north = slot_wind[0, :, span], slot_wind[1, :, span]
        for j in range(turns):
            sin, cos = signs(part, parts, turns, directions, j)
            along = east * cos + north * sin
            for source in range(half):
                slope, threshold = rates[source]
                near_ref[source, j, :, span] = jnp.exp(jnp.maximum(along * slope - threshold, 0.0))
                slope, threshold = rates[half + source]
                far_ref[(comp % half) ^ source, j, :, span] = jnp.exp(jnp.maximum(along * slope - threshold, 0.0))
        return carry

    lax.fori_loop(0, spans, one_span, 0)


def decode(arrived, half, turns, scale, span, store):
    sums = [jnp.zeros((SUBLANES, LANES), F32) for _ in range(2)]
    for source in range(half):
        for unit in range(turns // UNIT):
            words = [
                arrived[source, n * SUBLANES : (n + 1) * SUBLANES, span]
                for n in range(unit * WORDS, (unit + 1) * WORDS)
            ]
            rest = words[4]
            level = lax.shift_right_logical(rest, 17) & 127
            size = jnp.take_along_axis(scale, level, axis=1, mode="promise_in_bounds")
            offset = size * 65536.0
            for n in range(UNIT):
                if n == 8:
                    coded = rest & 0x1FFFF
                elif n % 2 == 0:
                    coded = words[n // 2] & 0x1FFFF
                else:
                    coded = lax.shift_right_logical(words[n // 2], 17) | (
                        lax.shift_right_logical(rest, 9 + n - 1) & 0x18000
                    )
                value = coded.astype(F32) * size - offset
                sums[n % 2] = sums[n % 2] + value * value
                j = unit * UNIT + n
                store(source, j, value)
    return sums[0] + sums[1]


def gate_kernel(*refs):
    refs[-1][...] = jnp.zeros(refs[-1].shape, F32)


def finish_kernel(freqs, half, *refs):
    far_refs, refs = refs[:half], refs[half:]
    near_ref, grown_near_ref, grown_far_ref, _, counts_ref, out_ref = refs[:6]
    far_words, near_words, near_values, far_values, ordered, arrivals = refs[6:]
    groups = 2 * half
    turns = near_values.shape[1]
    each = turns * SUBLANES
    shape = (SUBLANES, LANES)
    comp = lax.axis_index("comp")
    side, own = comp // half, comp % half
    count = counts_ref[0, comp]
    spans = [slice(low, low + LANES) for low in range(0, near_values.shape[-1], LANES)]
    copies = []
    for m, span in enumerate(spans):
        pairs = [(ref.at[0, :, span], far_words.at[n, :, span]) for n, ref in enumerate(far_refs)]
        pairs.append((near_ref.at[:, :, span], near_words.at[:, :, span]))
        pairs.append((grown_far_ref.at[:, :, :, span], far_values.at[:, :, :, span]))
        pairs.append((grown_near_ref.at[:, :, :, span], near_values.at[:, :, :, span]))
        copies.append([pltpu.make_async_copy(*pair, arrivals.at[m, n]) for n, pair in enumerate(pairs)])
        for copy in copies[-1]:
            copy.start()
    scale = power_table(2.0**-EXPONENT_ZERO / STEP_COUNT, 1)
    freq = iota(shape, 0) // (SUBLANES // freqs)
    square = (LANES, LANES)
    unit_matrix = (iota(square, 0) == iota(square, 1)).astype(jnp.bfloat16)
    steps = [jnp.where(side ^ far == 0, jnp.float32(1.0), jnp.float32(1.1 ** (half * freqs))) for far in range(2)]
    for m, span in enumerate(spans):
        for copy in copies[m]:
            copy.wait()

        def store_far(source, j, value):
            far_values[source, j, :, span] = value * far_values[source, j, :, span]

        def store_near(source, j, value):
            near_values[source, j, :, span] = value * near_values[source, j, :, span]

        sums = decode(far_words, half, turns, scale, span, store_far)
        sums = sums + decode(near_words, half, turns, scale, span, store_near)
        mean_sq = jnp.sum(sums, axis=0, keepdims=True) / float(groups * each)
        strength = jnp.broadcast_to(jnp.sqrt(mean_sq + 1e-06), shape)
        occupied = (m * LANES + iota(shape, 1)) < count
        for far in range(2):
            for source in range(half):
                rate = jnp.zeros(shape, F32)
                for f in range(freqs):
                    rate = jnp.where(freq == f, DAMPING * frequency(source * freqs + f, groups * freqs)[1], rate)
                factor = jnp.exp(-(rate * steps[far] * strength))
                for j in range(turns):
                    value = far_values[own ^ source, j, :, span] if far else near_values[source, j, :, span]
                    value = jnp.where(occupied, value * factor, 0.0)
                    ordered[m, side ^ far, pl.ds(source * each + j, SUBLANES, stride=turns), :] = value
        slots = slice(m * LANES, min((m + 1) * LANES, out_ref.shape[0]))
        for place in range(2):
            if place == 0:
                turned = lax.dot_general(
                    unit_matrix,
                    ordered[m, place].astype(jnp.bfloat16),
                    (((1,), (1,)), ((), ())),
                    preferred_element_type=F32,
                )
            else:
                turned = ordered[m, place].T
            out_ref[slots, place * half * each : (place + 1) * half * each] = turned[
                : slots.stop - slots.start
            ].astype(jnp.bfloat16)


def frequency(index, count):
    angular = 2.0 * math.pi * 0.0418 * 1.1**index
    return angular, 1.1 ** (index - (count - 1))


def body(spectra, depth_class, group_speed, current, depth_slope, wind, land_mask, block_counts):
    freqs, directions, rows, lon = spectra.shape
    total_freqs = group_speed.shape[1]
    groups = lax.axis_size("comp")
    bands = lax.axis_size("band")
    slot_count = rows * lon * 7 // (8 * groups)
    slots = -(-slot_count // LANES) * LANES
    parts = SUBLANES // freqs
    turns = directions // parts
    units = turns // UNIT
    chunks = -(-lon // LANES)
    padded = chunks * LANES
    height = rows * SUBLANES
    words = units * WORDS
    hbm = 2 * turns * height * padded
    latitude = (-60.0 + 120.0 * (np.arange(rows * bands) + 0.5) / (rows * bands)) * (math.pi / 180.0)
    stretch = [float(value) for value in 1.0 / np.cos(latitude)]
    smem = pl.BlockSpec(memory_space=pltpu.SMEM)
    vmem = pl.BlockSpec(memory_space=pltpu.VMEM)
    anywhere = pl.BlockSpec(memory_space=pl.ANY)

    range_rows = 2 * SUBLANES if groups < 2 * SUBLANES else 3 * SUBLANES
    cells, ranges = call(
        index_kernel,
        [
            jax.ShapeDtypeStruct((groups, SUBLANES, slots), I32),
            jax.ShapeDtypeStruct((range_rows, LANES), I32),
        ],
        (400_000 * groups * slots, 8 * groups * slots),
        in_specs=[vmem],
        out_specs=[vmem, vmem],
        scratch_shapes=[pltpu.VMEM((rows * chunks, LANES), I32)],
    )(jnp.concatenate([land_mask, jnp.pad(block_counts, ((0, 0), (0, lon - groups)))]))

    step = 3
    half = jax.ShapeDtypeStruct((turns, height // 2, padded), jnp.bfloat16)
    half_spec = pl.BlockSpec((step, height // 2, padded), lambda i: (i, 0, 0))
    bottom, top = call(
        arrange_kernel,
        [half, half],
        (4 * hbm, 2 * hbm),
        grid=(turns // step,),
        in_specs=[
            pl.BlockSpec((freqs, parts, step, rows, lon), lambda i: (0, 0, i, 0, 0)),
            pl.BlockSpec((rows, lon), lambda i: (0, 0)),
            anywhere,
        ],
        out_specs=[half_spec, half_spec],
        scratch_shapes=[pltpu.VMEM((step, chunks, height, LANES), F32)],
    )(spectra.reshape(freqs, parts, turns, rows, lon), land_mask, ranges)
    down = [(i, i + 1) for i in range(bands - 1)]
    below = lax.ppermute(top, "band", [(j, i) for i, j in down])
    above = lax.ppermute(bottom, "band", down)

    advected, coefs = call(
        functools.partial(advect_kernel, directions, stretch),
        [
            jax.ShapeDtypeStruct((turns, height, padded), F32),
            jax.ShapeDtypeStruct((4, height, padded), F32),
        ],
        (50 * hbm, 4 * hbm),
        in_specs=[vmem] * 6,
        out_specs=[vmem, vmem],
        scratch_shapes=[
            pltpu.VMEM((2, height, padded), F32),
            pltpu.VMEM((3 if chunks % 3 == 0 else 1, rows // 2, turns, 2 * SUBLANES, 2 * LANES), F32),
            pltpu.VMEM((2, turns, SUBLANES, LANES), F32),
        ],
    )(top, bottom, group_speed.T, depth_class, current, depth_slope)

    half = groups // 2
    block = (words * SUBLANES, slots)
    after, shipped = ranges, []
    pair = half // 2
    for offsets in (range(half, half + pair), range(half + pair, groups), range(half)):
        last = len(offsets) == half
        outputs = [(half,) + block] if last else [(1,) + block] * pair
        shipped.append(
            call(
                functools.partial(pack_kernel, directions, tuple(offsets)),
                [jax.ShapeDtypeStruct(shape, I32) for shape in outputs],
                LITTLE if shipped else (12 * hbm, 2 * hbm),
                in_specs=[vmem] * 5 + [smem, anywhere],
                out_specs=[vmem] * len(outputs),
                scratch_shapes=[
                    pltpu.VMEM((rows * chunks, words, SUBLANES, LANES), I32),
                    pltpu.VMEM((6 if chunks % 6 == 0 else 1, turns, SUBLANES, LANES), F32),
                    pltpu.VMEM((2, turns, SUBLANES, LANES), F32),
                ],
            )(advected, below, above, coefs, cells, ranges, after)
        )
        after = shipped[-1][0]
    far = [
        lax.ppermute(part, "comp", [(i, i ^ (half + n)) for i in range(groups)])
        for n, part in enumerate(shipped[0] + shipped[1])
    ]
    halves = [list(range(half)), list(range(half, groups))]
    near = lax.all_to_all(shipped[2][0], "comp", split_axis=0, concat_axis=0, axis_index_groups=halves, tiled=True)

    total = total_freqs * directions
    values = jax.ShapeDtypeStruct((half, turns, SUBLANES, slots), F32)
    grown_near, grown_far = call(
        functools.partial(grow_kernel, directions),
        [values, values],
        LITTLE,
        vmem=WHOLE_VMEM,
        in_specs=[vmem, vmem, smem, anywhere],
        out_specs=[vmem, vmem],
        scratch_shapes=[
            pltpu.VMEM((rows * chunks, SUBLANES, LANES), F32),
            pltpu.VMEM((2, SUBLANES, slots), F32),
        ],
    )(wind, cells, ranges, shipped[2][0])

    gate = call(
        gate_kernel,
        jax.ShapeDtypeStruct((SUBLANES, LANES), F32),
        MUCH,
        vmem=WHOLE_VMEM,
        in_specs=[anywhere] * half,
        out_specs=vmem,
    )(*far)

    result = call(
        functools.partial(finish_kernel, freqs, half),
        jax.ShapeDtypeStruct((slot_count, total), jnp.bfloat16),
        (50 * total * slots, 6 * total * slots),
        vmem=WHOLE_VMEM,
        in_specs=[anywhere] * (half + 3) + [vmem, smem],
        out_specs=vmem,
        scratch_shapes=[
            pltpu.VMEM((half,) + block, I32),
            pltpu.VMEM((half,) + block, I32),
            pltpu.VMEM((half, turns, SUBLANES, slots), F32),
            pltpu.VMEM((half, turns, SUBLANES, slots), F32),
            pltpu.VMEM((slots // LANES, 2, total // 2, LANES), F32),
            pltpu.SemaphoreType.DMA((slots // LANES, half + 3)),
        ],
    )(*far, near, grown_near, grown_far, gate, block_counts)
    return result.T


def solution(mesh):
    return jax.shard_map(
        body,
        mesh=mesh,
        in_specs=(
            P("comp", None, "band", None),
            P("band", None),
            P(),
            P(None, "band", None),
            P(None, "band", None),
            P(None, "band", None),
            P("band", None),
            P("band", None),
        ),
        out_specs=P(None, ("comp", "band")),
        check_vma=False,
    )
```
